256 devices in a mesh: sec: 4 (over x), tile: 64 (over z, y, core).
Axes of the slice: x: 4, y: 4, z: 8, core: 2. Of those that a mesh axis runs over, the one named last changes fastest.
Arguments:
- sections: bfloat16 [8, 64, 256, 512], P('sec', 'tile'), may hold values from -40 to 40
- corner_offsets: int32 [2, 8, 64, 256, 512], P(None, 'sec', 'tile'), may hold values from -2 to 1
Outputs:
- node_mesh: float32 [8, 2, 64, 8, 16], P('sec', None, 'tile')
- warped: float32 [8, 64, 256, 512], P('sec', 'tile')
The draws below stay inside these ranges and needn't reach their ends.
All inputs are finite; a program needn't handle non-finite values.
Results may differ from the reference program's by a relative error of at most 0.0035.
Values may be sent and summed in bfloat16 or wider, within the bound.
A program may use at most 64 MiB of HBM per device.

```python
import math
import jax
import jax.numpy as jnp
from jax import lax

TILE_ROWS = 256
TILE_COLS = 512
TILE_GRID = 8
PATCH = 128
STRIDE = 32
SHIFTS = 32
ITERS = 4
HALO = 48
SECTIONS = 8
GRID_ROWS = 8
HEIGHT = 2048
COLS = 4096
TILE_NODE_ROWS = 8
TILE_NODE_COLS = 16
NODE_ROWS = 64
NODE_COLS = 128
N_TILE = 64


def draw_sections(key, part):
    key = jax.random.fold_in(key, 11)
    subkeys = jax.random.split(key, 3)
    row_scale = jnp.exp(jax.random.uniform(subkeys[1], (SECTIONS, N_TILE, TILE_ROWS, 1), jnp.float32, -1.15, 1.15))
    col_scale = jnp.exp(jax.random.uniform(subkeys[2], (SECTIONS, N_TILE, 1, TILE_COLS), jnp.float32, -1.15, 1.15))
    texture = jnp.clip(jax.random.normal(subkeys[0], (SECTIONS, N_TILE, TILE_ROWS, TILE_COLS), jnp.float32), -4.0, 4.0)
    return (texture * row_scale * col_scale).astype(jnp.bfloat16)


def plant(result, rng, smallest, top_value):
    spot = [jax.random.randint(jax.random.fold_in(rng, axis), (), 0, length) for axis, length in enumerate(result.shape)]
    longest = result.shape.index(max(result.shape))
    neighbour = spot[:longest] + [(spot[longest] + 1) % result.shape[longest]] + spot[longest + 1:]
    return result.at[tuple(spot)].set(smallest).at[tuple(neighbour)].set(top_value)


def setup_inputs(seed: int = 0) -> dict:
    keys = jax.random.split(jax.random.key(seed), 3)
    sections = draw_sections(jax.random.fold_in(keys[2], 71), 0)
    corner_offsets = plant(jax.random.randint(keys[1], (2, SECTIONS, N_TILE, TILE_ROWS, TILE_COLS), -2, 2), jax.random.fold_in(keys[1], 1), -2, 1).astype(jnp.int32)
    return {"sections": sections, "corner_offsets": corner_offsets}


EPS = 1e-05
STEP_RATE = 0.15

def dft_tables(patch_size, shift_count):
    counter = jnp.arange(patch_size, dtype=jnp.int32)
    forward = counter[:, None] * counter[None, :] % patch_size
    angles = forward.astype(jnp.float32) * (2.0 * math.pi / patch_size)
    shift_values = jnp.arange(shift_count, dtype=jnp.int32) - shift_count // 2
    backward = shift_values[:, None] * counter[None, :] % patch_size
    back_angles = backward.astype(jnp.float32) * (2.0 * math.pi / patch_size)
    return (jnp.cos(angles).astype(jnp.bfloat16), jnp.sin(angles).astype(jnp.bfloat16), jnp.cos(back_angles).astype(jnp.bfloat16), jnp.sin(back_angles).astype(jnp.bfloat16))

def window_patches(row_band, stride):
    stack_count, patch_size, band_width = row_band.shape
    patch_count = (band_width - patch_size) // stride + 1
    blocks = row_band.reshape(stack_count, patch_size, band_width // stride, stride)
    pieces = [blocks[:, :, offset:offset + patch_count, :] for offset in range(patch_size // stride)]
    joined = jnp.stack(pieces, 3).reshape(stack_count, patch_size, patch_count, patch_size)
    return jnp.transpose(joined, (0, 2, 1, 3))

def spectral_product(form, left, right):
    return jnp.einsum(form, left.astype(jnp.float32), right.astype(jnp.float32), precision=lax.Precision.HIGHEST)

def spectrum(patches, tables):
    cosine_lookup, sine_lookup = (tables[0], tables[1])
    real_row_pass = spectral_product('jpq,qk->jpk', patches, cosine_lookup).astype(jnp.bfloat16)
    imaginary_row_pass = (-spectral_product('jpq,qk->jpk', patches, sine_lookup)).astype(jnp.bfloat16)
    real_complete = (spectral_product('gh,tho->tgo', cosine_lookup, real_row_pass) + spectral_product('gh,tho->tgo', sine_lookup, imaginary_row_pass)).astype(jnp.bfloat16)
    imaginary_complete = (spectral_product('gh,tho->tgo', cosine_lookup, imaginary_row_pass) - spectral_product('gh,tho->tgo', sine_lookup, real_row_pass)).astype(jnp.bfloat16)
    return (real_complete, imaginary_complete)

def patch_energy(patches):
    values = patches.astype(jnp.float32)
    return lax.optimization_barrier(jnp.mean(values * values, axis=(1, 2))) + EPS

def displacement(current, current_energy, later, later_energy, tables):
    back_cos, back_sin = (tables[2], tables[3])
    shift_count, patch_size = back_cos.shape
    first_real = current[0].astype(jnp.float32)
    first_imag = current[1].astype(jnp.float32)
    second_real = later[0].astype(jnp.float32)
    second_imag = later[1].astype(jnp.float32)
    cross_real = (first_real * second_real + first_imag * second_imag).astype(jnp.bfloat16)
    cross_imag = (first_real * second_imag - first_imag * second_real).astype(jnp.bfloat16)
    half_real = (spectral_product('uk,jkm->jum', back_cos, cross_real) - spectral_product('uk,jkm->jum', back_sin, cross_imag)).astype(jnp.bfloat16)
    half_imag = (spectral_product('uk,jkm->jum', back_cos, cross_imag) + spectral_product('uk,jkm->jum', back_sin, cross_real)).astype(jnp.bfloat16)
    correlation = (spectral_product('jum,vm->juv', half_real, back_cos) - spectral_product('jum,vm->juv', half_imag, back_sin)) / float(patch_size * patch_size)
    scale_term = patch_size * patch_size * jnp.sqrt(current_energy * later_energy)
    weights = jnp.exp(patch_size / 2.0 * correlation / scale_term[:, None, None])
    total = lax.optimization_barrier(jnp.sum(weights, axis=(1, 2)))
    shift_values = (jnp.arange(shift_count, dtype=jnp.int32) - shift_count // 2).astype(jnp.float32)
    along_rows = lax.optimization_barrier(jnp.sum(weights * shift_values[None, :, None], axis=(1, 2))) / total
    along_cols = lax.optimization_barrier(jnp.sum(weights * shift_values[None, None, :], axis=(1, 2))) / total
    return jnp.stack([along_rows, along_cols], 0)

def relax_step(field, pull):
    zero_layer = jnp.zeros_like(field[:1])
    following = jnp.concatenate([field[1:], zero_layer], 0)
    spring = field - following - pull
    earlier = jnp.concatenate([zero_layer, spring[:-1]], 0)
    framed = jnp.pad(field, ((0, 0), (0, 0), (1, 1), (1, 1)))
    beside_all = framed[:, :, 2:, 1:-1] + framed[:, :, :-2, 1:-1] + framed[:, :, 1:-1, 2:] + framed[:, :, 1:-1, :-2]
    return field - STEP_RATE * (spring - earlier + 4.0 * field - beside_all)

def warp_one(items):
    section_pad, offsets, mesh_one = items
    shift_rows = jnp.repeat(jnp.repeat(mesh_one[0], STRIDE, 0), STRIDE, 1)
    shift_cols = jnp.repeat(jnp.repeat(mesh_one[1], STRIDE, 0), STRIDE, 1)
    row_frac = shift_rows - offsets[0].astype(jnp.float32)
    col_frac = shift_cols - offsets[1].astype(jnp.float32)
    row_base = jnp.arange(HEIGHT, dtype=jnp.int32)[:, None] + offsets[0] + HALO
    col_base = jnp.arange(COLS, dtype=jnp.int32)[None, :] + offsets[1] + HALO
    pixels = section_pad.astype(jnp.float32)
    upper = (1.0 - col_frac) * pixels[row_base, col_base] + col_frac * pixels[row_base, col_base + 1]
    lower = (1.0 - col_frac) * pixels[row_base + 1, col_base] + col_frac * pixels[row_base + 1, col_base + 1]
    return (1.0 - row_frac) * upper + row_frac * lower

def assemble(tiled):
    count = tiled.shape[0]
    joined = tiled.reshape(count, GRID_ROWS, TILE_GRID, TILE_ROWS, TILE_COLS)
    return jnp.transpose(joined, (0, 1, 3, 2, 4)).reshape(count, HEIGHT, COLS)

def reference(sections, corner_offsets):
    tables = dft_tables(PATCH, SHIFTS)
    image = assemble(sections)
    offsets_whole = assemble(corner_offsets.reshape(2 * SECTIONS, N_TILE, TILE_ROWS, TILE_COLS)).reshape(2, SECTIONS, HEIGHT, COLS)
    padded = jnp.pad(image, ((0, 0), (HALO, HALO), (HALO, HALO)))
    has_next = (jnp.arange(SECTIONS, dtype=jnp.int32) < SECTIONS - 1).astype(jnp.float32)

    def node_row(row_number):
        row_band = lax.dynamic_slice_in_dim(padded, row_number * STRIDE, PATCH, 1)
        patches = window_patches(row_band, STRIDE)
        flat = patches.reshape(SECTIONS * NODE_COLS, PATCH, PATCH)
        spec_real, spec_imag = spectrum(flat, tables)
        energy = patch_energy(flat).reshape(SECTIONS, NODE_COLS)
        spec_real = spec_real.reshape(SECTIONS, NODE_COLS, PATCH, PATCH)
        spec_imag = spec_imag.reshape(SECTIONS, NODE_COLS, PATCH, PATCH)
        next_real = jnp.concatenate([spec_real[1:], jnp.zeros_like(spec_real[:1])], 0)
        next_imag = jnp.concatenate([spec_imag[1:], jnp.zeros_like(spec_imag[:1])], 0)
        next_energy = jnp.concatenate([energy[1:], jnp.full((1, NODE_COLS), EPS, jnp.float32)], 0)
        flows = displacement((spec_real.reshape(-1, PATCH, PATCH), spec_imag.reshape(-1, PATCH, PATCH)), energy.reshape(-1), (next_real.reshape(-1, PATCH, PATCH), next_imag.reshape(-1, PATCH, PATCH)), next_energy.reshape(-1), tables)
        return flows.reshape(2, SECTIONS, NODE_COLS)
    flow = lax.map(node_row, jnp.arange(NODE_ROWS, dtype=jnp.int32))
    flow = jnp.transpose(flow, (2, 1, 0, 3)) * has_next[:, None, None, None]
    node_mesh = jnp.zeros_like(flow)
    for step_number in range(ITERS):
        node_mesh = relax_step(node_mesh, flow)
    warped = lax.map(warp_one, (padded, jnp.transpose(offsets_whole, (1, 0, 2, 3)), node_mesh))
    warped_tiles = jnp.transpose(warped.reshape(SECTIONS, GRID_ROWS, TILE_ROWS, TILE_GRID, TILE_COLS), (0, 1, 3, 2, 4))
    warped_tiles = warped_tiles.reshape(SECTIONS, N_TILE, TILE_ROWS, TILE_COLS)
    mesh_tiles = node_mesh.reshape(SECTIONS, 2, GRID_ROWS, TILE_NODE_ROWS, TILE_GRID, TILE_NODE_COLS)
    mesh_tiles = jnp.transpose(mesh_tiles, (0, 1, 2, 4, 3, 5)).reshape(SECTIONS, 2, N_TILE, TILE_NODE_ROWS, TILE_NODE_COLS)
    return (mesh_tiles, warped_tiles)
```

```python
import math

import jax
import jax.numpy as jnp
import ml_dtypes
import numpy as np
from jax import lax
from jax.experimental import pallas as pl
from jax.experimental.pallas import tpu as pltpu
from jax.sharding import PartitionSpec as P

TILE_GRID = 8
PATCH = 128
STRIDE = 32
SHIFTS = 32
ITERS = 4
HALO = 48
EPS = 1e-05
STEP_RATE = 0.15
ROWS = 352
LANES = 640
OWN_LANES = 512
F32 = jnp.float32
BF16 = jnp.bfloat16


def build_tables():
    k = np.arange(PATCH)
    u = np.arange(SHIFTS) - SHIFTS // 2

    def cos_of(m):
        return np.cos(2 * np.pi * (m % PATCH) / PATCH)

    def sin_of(m):
        return np.sin(2 * np.pi * (m % PATCH) / PATCH)

    c, s = cos_of(np.outer(k, k)), sin_of(np.outer(k, k))
    gc, gs = cos_of(np.outer(u, k)), sin_of(np.outer(u, k))
    row_pass = np.zeros((2, 256, 256))
    for half in range(2):
        for w in range(2):
            start = 16 + 64 * half + 32 * w
            row_pass[half, start : start + 128, 64 * w : 64 * w + 64] = c[:, :64]
            row_pass[half, start : start + 128, 128 + 64 * w : 192 + 64 * w] = -s[:, :64]
    row_last = np.zeros((LANES, 128))
    for i in range(8):
        for j in range(16):
            lanes = (32 * j - HALO + k) % LANES
            row_last[lanes, 16 * i + j] = (-1.0) ** k
    col_pass = np.block([[c, s], [-s, c]])
    back_rows = np.block([[gc, -gs], [gs, gc]])
    factor = np.where(np.arange(64) == 0, 1.0, 2.0)[:, None]
    back_cols = np.zeros((512, 128))
    for jj in range(4):
        back_cols[64 * jj : 64 * jj + 64, 32 * jj : 32 * jj + 32] = factor * gc[:, :64].T
        back_cols[256 + 64 * jj : 320 + 64 * jj, 32 * jj : 32 * jj + 32] = -factor * gs[:, :64].T
    back_last = np.zeros((128, 512))
    for i in range(8):
        for j in range(16):
            back_last[16 * i + j, 32 * j : 32 * j + 32] = (-1.0) ** np.arange(32)
    energy_cols = np.zeros((384, 128))
    for jj in range(4):
        energy_cols[128 + 32 * jj - HALO : 256 + 32 * jj - HALO, 32 * jj : 32 * jj + 32] = 1.0
    sums = np.zeros((256, 256))
    for lane in range(128):
        jj, comp = lane % 4, (lane // 32) % 2
        sums[32 * jj : 32 * jj + 32, lane] = 1.0
        if comp == 0:
            sums[128 + 32 * jj : 160 + 32 * jj, 128 + lane] = 1.0
        else:
            sums[32 * jj : 32 * jj + 32, 128 + lane] = u
    tables = {
        "row_first": row_pass[0], "row_second": row_pass[1], "row_last": row_last, "col_pass": col_pass,
        "back_rows": back_rows, "back_cols": back_cols, "back_last": back_last, "energy_cols": energy_cols, "sums": sums,
    }
    places, pieces, base = {}, [], 0
    for name, table in tables.items():
        rows, tiles = table.shape[0], table.shape[1] // 128
        places[name] = (base, rows, tiles)
        pieces += [table[:, 128 * t : 128 * t + 128] for t in range(tiles)]
        base += rows * tiles
    packed = np.concatenate(pieces, axis=0).astype(np.float32).astype(ml_dtypes.bfloat16)
    return places, packed


PLACES, PACKED = build_tables()


class Table:
    def __init__(self, ref, name):
        self.ref = ref
        self.base, self.rows, self.tiles = PLACES[name]

    def read(self, rows=None, tiles=None):
        rows = rows or slice(0, self.rows)
        tiles = range(self.tiles) if tiles is None else tiles
        starts = [self.base + t * self.rows for t in tiles]
        parts = [self.ref[b + rows.start : b + rows.stop, :] for b in starts]
        return parts[0] if len(parts) == 1 else jnp.concatenate(parts, axis=1)


def mm(a, b):
    return jnp.dot(a, b, preferred_element_type=F32)


def split3(x):
    hi = x.astype(BF16)
    rest = x - hi.astype(F32)
    mid = rest.astype(BF16)
    low = (rest - mid.astype(F32)).astype(BF16)
    return jnp.concatenate([hi, mid, low], axis=0)


def mm_exact(x, w):
    n = x.shape[0]
    y = mm(split3(x), w)
    return y[:n] + y[n : 2 * n] + y[2 * n :]


def tile_lanes(block, t):
    if t == 0:
        return jnp.concatenate([block[:, 512:640], block[:, 0:128]], axis=1)
    return block[:, 128 * (t - 1) : 128 * (t + 1)]


def row_transform(s, pad, ri, row_pass):
    for jp in range(8):
        t, half = (jp + 1) // 2, (jp + 1) % 2
        y = mm(tile_lanes(pad[s], t), row_pass[half].read()).astype(BF16)
        ri[s, 0, :, 128 * jp : 128 * jp + 128] = y[:, :128]
        ri[s, 1, :, 128 * jp : 128 * jp + 128] = y[:, 128:]


def last_spectrum(s, pad, nq, spec_last, row_last, col_pass):
    nq[...] = mm(pad[s], row_last.read())
    lane = lax.broadcasted_iota(jnp.int32, (128, 128), 1) // 16
    picked = nq[0:128, :]
    for i in range(1, 8):
        picked = jnp.where(lane == i, nq[32 * i : 32 * i + 128, :], picked)
    spec_last[s] = mm(col_pass.read(tiles=[0]), picked.astype(BF16))


def energies(s, pad, eb, en, energy_cols):
    for b in range(11):
        x = pad[s, 32 * b : 32 * b + 32, :].astype(F32)
        eb[b : b + 1, :] = jnp.sum(x * x, axis=0, keepdims=True)
    e4 = eb[0:8, :] + eb[1:9, :] + eb[2:10, :] + eb[3:11, :]
    tiles = [e4[:, 128 * t : 128 * t + 128] for t in range(5)]
    rows = [jnp.concatenate([tiles[(q - 1) % 5], tiles[q], tiles[q + 1]], axis=1) for q in range(4)]
    y = mm_exact(jnp.concatenate(rows, axis=0), energy_cols.read())
    for q in range(4):
        en[s, q] = y[8 * q : 8 * q + 8] * (1.0 / PATCH**2) + EPS


def cross_half(x0, x1, back_rows):
    ar, ai, br, bi = x0[:128], x0[128:], x1[:128], x1[128:]
    cross = jnp.concatenate(
        [(ar * br + ai * bi).astype(BF16), (ar * bi - ai * br).astype(BF16)], axis=0
    )
    return mm(back_rows, cross)


def spectrum_of(s, i, lanes, ri, col_pass):
    rows = pl.ds(pl.multiple_of(32 * i, 32), 128)
    rhs = jnp.concatenate([ri[s, 0, rows, lanes], ri[s, 1, rows, lanes]], axis=0)
    return mm(col_pass.read(), rhs)


def store_half(half, pair, i, chunk, h):
    for t in range(2):
        half[pair, 2 * chunk + t, pl.ds(i, 64, stride=8), :] = h[:, 128 * t : 128 * t + 128]


def load_half(half, pair, rows, q):
    pieces = [half[pair, 2 * q + t, rows, :].astype(BF16) for t in range(2)]
    return jnp.concatenate(pieces, axis=1)


def first_pair(i, ri, spec, half, col_pass, back_rows):
    for chunk in range(4):
        lanes = slice(256 * chunk, 256 * chunk + 256)
        x0 = spectrum_of(0, i, lanes, ri, col_pass)
        x1 = spectrum_of(1, i, lanes, ri, col_pass)
        spec[i, :, lanes] = x1.astype(BF16)
        store_half(half, 0, i, chunk, cross_half(x0, x1, back_rows.read()))


def second_pair(i, ri, spec, half, col_pass, back_rows):
    for chunk in range(4):
        lanes = slice(256 * chunk, 256 * chunk + 256)
        x1 = spec[i, :, lanes].astype(F32)
        x2 = spectrum_of(2, i, lanes, ri, col_pass)
        store_half(half, 1, i, chunk, cross_half(x1, x2, back_rows.read()))


def pair_sums(pair, half, spec_last, en, sums_in, back_rows, back_cols, back_last):
    h_last = cross_half(spec_last[pair], spec_last[pair + 1], back_rows.read(slice(0, 32)))
    lane = lax.broadcasted_iota(jnp.int32, (8, 128), 1) // 16
    own_row = lane == lax.broadcasted_iota(jnp.int32, (8, 128), 0)
    spread = [jnp.where(own_row, h_last[u : u + 1, :], 0.0) for u in range(SHIFTS)]
    spread = jnp.concatenate(spread, axis=0).astype(BF16)
    for q in range(4):
        corr = mm(load_half(half, pair, slice(0, 256), q), back_cols.read(slice(0, 256)))
        corr += mm(load_half(half, pair, slice(256, 512), q), back_cols.read(slice(256, 512)))
        corr += mm(spread, back_last.read(tiles=[q]))
        scale = (PATCH / 2.0 / PATCH**4) * lax.rsqrt(en[pair, q] * en[pair + 1, q])
        total = jnp.zeros((8, 128), F32)
        along = jnp.zeros((8, 128), F32)
        for u in range(SHIFTS):
            w = jnp.exp(corr[8 * u : 8 * u + 8] * scale)
            total += w
            along += w * float(u - SHIFTS // 2)
        sums_in[32 * pair + 8 * q : 32 * pair + 8 * q + 8, 0:128] = total
        sums_in[32 * pair + 8 * q : 32 * pair + 8 * q + 8, 128:256] = along


def flow_block(sums_in, sums, last_sec):
    y = mm_exact(sums_in[...], sums.read())
    flow = y[:, 128:] / y[:, :128]
    lane = lax.broadcasted_iota(jnp.int32, (8, 128), 1)
    block = jnp.zeros((8, 128), F32)
    for pair in range(2):
        for q in range(4):
            first = 8 + 4 * q
            mine = (lane // 64 == pair) & (lane % 32 >= first) & (lane % 32 < first + 4)
            r = 32 * pair + 8 * q
            block = jnp.where(mine, flow[r : r + 8], block)
    return jnp.where((lane >= 64) & last_sec, 0.0, block)


def extend(own, left, right):
    lane = lax.broadcasted_iota(jnp.int32, own.shape, own.ndim - 1) % 32
    from_left = pltpu.roll(left, 112, own.ndim - 1)
    from_right = pltpu.roll(right, 16, own.ndim - 1)
    return jnp.where(lane < 8, from_left, jnp.where(lane >= 24, from_right, own))


def relax(flow, row_pos, col_pos):
    shape = flow[0].shape
    row = lax.broadcasted_iota(jnp.int32, shape, 0)
    lane = lax.broadcasted_iota(jnp.int32, shape, 1)
    node = lane % 32
    inside = ((row >= 8) | (row_pos > 0)) & ((row < 16) | (row_pos < TILE_GRID - 1))
    inside &= ((node >= 8) | (col_pos > 0)) & ((node < 24) | (col_pos < TILE_GRID - 1))
    mask = jnp.where(inside, 1.0, 0.0)
    low = lane < 64
    count = len(flow)
    zero = jnp.zeros(shape, F32)

    def following(f):
        turned = [pltpu.roll(x, 64, 1) for x in f] + [zero]
        return [jnp.where(low, turned[d], turned[d + 1]) for d in range(count)]

    def preceding(f):
        turned = [zero] + [pltpu.roll(x, 64, 1) for x in f]
        return [jnp.where(low, turned[d], turned[d + 1]) for d in range(count)]

    flow = [f * mask for f in flow]
    mesh = [zero] * count
    for step in range(ITERS):
        if step == 0:
            spring = [-f for f in flow]
        else:
            spring = [m - n - f for m, n, f in zip(mesh, following(mesh), flow)]
        earlier = preceding(spring)
        updated = []
        for m, sp, ea in zip(mesh, spring, earlier):
            change = sp - ea
            if step > 0:
                around = pltpu.roll(m, 1, 0) + pltpu.roll(m, 23, 0) + pltpu.roll(m, 1, 1) + pltpu.roll(m, 127, 1)
                change = change + 4.0 * m - around
            updated.append((m - STEP_RATE * change) * mask)
        mesh = updated
    return mesh


def pick_four(code, values):
    low = jnp.where(code == -2, values[0], values[1])
    high = jnp.where(code == 0, values[2], values[3])
    return jnp.where(code < 0, low, high)


def shifted_columns(s, r, pad, cols):
    x = pad[s, pl.ds(pl.multiple_of(32 * r + 32, 32), 64), :].astype(F32)[8:56]
    for d in range(5):
        y = x if d == 2 else pltpu.roll(x, (2 - d) % LANES, 1)
        cols[d] = y[:, :OWN_LANES]


def corners(s, r, offsets, cols, coef):
    band = pl.ds(pl.multiple_of(32 * r, 32), 32)
    for q in range(4):
        lanes = slice(128 * q, 128 * q + 128)
        ro = offsets[0, s, 0, band, lanes]
        co = offsets[1, s, 0, band, lanes]
        left, right = [], []
        for dr in range(-2, 3):
            v = [cols[d, 8 + dr : 40 + dr, lanes] for d in range(5)]
            left.append(pick_four(co, v[0:4]))
            right.append(pick_four(co, v[1:5]))
        i00, i10 = pick_four(ro, left[0:4]), pick_four(ro, left[1:5])
        i01, i11 = pick_four(ro, right[0:4]), pick_four(ro, right[1:5])
        rf, cf = ro.astype(F32), co.astype(F32)
        top, low = i01 - i00, i11 - i10
        top0, low0 = i00 - cf * top, i10 - cf * low
        twist, lean = low - top, low0 - top0
        coef[0, s, band, lanes] = top0 - rf * lean
        coef[1, s, band, lanes] = lean
        coef[2, s, band, lanes] = top - rf * twist
        coef[3, s, band, lanes] = twist


def write_mesh(mesh, out):
    for s in range(2):
        for c in range(2):
            lane = 64 * s + 32 * c + 8
            out[s, c, 0] = mesh[:, lane : lane + 16]


def spread_lanes(mesh, s, c, q):
    lane = lax.broadcasted_iota(jnp.int32, (8, 128), 1)
    return jnp.take_along_axis(mesh, 64 * s + 32 * c + 8 + 4 * q + lane // 32, axis=1)


def blend(s, mesh, coef, out):
    for q in range(4):
        lanes = slice(128 * q, 128 * q + 128)
        mr, mc = spread_lanes(mesh, s, 0, q), spread_lanes(mesh, s, 1, q)
        for r in range(8):
            band = slice(32 * r, 32 * r + 32)
            a, b = mr[r : r + 1], mc[r : r + 1]
            first = coef[0, s, band, lanes] + a * coef[1, s, band, lanes]
            second = coef[2, s, band, lanes] + a * coef[3, s, band, lanes]
            out[s, 0, band, lanes] = first + b * second


MESH = pl.DeviceIdType.MESH
AROUND = [(0, -1), (0, 1), (-1, 0), (1, 0), (-1, -1), (-1, 1), (1, -1), (1, 1)]


def pixel_part(dr, dc, sections, pad, from_left, from_right, src, dst):
    src_rows = {-1: pl.ds(0, HALO), 0: pl.ds(0, 256), 1: pl.ds(256 - HALO, HALO)}[dr]
    dst_rows = {-1: pl.ds(HALO + 256, HALO), 0: pl.ds(HALO, 256), 1: pl.ds(0, HALO)}[dr]
    if dc == 0:
        return sections.at[src, 0, src_rows, :], pad.at[dst, dst_rows, pl.ds(0, OWN_LANES)]
    if dc < 0:
        return sections.at[src, 0, src_rows, pl.ds(0, 128)], from_right.at[dst, dst_rows, :]
    return sections.at[src, 0, src_rows, pl.ds(OWN_LANES - 128, 128)], from_left.at[dst, dst_rows, :]


def merge_sides(s, rows, pad, from_left, from_right, col_pos):
    lane = lax.broadcasted_iota(jnp.int32, (rows.stop - rows.start, 128), 1)
    side = jnp.where(lane < 64, from_right[s, rows, :].astype(F32), from_left[s, rows, :].astype(F32))
    keep = ((lane < 64) & (col_pos < TILE_GRID - 1)) | ((lane >= 64) & (col_pos > 0))
    pad[s, rows, OWN_LANES:LANES] = jnp.where(keep, side, 0.0).astype(BF16)


def clear_edges(first, count, pad, row_pos):
    @pl.when(row_pos == 0)
    def _():
        pad[first : first + count, 0:HALO, :] = jnp.zeros((count, HALO, LANES), BF16)

    @pl.when(row_pos == TILE_GRID - 1)
    def _():
        pad[first : first + count, ROWS - HALO : ROWS, :] = jnp.zeros((count, HALO, LANES), BF16)


def whole_kernel(sections, offsets_in, packed, mesh_out, warped,
                 pad, from_left, from_right, offsets, ri, spec, half, nq, spec_last, eb, en, sums_in, flows, cols, coef,
                 local_sem, pixel_send, pixel_recv, sec_send, sec_recv, near_send, near_recv):
    row_pass = [Table(packed, "row_first"), Table(packed, "row_second")]
    row_last, col_pass, back_rows, back_cols, back_last, energy_cols, sums = (
        Table(packed, name)
        for name in ("row_last", "col_pass", "back_rows", "back_cols", "back_last", "energy_cols", "sums")
    )
    sec, tile = lax.axis_index("sec"), lax.axis_index("tile")
    sec_count = lax.axis_size("sec")
    row_pos, col_pos = tile // TILE_GRID, tile % TILE_GRID

    def device(ds, dr, dc):
        row = lax.rem(row_pos + (dr + TILE_GRID), TILE_GRID)
        col = lax.rem(col_pos + (dc + TILE_GRID), TILE_GRID)
        return (lax.rem(sec + ds, sec_count), row * TILE_GRID + col)

    own_copy = pltpu.make_async_copy(
        sections.at[:, 0], pad.at[pl.ds(0, 2), pl.ds(HALO, 256), pl.ds(0, OWN_LANES)], local_sem.at[0]
    )
    offset_copy = pltpu.make_async_copy(offsets_in, offsets, local_sem.at[1])
    own_copy.start()
    offset_copy.start()

    barrier = pltpu.get_barrier_semaphore()
    partners = [(0, dr, dc) for dr, dc in AROUND] + [(2, 0, 0)]
    partners += [(ds, dr, dc) for ds in (1, 3) for dr, dc in AROUND + [(0, 0)]]
    for p in partners:
        pl.semaphore_signal(barrier, inc=1, device_id=device(*p), device_id_type=MESH)
    pl.semaphore_wait(barrier, len(partners))

    def pixel_copy(k, ds, dr, dc, src, dst):
        src_ref, dst_ref = pixel_part(dr, dc, sections, pad, from_left, from_right, src, dst)
        return pltpu.make_async_remote_copy(
            src_ref=src_ref, dst_ref=dst_ref, send_sem=pixel_send.at[k], recv_sem=pixel_recv.at[k],
            device_id=device(ds, dr, dc), device_id_type=MESH,
        )

    both, first, third = pl.ds(0, 2), pl.ds(0, 1), pl.ds(2, 1)
    own = [pixel_copy(k, 0, dr, dc, both, both) for k, (dr, dc) in enumerate(AROUND)]
    after = [pixel_copy(8 + k, 3, dr, dc, first, third) for k, (dr, dc) in enumerate([(0, 0)] + AROUND)]
    for copy in own + after:
        copy.start()

    def bands(s, start, step, count):
        @pl.loop(0, count)
        def _(k):
            r = start + step * k
            shifted_columns(s, r, pad, cols)
            corners(s, r, offsets, cols, coef)

    own_copy.wait()
    own[0].wait_recv()
    own[1].wait_recv()
    offset_copy.wait()
    for s in range(2):
        merge_sides(s, slice(HALO, HALO + 256), pad, from_left, from_right, col_pos)
        bands(s, 1, 1, 6)
    for copy in own[2:]:
        copy.wait_recv()
    for s in range(2):
        merge_sides(s, slice(0, HALO), pad, from_left, from_right, col_pos)
        merge_sides(s, slice(HALO + 256, ROWS), pad, from_left, from_right, col_pos)
    clear_edges(0, 2, pad, row_pos)

    def transform(s):
        row_transform(s, pad, ri, row_pass)
        last_spectrum(s, pad, nq, spec_last, row_last, col_pass)
        energies(s, pad, eb, en, energy_cols)

    transform(0)
    transform(1)

    @pl.loop(0, 8)
    def _(i):
        first_pair(i, ri, spec, half, col_pass, back_rows)

    for copy in after:
        copy.wait_recv()
    merge_sides(2, slice(0, ROWS), pad, from_left, from_right, col_pos)
    clear_edges(2, 1, pad, row_pos)
    transform(2)

    @pl.loop(0, 8)
    def _(i):
        second_pair(i, ri, spec, half, col_pass, back_rows)

    for pair in range(2):
        pair_sums(pair, half, spec_last, en, sums_in, back_rows, back_cols, back_last)
    flows[4, sec] = flow_block(sums_in, sums, sec == sec_count - 1)

    along = [
        pltpu.make_async_remote_copy(
            src_ref=flows.at[4, sec], dst_ref=flows.at[4, sec], send_sem=sec_send.at[ds - 1],
            recv_sem=sec_recv.at[ds - 1], device_id=device(ds, 0, 0), device_id_type=MESH,
        )
        for ds in (1, 2, 3)
    ]
    for copy in along:
        copy.start()
    bands(0, 0, 7, 2)
    for copy in along:
        copy.wait_recv()
    beside = [
        pltpu.make_async_remote_copy(
            src_ref=flows.at[4], dst_ref=flows.at[3 * (1 - dr) + 1 - dc], send_sem=near_send.at[k],
            recv_sem=near_recv.at[k], device_id=device(0, dr, dc), device_id_type=MESH,
        )
        for k, (dr, dc) in enumerate(AROUND)
    ]
    for copy in beside:
        copy.start()
    bands(1, 0, 7, 2)
    for copy in beside:
        copy.wait_recv()

    def column(d, c):
        return jnp.concatenate([flows[c, d], flows[3 + c, d], flows[6 + c, d]], axis=0)

    mesh = relax([extend(column(d, 1), column(d, 0), column(d, 2)) for d in range(4)], row_pos, col_pos)
    mine = mesh[0][8:16]
    for d in range(1, 4):
        mine = jnp.where(sec == d, mesh[d][8:16], mine)
    write_mesh(mine, mesh_out)
    for s in range(2):
        blend(s, mine, coef, warped)
    for copy in own + after + along + beside:
        copy.wait_send()


def vmem():
    return pl.BlockSpec(memory_space=pltpu.VMEM)


def shards(sections, corner_offsets):
    anywhere = pl.BlockSpec(memory_space=pl.ANY)
    dma = pltpu.SemaphoreType.DMA
    return pl.pallas_call(
        whole_kernel,
        out_shape=(
            jax.ShapeDtypeStruct((2, 2, 1, 8, 16), F32),
            jax.ShapeDtypeStruct((2, 1, 256, 512), F32),
        ),
        in_specs=[anywhere, anywhere, vmem()],
        out_specs=(vmem(), vmem()),
        scratch_shapes=[
            pltpu.VMEM((3, ROWS, LANES), BF16),
            pltpu.VMEM((3, ROWS, 128), BF16),
            pltpu.VMEM((3, ROWS, 128), BF16),
            pltpu.VMEM((2, 2, 1, 256, OWN_LANES), jnp.int32),
            pltpu.VMEM((3, 2, ROWS, 1024), BF16),
            pltpu.VMEM((8, 256, 1024), BF16),
            pltpu.VMEM((2, 8, 512, 128), F32),
            pltpu.VMEM((ROWS, 128), F32),
            pltpu.VMEM((3, 256, 128), F32),
            pltpu.VMEM((16, LANES), F32),
            pltpu.VMEM((3, 4, 8, 128), F32),
            pltpu.VMEM((64, 256), F32),
            pltpu.VMEM((9, 4, 8, 128), F32),
            pltpu.VMEM((5, 48, OWN_LANES), F32),
            pltpu.VMEM((4, 2, 256, OWN_LANES), F32),
            dma((2,)),
            dma((17,)),
            dma((17,)),
            dma((3,)),
            dma((3,)),
            dma((8,)),
            dma((8,)),
        ],
        compiler_params=pltpu.CompilerParams(
            vmem_limit_bytes=60 * 2**20, collective_id=0, has_side_effects=True
        ),
    )(sections, corner_offsets, jnp.asarray(PACKED))


def solution(mesh):
    in_specs = (P("sec", "tile", None, None), P(None, "sec", "tile", None, None))
    out_specs = (P("sec", None, "tile", None, None), P("sec", "tile", None, None))
    return jax.shard_map(shards, mesh=mesh, in_specs=in_specs, out_specs=out_specs, check_vma=False)
```

```python
import math

import jax
import jax.numpy as jnp
import ml_dtypes
import numpy as np
from jax import lax
from jax.experimental import pallas as pl
from jax.experimental.pallas import tpu as pltpu
from jax.sharding import PartitionSpec as P

TILE_GRID = 8
PATCH = 128
STRIDE = 32
SHIFTS = 32
ITERS = 4
HALO = 48
EPS = 1e-05
STEP_RATE = 0.15
ROWS = 352
LANES = 640
OWN_LANES = 512
F32 = jnp.float32
BF16 = jnp.bfloat16


def build_tables():
    k = np.arange(PATCH)
    u = np.arange(SHIFTS) - SHIFTS // 2

    def cos_of(m):
        return np.cos(2 * np.pi * (m % PATCH) / PATCH)

    def sin_of(m):
        return np.sin(2 * np.pi * (m % PATCH) / PATCH)

    c, s = cos_of(np.outer(k, k)), sin_of(np.outer(k, k))
    gc, gs = cos_of(np.outer(u, k)), sin_of(np.outer(u, k))
    factor = np.where(k[:64] == 0, 1.0, 2.0)
    first = []
    for count, shift, slot in ((4, 16, 0), (2, 0, 0), (2, 96, 2)):
        table = np.zeros((128 * count + 16, 256))
        for i in range(count):
            rows = slice(32 * i + shift, 32 * i + shift + 128)
            table[i : 64 * count : count, rows] = c[:64]
            table[64 * count + i : 128 * count : count, rows] = -s[:64]
            table[128 * count + slot + i, rows] = (-1.0) ** k
        first.append(table)
    second = np.block([[c, -s], [s, c]])
    back_second = np.zeros((1024, 256))
    for w in range(4):
        rows, lanes = 256 * w, 32 * w
        back_second[rows : rows + 128, lanes : lanes + 32] = gc.T
        back_second[rows + 128 : rows + 256, lanes : lanes + 32] = -gs.T
        back_second[rows : rows + 128, 128 + lanes : 160 + lanes] = gs.T
        back_second[rows + 128 : rows + 256, 128 + lanes : 160 + lanes] = gc.T
    inner, outer = np.zeros((128, 512)), np.zeros((128, 512))
    for i in range(4):
        inner[i::4, i:256:4] = factor * gc[:, :64]
        inner[i::4, 256 + i : 512 : 4] = -factor * gs[:, :64]
        start = 128 * (i // 2) + i % 2
        outer[i::4, start : 128 * (i // 2) + 128 : 2] = factor * gc[:, :64]
        outer[i::4, 256 + start : 384 + 128 * (i // 2) : 2] = -factor * gs[:, :64]
    energy_cols = np.zeros((384, 128))
    for jj in range(4):
        energy_cols[128 + 32 * jj - HALO : 256 + 32 * jj - HALO, 32 * jj : 32 * jj + 32] = 1.0
    sums = np.zeros((256, 256))
    for lane in range(128):
        jj, comp = lane % 4, (lane // 32) % 2
        sums[32 * jj : 32 * jj + 32, lane] = 1.0
        if comp == 0:
            sums[128 + 32 * jj : 160 + 32 * jj, 128 + lane] = 1.0
        else:
            sums[32 * jj : 32 * jj + 32, 128 + lane] = u
    tables = {
        "inner": first[0], "upper": first[1], "lower": first[2], "second": second, "back_second": back_second,
        "back_first": np.concatenate([inner, outer], axis=0), "energy_cols": energy_cols, "sums": sums,
    }
    places, pieces, base = {}, [], 0
    for name, table in tables.items():
        rows, tiles = table.shape[0], table.shape[1] // 128
        places[name] = (base, rows, tiles)
        pieces += [table[:, 128 * t : 128 * t + 128] for t in range(tiles)]
        base += rows * tiles
    packed = np.concatenate(pieces, axis=0).astype(np.float32).astype(ml_dtypes.bfloat16)
    return places, packed


PLACES, PACKED = build_tables()


class Table:
    def __init__(self, ref, name):
        self.ref = ref
        self.base, self.rows, self.tiles = PLACES[name]

    def read(self, rows=None, tiles=None):
        rows = rows or slice(0, self.rows)
        tiles = range(self.tiles) if tiles is None else tiles
        starts = [self.base + t * self.rows for t in tiles]
        parts = [self.ref[b + rows.start : b + rows.stop, :] for b in starts]
        return parts[0] if len(parts) == 1 else jnp.concatenate(parts, axis=1)

    def read_part(self, part, rows):
        starts = [self.base + t * self.rows for t in range(self.tiles)]
        parts = [self.ref[pl.ds(pl.multiple_of(b + part * rows, 16), rows), :] for b in starts]
        return jnp.concatenate(parts, axis=1)


def mm(a, b):
    return jnp.dot(a, b, preferred_element_type=F32)


def split3(x):
    hi = x.astype(BF16)
    rest = x - hi.astype(F32)
    mid = rest.astype(BF16)
    low = (rest - mid.astype(F32)).astype(BF16)
    return jnp.concatenate([hi, mid, low], axis=0)


def mm_exact(x, w):
    n = x.shape[0]
    y = mm(split3(x), w)
    return y[:n] + y[n : 2 * n] + y[2 * n :]


def block_energies(s, blocks, lanes, pad, eb):
    for b in blocks:
        x = pad[s, 32 * b : 32 * b + 32, lanes].astype(F32)
        eb[s, b : b + 1, lanes] = jnp.sum(x * x, axis=0, keepdims=True)


def node_energies(s, columns, eb, en, energy_cols):
    e4 = eb[s, 0:8, :] + eb[s, 1:9, :] + eb[s, 2:10, :] + eb[s, 3:11, :]
    tiles = [e4[:, 128 * t : 128 * t + 128] for t in range(5)]
    rows = [jnp.concatenate([tiles[(q - 1) % 5], tiles[q], tiles[q + 1]], axis=1) for q in columns]
    y = mm_exact(jnp.concatenate(rows, axis=0), energy_cols.read())
    row = lax.broadcasted_iota(jnp.int32, (8, 128), 0)
    for n, q in enumerate(columns):
        e = y[8 * n : 8 * n + 8] * (1.0 / PATCH**2) + EPS
        en[s, INNER, q] = jnp.where(row < 4, pltpu.roll(e, 6, 0), pltpu.roll(e, 2, 0))
        en[s, OUTER, q] = jnp.where((row < 2) | (row >= 6), e, pltpu.roll(e, 4, 0))


INNER, OUTER = 0, 1
OWN_COLS, SIDE_COLS = (slice(0, 256), slice(256, 512)), (slice(512, 640),)


def first_transform(s, group, columns, pad, spec, tables):
    for lanes in columns:
        if group == INNER:
            parts = [(0, 256, mm(tables["inner"].read(), pad[s, HALO : HALO + 256, lanes]))]
        else:
            parts = [
                (0, 128, mm(tables["upper"].read(), pad[s, 0:256, lanes])),
                (128, 128, mm(tables["lower"].read(), pad[s, 96:352, lanes])),
            ]
        for n in range((lanes.stop - lanes.start) // 128):
            t = (lanes.start // 128 + n + 1) % 5
            cols = slice(128 * n, 128 * n + 128)
            last = None
            for row, count, y in parts:
                spec[s, group, t, 0, row : row + count, :] = y[0:count, cols].astype(BF16)
                spec[s, group, t, 1, row : row + count, :] = y[count : 2 * count, cols].astype(BF16)
                end = y[2 * count : 2 * count + 16, cols]
                last = end if last is None else last + end
            spec[s, group, t, 0, 256:272, :] = last.astype(BF16)
            spec[s, group, t, 1, 256:272, :] = jnp.zeros((16, 128), BF16)


def window(s, group, q, w, spec):
    start = 32 * w - HALO
    before = lax.rem(q + (1 if start >= 0 else 0), 5)
    after = lax.rem(before + 1, 5)
    lane = lax.broadcasted_iota(jnp.int32, (272, 128), 1)
    parts = []
    for part in range(2):
        parts.append(jnp.where(lane < start % 128, spec[s, group, after, part], spec[s, group, before, part]))
    return jnp.concatenate(parts, axis=1)


def cross(x0, x1):
    ar, ai, br, bi = x0[:, :128], x0[:, 128:], x1[:, :128], x1[:, 128:]
    return jnp.concatenate([(ar * br + ai * bi).astype(BF16), (ar * bi - ai * br).astype(BF16)], axis=1)


def unit_of(n):
    m = lax.rem(n, 4)
    return n // 8, lax.rem(n // 4, 2), lax.rem(m + 1, 3) + 2 * (m // 3)


def cross_unit(pair, n, spec, kept, crossed, tables):
    _, group, q = unit_of(n)
    for w in range(4):
        x1 = mm(window(pair + 1, group, q, w, spec), tables["second"].read())
        if pair == 0:
            x0 = mm(window(0, group, q, w, spec), tables["second"].read())
            kept[group, q, w] = x1.astype(BF16)
        else:
            x0 = kept[group, q, w].astype(F32)
        crossed[:, 256 * w : 256 * w + 256] = cross(x0, x1)


def columns_back(crossed, turned, last_row, tables):
    back = mm(crossed[...], tables["back_second"].read())
    turned[0:256, :] = back[0:256, :128].astype(BF16)
    turned[256:512, :] = back[0:256, 128:].astype(BF16)
    last = back[256:264, 0:128]
    low = lax.broadcasted_iota(jnp.int32, (8, 128), 0) < 4
    last_row[...] = jnp.where(low, last, -pltpu.roll(last, 4, 0))


def rows_back(n, turned, last_row, en, unit_sums, tables):
    pair, group, q = unit_of(n)
    corr = mm(tables["back_first"].read_part(group, 128), turned[...])
    low = lax.broadcasted_iota(jnp.int32, (8, 128), 0) < 4
    scale = (PATCH / 2.0 / PATCH**4) * lax.rsqrt(en[pair, group, q] * en[pair + 1, group, q])
    last = last_row[...]
    total = jnp.zeros((8, 128), F32)
    along = jnp.zeros((8, 128), F32)
    for u in range(0, SHIFTS, 2):
        weight = jnp.exp((corr[4 * u : 4 * u + 8] + last) * scale)
        total += weight
        along += weight * jnp.where(low, float(u - SHIFTS // 2), float(u + 1 - SHIFTS // 2))
    unit_sums[n, :, 0:128] = total + pltpu.roll(total, 4, 0)
    unit_sums[n, :, 128:256] = along + pltpu.roll(along, 4, 0)


def flow_block(unit_sums, sums, last_sec):
    row = lax.broadcasted_iota(jnp.int32, (8, 256), 0)
    pieces = []
    for pair in range(2):
        for q in range(4):
            m = (2, 0, 1, 3)[q]
            inner, outer = unit_sums[8 * pair + m], unit_sums[8 * pair + 4 + m]
            pieces.append(jnp.where((row >= 2) & (row < 6), pltpu.roll(inner, 2, 0), outer))
    y = mm_exact(jnp.concatenate(pieces, axis=0), sums.read())
    flow = y[:, 128:] / y[:, :128]
    lane = lax.broadcasted_iota(jnp.int32, (8, 128), 1)
    block = jnp.zeros((8, 128), F32)
    for pair in range(2):
        for q in range(4):
            first = 8 + 4 * q
            mine = (lane // 64 == pair) & (lane % 32 >= first) & (lane % 32 < first + 4)
            r = 32 * pair + 8 * q
            block = jnp.where(mine, flow[r : r + 8], block)
    return jnp.where((lane >= 64) & last_sec, 0.0, block)


def extend(own, left, right):
    lane = lax.broadcasted_iota(jnp.int32, own.shape, own.ndim - 1) % 32
    from_left = pltpu.roll(left, 112, own.ndim - 1)
    from_right = pltpu.roll(right, 16, own.ndim - 1)
    return jnp.where(lane < 8, from_left, jnp.where(lane >= 24, from_right, own))


def relax(flow, row_pos, col_pos):
    shape = flow[0].shape
    row = lax.broadcasted_iota(jnp.int32, shape, 0)
    lane = lax.broadcasted_iota(jnp.int32, shape, 1)
    node = lane % 32
    inside = ((row >= 8) | (row_pos > 0)) & ((row < 16) | (row_pos < TILE_GRID - 1))
    inside &= ((node >= 8) | (col_pos > 0)) & ((node < 24) | (col_pos < TILE_GRID - 1))
    mask = jnp.where(inside, 1.0, 0.0)
    low = lane < 64
    count = len(flow)
    zero = jnp.zeros(shape, F32)

    def following(f):
        turned = [pltpu.roll(x, 64, 1) for x in f] + [zero]
        return [jnp.where(low, turned[d], turned[d + 1]) for d in range(count)]

    def preceding(f):
        turned = [zero] + [pltpu.roll(x, 64, 1) for x in f]
        return [jnp.where(low, turned[d], turned[d + 1]) for d in range(count)]

    flow = [f * mask for f in flow]
    mesh = [zero] * count
    for step in range(ITERS):
        if step == 0:
            spring = [-f for f in flow]
        else:
            spring = [m - n - f for m, n, f in zip(mesh, following(mesh), flow)]
        earlier = preceding(spring)
        updated = []
        for m, sp, ea in zip(mesh, spring, earlier):
            change = sp - ea
            if step > 0:
                around = pltpu.roll(m, 1, 0) + pltpu.roll(m, 23, 0) + pltpu.roll(m, 1, 1) + pltpu.roll(m, 127, 1)
                change = change + 4.0 * m - around
            updated.append((m - STEP_RATE * change) * mask)
        mesh = updated
    return mesh


SHIFT_ROWS = 288


def shifted_columns(pad, cols):
    @pl.loop(0, SHIFT_ROWS // 16)
    def _(k):
        for s in range(2):
            x = pad[s, pl.ds(pl.multiple_of(32 + 16 * k, 16), 16), :].astype(F32)
            for d in range(5):
                y = x if d == 2 else pltpu.roll(x, (2 - d) % LANES, 1)
                for t in range(4):
                    cols[d, pl.ds(128 * k + (4 * s + t), 16, stride=8), :] = y[:, 128 * t : 128 * t + 128]


def pick_pair(high, odd, values):
    near = [jnp.where(high, values[k + 2], values[k]) for k in range(3)]
    return jnp.where(odd, near[1], near[0]), jnp.where(odd, near[2], near[1])


def corners(r, offsets, by_row, cols, coef):
    base = pl.multiple_of(8 * r, 8)
    for c in range(2):
        for st in range(8):
            by_row[c, pl.ds(st, 8, stride=8), :] = offsets[c, pl.ds(pl.multiple_of(256 * st + base, 8), 8), :]
    view = [
        [cols[d, pl.ds(pl.multiple_of(8 * base + 8 * (14 + k), 8), 8), :] for d in range(5)] for k in range(12)
    ]
    for k in range(8):
        ro = by_row[0, 8 * k : 8 * k + 8, :]
        co = by_row[1, 8 * k : 8 * k + 8, :]
        row_high, row_odd = ro >= 0, (ro & 1) == 1
        col_high, col_odd = co >= 0, (co & 1) == 1
        pairs = [pick_pair(col_high, col_odd, view[k + dr]) for dr in range(5)]
        i00, i10 = pick_pair(row_high, row_odd, [p[0] for p in pairs])
        i01, i11 = pick_pair(row_high, row_odd, [p[1] for p in pairs])
        rf, cf = ro.astype(F32), co.astype(F32)
        top, low = i01 - i00, i11 - i10
        top0, low0 = i00 - cf * top, i10 - cf * low
        twist, lean = low - top, low0 - top0
        coef[0, base + k] = top0 - rf * lean
        coef[1, base + k] = lean
        coef[2, base + k] = top - rf * twist
        coef[3, base + k] = twist


def write_mesh(mesh, out):
    for s in range(2):
        for c in range(2):
            lane = 64 * s + 32 * c + 8
            out[s, c, 0] = mesh[:, lane : lane + 16]


def spread_lanes(mesh, i, c):
    tile = lax.broadcasted_iota(jnp.int32, (8, 128), 0)
    lane = lax.broadcasted_iota(jnp.int32, (8, 128), 1)
    place = 64 * (tile // 4) + 4 * (tile % 4) + lane // 32 + (32 * c + 8)
    return jnp.take_along_axis(jnp.broadcast_to(mesh[i : i + 1], (8, 128)), place, axis=1)


MESH = pl.DeviceIdType.MESH
AROUND = [(0, -1), (0, 1), (-1, 0), (1, 0), (-1, -1), (-1, 1), (1, -1), (1, 1)]


def pixel_part(dr, dc, sections, pad, from_left, from_right, src, dst):
    src_rows = {-1: pl.ds(0, HALO), 0: pl.ds(0, 256), 1: pl.ds(256 - HALO, HALO)}[dr]
    dst_rows = {-1: pl.ds(HALO + 256, HALO), 0: pl.ds(HALO, 256), 1: pl.ds(0, HALO)}[dr]
    if dc == 0:
        return sections.at[src, 0, src_rows, :], pad.at[dst, dst_rows, pl.ds(0, OWN_LANES)]
    if dc < 0:
        return sections.at[src, 0, src_rows, pl.ds(0, 128)], from_right.at[dst, dst_rows, :]
    return sections.at[src, 0, src_rows, pl.ds(OWN_LANES - 128, 128)], from_left.at[dst, dst_rows, :]


def merge_sides(s, rows, pad, from_left, from_right, col_pos):
    lane = lax.broadcasted_iota(jnp.int32, (rows.stop - rows.start, 128), 1)
    side = jnp.where(lane < 64, from_right[s, rows, :].astype(F32), from_left[s, rows, :].astype(F32))
    keep = ((lane < 64) & (col_pos < TILE_GRID - 1)) | ((lane >= 64) & (col_pos > 0))
    pad[s, rows, OWN_LANES:LANES] = jnp.where(keep, side, 0.0).astype(BF16)


def clear_edges(first, count, pad, row_pos):
    @pl.when(row_pos == 0)
    def _():
        pad[first : first + count, 0:HALO, :] = jnp.zeros((count, HALO, LANES), BF16)

    @pl.when(row_pos == TILE_GRID - 1)
    def _():
        pad[first : first + count, ROWS - HALO : ROWS, :] = jnp.zeros((count, HALO, LANES), BF16)


def pixel_forward(dr, dc, pad, from_left, from_right):
    src_rows = {-1: pl.ds(HALO, HALO), 0: pl.ds(HALO, 256), 1: pl.ds(256, HALO)}[dr]
    dst_rows = {-1: pl.ds(HALO + 256, HALO), 0: pl.ds(HALO, 256), 1: pl.ds(0, HALO)}[dr]
    if dc == 0:
        return pad.at[2, src_rows, pl.ds(0, OWN_LANES)], pad.at[2, dst_rows, pl.ds(0, OWN_LANES)]
    if dc < 0:
        return pad.at[2, src_rows, pl.ds(0, 128)], from_right.at[2, dst_rows, :]
    return pad.at[2, src_rows, pl.ds(OWN_LANES - 128, 128)], from_left.at[2, dst_rows, :]


def flow_kernel(sections, offsets_in, packed_in, coef, block_out,
                pad, from_left, from_right, offsets, by_row, packed, spec, kept, crossed, turned, last_row, eb, en, unit_sums, flows, cols,
                local_sem, pixel_send, pixel_recv, flow_send, flow_recv):
    tables = {name: Table(packed, name) for name in PLACES}
    sec, tile = lax.axis_index("sec"), lax.axis_index("tile")
    sec_count = lax.axis_size("sec")
    row_pos, col_pos = tile // TILE_GRID, tile % TILE_GRID

    def device(ds, dr, dc):
        row = lax.rem(row_pos + (dr + TILE_GRID), TILE_GRID)
        col = lax.rem(col_pos + (dc + TILE_GRID), TILE_GRID)
        return (lax.rem(sec + ds, sec_count), row * TILE_GRID + col)

    barrier = pltpu.get_barrier_semaphore()
    partners = [(ds, dr, dc) for ds in range(4) for dr, dc in AROUND + [(0, 0)] if (ds, dr, dc) != (0, 0, 0)]
    for p in partners:
        pl.semaphore_signal(barrier, inc=1, device_id=device(*p), device_id_type=MESH)
    own_copy = pltpu.make_async_copy(
        sections.at[:, 0], pad.at[pl.ds(0, 2), pl.ds(HALO, 256), pl.ds(0, OWN_LANES)], local_sem.at[0]
    )
    offset_copies = [
        pltpu.make_async_copy(
            offsets_in.at[c, s, 0, :, pl.ds(128 * t, 128)],
            offsets.at[c, pl.ds((4 * s + t) * 256, 256), :],
            local_sem.at[2 + 8 * c + 4 * s + t],
        )
        for c in range(2) for s in range(2) for t in range(4)
    ]
    table_copy = pltpu.make_async_copy(packed_in, packed, local_sem.at[1])
    own_copy.start()
    table_copy.start()
    for copy in offset_copies:
        copy.start()
    pl.semaphore_wait(barrier, len(partners))

    def pixel_copy(k, ds, dr, dc, refs):
        return pltpu.make_async_remote_copy(
            src_ref=refs[0], dst_ref=refs[1], send_sem=pixel_send.at[k], recv_sem=pixel_recv.at[k],
            device_id=device(ds, dr, dc), device_id_type=MESH,
        )

    both = pl.ds(0, 2)
    own = [
        pixel_copy(k, 0, dr, dc, pixel_part(dr, dc, sections, pad, from_left, from_right, both, both))
        for k, (dr, dc) in enumerate(AROUND)
    ]
    after = pixel_copy(
        8, 3, 0, 0, pixel_part(0, 0, sections, pad, from_left, from_right, pl.ds(0, 1), pl.ds(2, 1))
    )
    for copy in own + [after]:
        copy.start()

    def transform(s, group, columns):
        first_transform(s, group, columns, pad, spec, tables)

    def energies(s, blocks, lanes, columns):
        block_energies(s, blocks, lanes, pad, eb)
        node_energies(s, columns, eb, en, tables["energy_cols"])

    def units(pair, first, count):
        @pl.loop(0, count)
        def _(k):
            n = first + k
            rows_back(n - 2, turned, last_row, en, unit_sums, tables)
            columns_back(crossed, turned, last_row, tables)
            cross_unit(pair, n, spec, kept, crossed, tables)

    inner_blocks, outer_blocks = range(2, 9), (0, 1, 9, 10)
    own_lanes, side_lanes, all_lanes = slice(0, OWN_LANES), slice(OWN_LANES, LANES), slice(0, LANES)

    def inner_own(s):
        transform(s, INNER, OWN_COLS)
        energies(s, inner_blocks, own_lanes, (1, 2))

    def inner_sides(s):
        merge_sides(s, slice(HALO, HALO + 256), pad, from_left, from_right, col_pos)
        transform(s, INNER, SIDE_COLS)
        energies(s, inner_blocks, side_lanes, (0, 3))

    def outer(s):
        merge_sides(s, slice(0, HALO), pad, from_left, from_right, col_pos)
        merge_sides(s, slice(HALO + 256, ROWS), pad, from_left, from_right, col_pos)
        clear_edges(s, 1, pad, row_pos)
        transform(s, OUTER, OWN_COLS + SIDE_COLS)
        energies(s, outer_blocks, all_lanes, (0, 1, 2, 3))

    eb[...] = jnp.zeros(eb.shape, F32)
    own_copy.wait()
    table_copy.wait()
    inner_own(0)
    inner_own(1)
    cross_unit(0, 0, spec, kept, crossed, tables)
    columns_back(crossed, turned, last_row, tables)
    cross_unit(0, 1, spec, kept, crossed, tables)
    own[0].wait_recv()
    own[1].wait_recv()
    inner_sides(0)
    inner_sides(1)
    units(0, 2, 2)
    for copy in own[2:]:
        copy.wait_recv()
    outer(0)
    outer(1)
    units(0, 4, 2)
    after.wait_recv()
    forward = [
        pixel_copy(9 + k, 0, dr, dc, pixel_forward(dr, dc, pad, from_left, from_right))
        for k, (dr, dc) in enumerate(AROUND)
    ]
    for copy in forward:
        copy.start()
    units(0, 6, 2)
    inner_own(2)
    units(1, 8, 2)
    forward[0].wait_recv()
    forward[1].wait_recv()
    inner_sides(2)
    units(1, 10, 2)
    for copy in forward[2:]:
        copy.wait_recv()
    outer(2)
    units(1, 12, 4)
    rows_back(14, turned, last_row, en, unit_sums, tables)
    columns_back(crossed, turned, last_row, tables)
    rows_back(15, turned, last_row, en, unit_sums, tables)

    flows[4, sec] = flow_block(unit_sums, tables["sums"], sec == sec_count - 1)
    spread = [(ds, dr, dc) for ds in range(4) for dr, dc in AROUND + [(0, 0)] if (ds, dr, dc) != (0, 0, 0)]
    share = [
        pltpu.make_async_remote_copy(
            src_ref=flows.at[4, sec], dst_ref=flows.at[3 * (1 - dr) + 1 - dc, sec], send_sem=flow_send.at[k],
            recv_sem=flow_recv.at[k], device_id=device(ds, dr, dc), device_id_type=MESH,
        )
        for k, (ds, dr, dc) in enumerate(spread)
    ]
    for copy in share:
        copy.start()
    shifted_columns(pad, cols)
    for copy in offset_copies:
        copy.wait()

    @pl.loop(0, 32)
    def _(r):
        corners(r, offsets, by_row, cols, coef)

    for copy in share:
        copy.wait_recv()

    def column(d, c):
        return jnp.concatenate([flows[c, d], flows[3 + c, d], flows[6 + c, d]], axis=0)

    mesh = relax([extend(column(d, 1), column(d, 0), column(d, 2)) for d in range(4)], row_pos, col_pos)
    mine = mesh[0][8:16]
    for d in range(1, 4):
        mine = jnp.where(sec == d, mesh[d][8:16], mine)
    block_out[...] = mine
    for copy in own + [after] + forward + share:
        copy.wait_send()


def blend_kernel(coef, block, mesh_out, warped, by_row, result, sem):
    mesh = block[...]
    write_mesh(mesh, mesh_out)
    copies = []
    for i in range(8):
        a, b = spread_lanes(mesh, i, 0), spread_lanes(mesh, i, 1)
        for k in range(32):
            r = 32 * i + k
            first = coef[0, r] + a * coef[1, r]
            second = coef[2, r] + a * coef[3, r]
            by_row[i % 2, 8 * k : 8 * k + 8, :] = first + b * second
        for k in range(4):
            for st in range(8):
                rows = slice(256 * st + 32 * i + 8 * k, 256 * st + 32 * i + 8 * k + 8)
                result[rows, :] = by_row[i % 2, pl.ds(64 * k + st, 8, stride=8), :]
        if i % 2 == 1:
            rows = pl.ds(32 * i - 32, 64)
            for s in range(2):
                for t in range(4):
                    copy = pltpu.make_async_copy(
                        result.at[pl.ds(256 * (4 * s + t) + 32 * i - 32, 64), :],
                        warped.at[s, 0, rows, pl.ds(128 * t, 128)],
                        sem.at[len(copies)],
                    )
                    copy.start()
                    copies.append(copy)
    for copy in copies:
        copy.wait()


def vmem():
    return pl.BlockSpec(memory_space=pltpu.VMEM)


def shards(sections, corner_offsets):
    anywhere = pl.BlockSpec(memory_space=pl.ANY)
    dma = pltpu.SemaphoreType.DMA
    coef, block = pl.pallas_call(
        flow_kernel,
        out_shape=(pltpu.VMEM((4, 256, 8, 128), F32), pltpu.VMEM((8, 128), F32)),
        in_specs=[anywhere, anywhere, anywhere],
        out_specs=(vmem(), vmem()),
        scratch_shapes=[
            pltpu.VMEM((3, ROWS, LANES), BF16),
            pltpu.VMEM((3, ROWS, 128), BF16),
            pltpu.VMEM((3, ROWS, 128), BF16),
            pltpu.VMEM((2, 8 * 256, 128), jnp.int32),
            pltpu.VMEM((2, 64, 128), jnp.int32),
            pltpu.VMEM(PACKED.shape, BF16),
            pltpu.VMEM((3, 2, 5, 2, 272, 128), BF16),
            pltpu.VMEM((2, 4, 4, 272, 256), BF16),
            pltpu.VMEM((272, 1024), BF16),
            pltpu.VMEM((512, 128), BF16),
            pltpu.VMEM((8, 128), F32),
            pltpu.VMEM((3, 16, LANES), F32),
            pltpu.VMEM((3, 2, 4, 8, 128), F32),
            pltpu.VMEM((16, 8, 256), F32),
            pltpu.VMEM((9, 4, 8, 128), F32),
            pltpu.VMEM((5, 8 * SHIFT_ROWS, 128), F32),
            dma((18,)),
            dma((17,)),
            dma((17,)),
            dma((35,)),
            dma((35,)),
        ],
        compiler_params=pltpu.CompilerParams(
            vmem_limit_bytes=58 * 2**20, collective_id=0, has_side_effects=True
        ),
    )(sections, corner_offsets, jnp.asarray(PACKED))
    return pl.pallas_call(
        blend_kernel,
        out_shape=(
            jax.ShapeDtypeStruct((2, 2, 1, 8, 16), F32),
            jax.ShapeDtypeStruct((2, 1, 256, 512), F32),
        ),
        in_specs=[vmem(), vmem()],
        out_specs=(vmem(), anywhere),
        scratch_shapes=[pltpu.VMEM((2, 256, 128), F32), pltpu.VMEM((8 * 256, 128), F32), dma((32,))],
        compiler_params=pltpu.CompilerParams(vmem_limit_bytes=20 * 2**20),
    )(coef, block)


def solution(mesh):
    in_specs = (P("sec", "tile", None, None), P(None, "sec", "tile", None, None))
    out_specs = (P("sec", None, "tile", None, None), P("sec", "tile", None, None))
    return jax.shard_map(shards, mesh=mesh, in_specs=in_specs, out_specs=out_specs, check_vma=False)
```

```python
import math

import jax
import jax.numpy as jnp
import ml_dtypes
import numpy as np
from jax import lax
from jax.experimental import pallas as pl
from jax.experimental.pallas import tpu as pltpu
from jax.sharding import PartitionSpec as P

TILE_GRID = 8
PATCH = 128
STRIDE = 32
SHIFTS = 32
ITERS = 4
HALO = 48
EPS = 1e-05
STEP_RATE = 0.15
ROWS = 352
LANES = 640
OWN_LANES = 512
F32 = jnp.float32
BF16 = jnp.bfloat16


def build_tables():
    k = np.arange(PATCH)
    u = np.arange(SHIFTS) - SHIFTS // 2

    def cos_of(m):
        return np.cos(2 * np.pi * (m % PATCH) / PATCH)

    def sin_of(m):
        return np.sin(2 * np.pi * (m % PATCH) / PATCH)

    c, s = cos_of(np.outer(k, k)), sin_of(np.outer(k, k))
    gc, gs = cos_of(np.outer(u, k)), sin_of(np.outer(u, k))
    factor = np.where(k[:64] == 0, 1.0, 2.0)
    first = []
    for count, shift, slot in ((4, 16, 0), (2, 0, 0), (2, 96, 2)):
        table = np.zeros((128 * count + 16, 256))
        for i in range(count):
            rows = slice(32 * i + shift, 32 * i + shift + 128)
            table[i : 64 * count : count, rows] = c[:64]
            table[64 * count + i : 128 * count : count, rows] = -s[:64]
            table[128 * count + slot + i, rows] = (-1.0) ** k
        first.append(table)
    second = np.block([[c, -s], [s, c]])
    back_second = np.zeros((1024, 256))
    for w in range(4):
        rows, lanes = 256 * w, 32 * w
        back_second[rows : rows + 128, lanes : lanes + 32] = gc.T
        back_second[rows + 128 : rows + 256, lanes : lanes + 32] = -gs.T
        back_second[rows : rows + 128, 128 + lanes : 160 + lanes] = gs.T
        back_second[rows + 128 : rows + 256, 128 + lanes : 160 + lanes] = gc.T
    inner, outer = np.zeros((128, 512)), np.zeros((128, 512))
    for i in range(4):
        inner[i::4, i:256:4] = factor * gc[:, :64]
        inner[i::4, 256 + i : 512 : 4] = -factor * gs[:, :64]
        start = 128 * (i // 2) + i % 2
        outer[i::4, start : 128 * (i // 2) + 128 : 2] = factor * gc[:, :64]
        outer[i::4, 256 + start : 384 + 128 * (i // 2) : 2] = -factor * gs[:, :64]
    energy_cols = np.zeros((384, 128))
    for jj in range(4):
        energy_cols[128 + 32 * jj - HALO : 256 + 32 * jj - HALO, 32 * jj : 32 * jj + 32] = 1.0
    sums = np.zeros((256, 256))
    for lane in range(128):
        jj, comp = lane % 4, (lane // 32) % 2
        sums[32 * jj : 32 * jj + 32, lane] = 1.0
        if comp == 0:
            sums[128 + 32 * jj : 160 + 32 * jj, 128 + lane] = 1.0
        else:
            sums[32 * jj : 32 * jj + 32, 128 + lane] = u
    tables = {
        "inner": first[0], "upper": first[1], "lower": first[2], "second": second, "back_second": back_second,
        "back_first": np.concatenate([inner, outer], axis=0), "energy_cols": energy_cols, "sums": sums,
    }
    places, pieces, base = {}, [], 0
    for name, table in tables.items():
        rows, tiles = table.shape[0], table.shape[1] // 128
        places[name] = (base, rows, tiles)
        pieces += [table[:, 128 * t : 128 * t + 128] for t in range(tiles)]
        base += rows * tiles
    packed = np.concatenate(pieces, axis=0).astype(np.float32).astype(ml_dtypes.bfloat16)
    return places, packed


PLACES, PACKED = build_tables()


class Table:
    def __init__(self, ref, name):
        self.ref = ref
        self.base, self.rows, self.tiles = PLACES[name]

    def read(self, rows=None, tiles=None):
        rows = rows or slice(0, self.rows)
        tiles = range(self.tiles) if tiles is None else tiles
        starts = [self.base + t * self.rows for t in tiles]
        parts = [self.ref[b + rows.start : b + rows.stop, :] for b in starts]
        return parts[0] if len(parts) == 1 else jnp.concatenate(parts, axis=1)

    def read_part(self, part, rows):
        starts = [self.base + t * self.rows for t in range(self.tiles)]
        parts = [self.ref[pl.ds(pl.multiple_of(b + part * rows, 16), rows), :] for b in starts]
        return jnp.concatenate(parts, axis=1)


def mm(a, b):
    return jnp.dot(a, b, preferred_element_type=F32)


def split3(x):
    hi = x.astype(BF16)
    rest = x - hi.astype(F32)
    mid = rest.astype(BF16)
    low = (rest - mid.astype(F32)).astype(BF16)
    return jnp.concatenate([hi, mid, low], axis=0)


def mm_exact(x, w):
    n = x.shape[0]
    y = mm(split3(x), w)
    return y[:n] + y[n : 2 * n] + y[2 * n :]


def block_energies(s, blocks, lanes, pad, eb):
    for b in blocks:
        x = pad[s, 32 * b : 32 * b + 32, lanes].astype(F32)
        eb[s, b : b + 1, lanes] = jnp.sum(x * x, axis=0, keepdims=True)


def node_energies(s, columns, eb, en, energy_cols):
    e4 = eb[s, 0:8, :] + eb[s, 1:9, :] + eb[s, 2:10, :] + eb[s, 3:11, :]
    tiles = [e4[:, 128 * t : 128 * t + 128] for t in range(5)]
    rows = [jnp.concatenate([tiles[(q - 1) % 5], tiles[q], tiles[q + 1]], axis=1) for q in columns]
    y = mm_exact(jnp.concatenate(rows, axis=0), energy_cols.read())
    row = lax.broadcasted_iota(jnp.int32, (8, 128), 0)
    for n, q in enumerate(columns):
        e = y[8 * n : 8 * n + 8] * (1.0 / PATCH**2) + EPS
        en[s, INNER, q] = jnp.where(row < 4, pltpu.roll(e, 6, 0), pltpu.roll(e, 2, 0))
        en[s, OUTER, q] = jnp.where((row < 2) | (row >= 6), e, pltpu.roll(e, 4, 0))


INNER, OUTER = 0, 1
OWN_COLS, SIDE_COLS = (slice(0, 256), slice(256, 512)), (slice(512, 640),)


def first_transform(s, group, columns, pad, spec, tables):
    for lanes in columns:
        if group == INNER:
            parts = [(0, 256, mm(tables["inner"].read(), pad[s, HALO : HALO + 256, lanes]))]
        else:
            parts = [
                (0, 128, mm(tables["upper"].read(), pad[s, 0:256, lanes])),
                (128, 128, mm(tables["lower"].read(), pad[s, 96:352, lanes])),
            ]
        for n in range((lanes.stop - lanes.start) // 128):
            t = (lanes.start // 128 + n + 1) % 5
            cols = slice(128 * n, 128 * n + 128)
            last = None
            for row, count, y in parts:
                spec[s, group, t, 0, row : row + count, :] = y[0:count, cols].astype(BF16)
                spec[s, group, t, 1, row : row + count, :] = y[count : 2 * count, cols].astype(BF16)
                end = y[2 * count : 2 * count + 16, cols]
                last = end if last is None else last + end
            spec[s, group, t, 0, 256:272, :] = last.astype(BF16)
            spec[s, group, t, 1, 256:272, :] = jnp.zeros((16, 128), BF16)


def window(s, group, q, w, spec):
    start = 32 * w - HALO
    before = lax.rem(q + (1 if start >= 0 else 0), 5)
    after = lax.rem(before + 1, 5)
    lane = lax.broadcasted_iota(jnp.int32, (272, 128), 1)
    parts = []
    for part in range(2):
        parts.append(jnp.where(lane < start % 128, spec[s, group, after, part], spec[s, group, before, part]))
    return jnp.concatenate(parts, axis=1)


def cross(x0, x1):
    ar, ai, br, bi = x0[:, :128], x0[:, 128:], x1[:, :128], x1[:, 128:]
    return jnp.concatenate([(ar * br + ai * bi).astype(BF16), (ar * bi - ai * br).astype(BF16)], axis=1)


def unit_of(n):
    m = lax.rem(n, 4)
    return n // 8, lax.rem(n // 4, 2), lax.rem(m + 1, 3) + 2 * (m // 3)


def cross_unit(pair, n, spec, kept, crossed, tables):
    _, group, q = unit_of(n)
    for w in range(4):
        x1 = mm(window(pair + 1, group, q, w, spec), tables["second"].read())
        if pair == 0:
            x0 = mm(window(0, group, q, w, spec), tables["second"].read())
            kept[group, q, w] = x1.astype(BF16)
        else:
            x0 = kept[group, q, w].astype(F32)
        crossed[:, 256 * w : 256 * w + 256] = cross(x0, x1)


def columns_back(crossed, turned, last_row, tables):
    back = mm(crossed[...], tables["back_second"].read())
    turned[0:256, :] = back[0:256, :128].astype(BF16)
    turned[256:512, :] = back[0:256, 128:].astype(BF16)
    last = back[256:264, 0:128]
    low = lax.broadcasted_iota(jnp.int32, (8, 128), 0) < 4
    last_row[...] = jnp.where(low, last, -pltpu.roll(last, 4, 0))


def rows_back(n, turned, last_row, en, unit_sums, tables):
    pair, group, q = unit_of(n)
    corr = mm(tables["back_first"].read_part(group, 128), turned[...])
    low = lax.broadcasted_iota(jnp.int32, (8, 128), 0) < 4
    scale = (PATCH / 2.0 / PATCH**4) * lax.rsqrt(en[pair, group, q] * en[pair + 1, group, q])
    last = last_row[...]
    total = jnp.zeros((8, 128), F32)
    along = jnp.zeros((8, 128), F32)
    for u in range(0, SHIFTS, 2):
        weight = jnp.exp((corr[4 * u : 4 * u + 8] + last) * scale)
        total += weight
        along += weight * jnp.where(low, float(u - SHIFTS // 2), float(u + 1 - SHIFTS // 2))
    unit_sums[n, :, 0:128] = total + pltpu.roll(total, 4, 0)
    unit_sums[n, :, 128:256] = along + pltpu.roll(along, 4, 0)


def flow_block(unit_sums, sums, last_sec):
    row = lax.broadcasted_iota(jnp.int32, (8, 256), 0)
    pieces = []
    for pair in range(2):
        for q in range(4):
            m = (2, 0, 1, 3)[q]
            inner, outer = unit_sums[8 * pair + m], unit_sums[8 * pair + 4 + m]
            pieces.append(jnp.where((row >= 2) & (row < 6), pltpu.roll(inner, 2, 0), outer))
    y = mm_exact(jnp.concatenate(pieces, axis=0), sums.read())
    flow = y[:, 128:] / y[:, :128]
    lane = lax.broadcasted_iota(jnp.int32, (8, 128), 1)
    block = jnp.zeros((8, 128), F32)
    for pair in range(2):
        for q in range(4):
            first = 8 + 4 * q
            mine = (lane // 64 == pair) & (lane % 32 >= first) & (lane % 32 < first + 4)
            r = 32 * pair + 8 * q
            block = jnp.where(mine, flow[r : r + 8], block)
    return jnp.where((lane >= 64) & last_sec, 0.0, block)


def extend(own, left, right):
    lane = lax.broadcasted_iota(jnp.int32, own.shape, own.ndim - 1) % 32
    from_left = pltpu.roll(left, 112, own.ndim - 1)
    from_right = pltpu.roll(right, 16, own.ndim - 1)
    return jnp.where(lane < 8, from_left, jnp.where(lane >= 24, from_right, own))


def relax(flow, row_pos, col_pos):
    shape = flow[0].shape
    row = lax.broadcasted_iota(jnp.int32, shape, 0)
    lane = lax.broadcasted_iota(jnp.int32, shape, 1)
    node = lane % 32
    inside = ((row >= 8) | (row_pos > 0)) & ((row < 16) | (row_pos < TILE_GRID - 1))
    inside &= ((node >= 8) | (col_pos > 0)) & ((node < 24) | (col_pos < TILE_GRID - 1))
    mask = jnp.where(inside, 1.0, 0.0)
    low = lane < 64
    count = len(flow)
    zero = jnp.zeros(shape, F32)

    def following(f):
        turned = [pltpu.roll(x, 64, 1) for x in f] + [zero]
        return [jnp.where(low, turned[d], turned[d + 1]) for d in range(count)]

    def preceding(f):
        turned = [zero] + [pltpu.roll(x, 64, 1) for x in f]
        return [jnp.where(low, turned[d], turned[d + 1]) for d in range(count)]

    flow = [f * mask for f in flow]
    mesh = [zero] * count
    for step in range(ITERS):
        if step == 0:
            spring = [-f for f in flow]
        else:
            spring = [m - n - f for m, n, f in zip(mesh, following(mesh), flow)]
        earlier = preceding(spring)
        updated = []
        for m, sp, ea in zip(mesh, spring, earlier):
            change = sp - ea
            if step > 0:
                around = pltpu.roll(m, 1, 0) + pltpu.roll(m, 23, 0) + pltpu.roll(m, 1, 1) + pltpu.roll(m, 127, 1)
                change = change + 4.0 * m - around
            updated.append((m - STEP_RATE * change) * mask)
        mesh = updated
    return mesh


SHIFT_ROWS = 288


def shifted_columns(pad, cols):
    @pl.loop(0, SHIFT_ROWS // 16)
    def _(k):
        for s in range(2):
            x = pad[s, pl.ds(pl.multiple_of(32 + 16 * k, 16), 16), :].astype(F32)
            for d in range(5):
                y = x if d == 2 else pltpu.roll(x, (2 - d) % LANES, 1)
                for t in range(4):
                    cols[d, pl.ds(128 * k + (4 * s + t), 16, stride=8), :] = y[:, 128 * t : 128 * t + 128]


def pick_pair(high, odd, values):
    near = [jnp.where(high, values[k + 2], values[k]) for k in range(3)]
    return jnp.where(odd, near[1], near[0]), jnp.where(odd, near[2], near[1])


def corners(r, offsets, cols, coef):
    base = pl.multiple_of(8 * r, 8)
    view = []
    for k in range(12):
        rows = pl.ds(pl.multiple_of(8 * (base + 14 + k), 8), 8)
        view.append([cols[d, rows, :] for d in range(5)])
    for k in range(8):
        ro, co = offsets[0, base + k], offsets[1, base + k]
        row_high, row_odd = ro >= 0, (ro & 1) == 1
        col_high, col_odd = co >= 0, (co & 1) == 1
        pairs = [pick_pair(col_high, col_odd, view[k + dr]) for dr in range(5)]
        i00, i10 = pick_pair(row_high, row_odd, [p[0] for p in pairs])
        i01, i11 = pick_pair(row_high, row_odd, [p[1] for p in pairs])
        rf, cf = ro.astype(F32), co.astype(F32)
        top, low = i01 - i00, i11 - i10
        top0, low0 = i00 - cf * top, i10 - cf * low
        twist, lean = low - top, low0 - top0
        coef[0, base + k] = top0 - rf * lean
        coef[1, base + k] = lean
        coef[2, base + k] = top - rf * twist
        coef[3, base + k] = twist


def write_mesh(mesh, out):
    for s in range(2):
        for c in range(2):
            lane = 64 * s + 32 * c + 8
            out[s, c, 0] = mesh[:, lane : lane + 16]


def spread_lanes(mesh, i, c):
    tile = lax.broadcasted_iota(jnp.int32, (8, 128), 0)
    lane = lax.broadcasted_iota(jnp.int32, (8, 128), 1)
    place = 64 * (tile // 4) + 4 * (tile % 4) + lane // 32 + (32 * c + 8)
    return jnp.take_along_axis(jnp.broadcast_to(mesh[i : i + 1], (8, 128)), place, axis=1)


MESH = pl.DeviceIdType.MESH
AROUND = [(0, -1), (0, 1), (-1, 0), (1, 0), (-1, -1), (-1, 1), (1, -1), (1, 1)]


def pixel_part(dr, dc, sections, pad, from_left, from_right, src, dst):
    src_rows = {-1: pl.ds(0, HALO), 0: pl.ds(0, 256), 1: pl.ds(256 - HALO, HALO)}[dr]
    dst_rows = {-1: pl.ds(HALO + 256, HALO), 0: pl.ds(HALO, 256), 1: pl.ds(0, HALO)}[dr]
    if dc == 0:
        return sections.at[src, 0, src_rows, :], pad.at[dst, dst_rows, pl.ds(0, OWN_LANES)]
    if dc < 0:
        return sections.at[src, 0, src_rows, pl.ds(0, 128)], from_right.at[dst, dst_rows, :]
    return sections.at[src, 0, src_rows, pl.ds(OWN_LANES - 128, 128)], from_left.at[dst, dst_rows, :]


def merge_sides(s, rows, pad, from_left, from_right, col_pos):
    lane = lax.broadcasted_iota(jnp.int32, (rows.stop - rows.start, 128), 1)
    side = jnp.where(lane < 64, from_right[s, rows, :].astype(F32), from_left[s, rows, :].astype(F32))
    keep = ((lane < 64) & (col_pos < TILE_GRID - 1)) | ((lane >= 64) & (col_pos > 0))
    pad[s, rows, OWN_LANES:LANES] = jnp.where(keep, side, 0.0).astype(BF16)


def clear_edges(s, pad, row_pos):
    @pl.when(row_pos == 0)
    def _():
        pad[s, 0:HALO, :] = jnp.zeros((HALO, LANES), BF16)

    @pl.when(row_pos == TILE_GRID - 1)
    def _():
        pad[s, ROWS - HALO : ROWS, :] = jnp.zeros((HALO, LANES), BF16)


def pixel_forward(dr, dc, pad, from_left, from_right):
    src_rows = {-1: pl.ds(HALO, HALO), 0: pl.ds(HALO, 256), 1: pl.ds(256, HALO)}[dr]
    dst_rows = {-1: pl.ds(HALO + 256, HALO), 0: pl.ds(HALO, 256), 1: pl.ds(0, HALO)}[dr]
    if dc == 0:
        return pad.at[2, src_rows, pl.ds(0, OWN_LANES)], pad.at[2, dst_rows, pl.ds(0, OWN_LANES)]
    if dc < 0:
        return pad.at[2, src_rows, pl.ds(0, 128)], from_right.at[2, dst_rows, :]
    return pad.at[2, src_rows, pl.ds(OWN_LANES - 128, 128)], from_left.at[2, dst_rows, :]


def flow_kernel(sections, offsets_in, packed_in, coef, block_out,
                pad, from_left, from_right, offsets, packed, spec, kept, crossed, turned, last_row, eb, en, unit_sums, flows, cols,
                local_sem, pixel_send, pixel_recv, flow_send, flow_recv):
    tables = {name: Table(packed, name) for name in PLACES}
    sec, tile = lax.axis_index("sec"), lax.axis_index("tile")
    sec_count = lax.axis_size("sec")
    row_pos, col_pos = tile // TILE_GRID, tile % TILE_GRID

    def device(ds, dr, dc):
        row = lax.rem(row_pos + (dr + TILE_GRID), TILE_GRID)
        col = lax.rem(col_pos + (dc + TILE_GRID), TILE_GRID)
        return (lax.rem(sec + ds, sec_count), row * TILE_GRID + col)

    barrier = pltpu.get_barrier_semaphore()
    partners = [(ds, dr, dc) for ds in range(4) for dr, dc in AROUND + [(0, 0)] if (ds, dr, dc) != (0, 0, 0)]
    for p in partners:
        pl.semaphore_signal(barrier, inc=1, device_id=device(*p), device_id_type=MESH)
    own_copy = pltpu.make_async_copy(
        sections.at[:, 0], pad.at[pl.ds(0, 2), pl.ds(HALO, 256), pl.ds(0, OWN_LANES)], local_sem.at[0]
    )
    offset_copies = [
        pltpu.make_async_copy(
            offsets_in.at[c, s, 0, :, pl.ds(128 * t, 128)],
            offsets.at[c, :, 4 * s + t, :],
            local_sem.at[2 + 8 * c + 4 * s + t],
        )
        for c in range(2) for s in range(2) for t in range(4)
    ]
    table_copy = pltpu.make_async_copy(packed_in, packed, local_sem.at[1])
    own_copy.start()
    table_copy.start()
    for copy in offset_copies:
        copy.start()
    pl.semaphore_wait(barrier, len(partners))

    def pixel_copy(k, ds, dr, dc, refs):
        return pltpu.make_async_remote_copy(
            src_ref=refs[0], dst_ref=refs[1], send_sem=pixel_send.at[k], recv_sem=pixel_recv.at[k],
            device_id=device(ds, dr, dc), device_id_type=MESH,
        )

    both = pl.ds(0, 2)
    own = [
        pixel_copy(k, 0, dr, dc, pixel_part(dr, dc, sections, pad, from_left, from_right, both, both))
        for k, (dr, dc) in enumerate(AROUND)
    ]
    after = pixel_copy(
        8, 3, 0, 0, pixel_part(0, 0, sections, pad, from_left, from_right, pl.ds(0, 1), pl.ds(2, 1))
    )
    for copy in own + [after]:
        copy.start()

    def transform(s, group, columns):
        first_transform(s, group, columns, pad, spec, tables)

    def energies(s, blocks, lanes, columns):
        block_energies(s, blocks, lanes, pad, eb)
        node_energies(s, columns, eb, en, tables["energy_cols"])

    def units(pair, first, count):
        @pl.loop(0, count)
        def _(k):
            n = first + k
            rows_back(n - 2, turned, last_row, en, unit_sums, tables)
            columns_back(crossed, turned, last_row, tables)
            cross_unit(pair, n, spec, kept, crossed, tables)

    inner_blocks, outer_blocks = range(2, 9), (0, 1, 9, 10)
    own_lanes, side_lanes, all_lanes = slice(0, OWN_LANES), slice(OWN_LANES, LANES), slice(0, LANES)

    def inner_own(s):
        transform(s, INNER, OWN_COLS)
        energies(s, inner_blocks, own_lanes, (1, 2))

    def inner_sides(s):
        merge_sides(s, slice(HALO, HALO + 256), pad, from_left, from_right, col_pos)
        transform(s, INNER, SIDE_COLS)
        energies(s, inner_blocks, side_lanes, (0, 3))

    def outer(s):
        merge_sides(s, slice(0, HALO), pad, from_left, from_right, col_pos)
        merge_sides(s, slice(HALO + 256, ROWS), pad, from_left, from_right, col_pos)
        clear_edges(s, pad, row_pos)
        transform(s, OUTER, OWN_COLS + SIDE_COLS)
        energies(s, outer_blocks, all_lanes, (0, 1, 2, 3))

    def corner_rows(first, count):
        @pl.loop(0, count)
        def _(k):
            corners(first + k, offsets, cols, coef)

    eb[...] = jnp.zeros(eb.shape, F32)
    own_copy.wait()
    table_copy.wait()
    pl.loop(0, 2)(inner_own)
    cross_unit(0, 0, spec, kept, crossed, tables)
    columns_back(crossed, turned, last_row, tables)
    cross_unit(0, 1, spec, kept, crossed, tables)
    own[0].wait_recv()
    own[1].wait_recv()
    pl.loop(0, 2)(inner_sides)
    units(0, 2, 2)
    for copy in own[2:]:
        copy.wait_recv()
    pl.loop(0, 2)(outer)
    units(0, 4, 2)
    after.wait_recv()
    forward = [
        pixel_copy(9 + k, 0, dr, dc, pixel_forward(dr, dc, pad, from_left, from_right))
        for k, (dr, dc) in enumerate(AROUND)
    ]
    for copy in forward:
        copy.start()
    units(0, 6, 2)
    inner_own(2)
    units(1, 8, 2)
    forward[0].wait_recv()
    forward[1].wait_recv()
    inner_sides(2)
    units(1, 10, 2)
    for copy in forward[2:]:
        copy.wait_recv()
    outer(2)
    units(1, 12, 4)
    rows_back(14, turned, last_row, en, unit_sums, tables)
    columns_back(crossed, turned, last_row, tables)
    rows_back(15, turned, last_row, en, unit_sums, tables)

    flows[4, sec] = flow_block(unit_sums, tables["sums"], sec == sec_count - 1)
    spread = [(ds, dr, dc) for ds in range(4) for dr, dc in AROUND + [(0, 0)] if (ds, dr, dc) != (0, 0, 0)]
    share = [
        pltpu.make_async_remote_copy(
            src_ref=flows.at[4, sec], dst_ref=flows.at[3 * (1 - dr) + 1 - dc, sec], send_sem=flow_send.at[k],
            recv_sem=flow_recv.at[k], device_id=device(ds, dr, dc), device_id_type=MESH,
        )
        for k, (ds, dr, dc) in enumerate(spread)
    ]
    for copy in share:
        copy.start()
    for copy in offset_copies:
        copy.wait()
    shifted_columns(pad, cols)
    corner_rows(0, 32)
    for copy in share:
        copy.wait_recv()

    def column(d, c):
        return jnp.concatenate([flows[c, d], flows[3 + c, d], flows[6 + c, d]], axis=0)

    mesh = relax([extend(column(d, 1), column(d, 0), column(d, 2)) for d in range(4)], row_pos, col_pos)
    mine = mesh[0][8:16]
    for d in range(1, 4):
        mine = jnp.where(sec == d, mesh[d][8:16], mine)
    block_out[...] = mine
    for copy in own + [after] + forward + share:
        copy.wait_send()


def blend_kernel(coef, block, mesh_out, warped, result, sem):
    mesh = block[...]
    write_mesh(mesh, mesh_out)
    copies = []
    for i in range(8):
        a, b = spread_lanes(mesh, i, 0), spread_lanes(mesh, i, 1)
        for k in range(32):
            r = 32 * i + k
            first = coef[0, r] + a * coef[1, r]
            second = coef[2, r] + a * coef[3, r]
            result[r] = first + b * second
        if i % 2 == 1:
            rows = pl.ds(32 * i - 32, 64)
            for s in range(2):
                for t in range(4):
                    copy = pltpu.make_async_copy(
                        result.at[rows, 4 * s + t, :], warped.at[s, 0, rows, pl.ds(128 * t, 128)], sem.at[len(copies)]
                    )
                    copy.start()
                    copies.append(copy)
    for copy in copies:
        copy.wait()


def vmem():
    return pl.BlockSpec(memory_space=pltpu.VMEM)


def shards(sections, corner_offsets):
    anywhere = pl.BlockSpec(memory_space=pl.ANY)
    dma = pltpu.SemaphoreType.DMA
    coef, block = pl.pallas_call(
        flow_kernel,
        out_shape=(pltpu.VMEM((4, 256, 8, 128), F32), pltpu.VMEM((8, 128), F32)),
        in_specs=[anywhere, anywhere, anywhere],
        out_specs=(vmem(), vmem()),
        scratch_shapes=[
            pltpu.VMEM((3, ROWS, LANES), BF16),
            pltpu.VMEM((3, ROWS, 128), BF16),
            pltpu.VMEM((3, ROWS, 128), BF16),
            pltpu.VMEM((2, 256, 8, 128), jnp.int32),
            pltpu.VMEM(PACKED.shape, BF16),
            pltpu.VMEM((3, 2, 5, 2, 272, 128), BF16),
            pltpu.VMEM((2, 4, 4, 272, 256), BF16),
            pltpu.VMEM((272, 1024), BF16),
            pltpu.VMEM((512, 128), BF16),
            pltpu.VMEM((8, 128), F32),
            pltpu.VMEM((3, 16, LANES), F32),
            pltpu.VMEM((3, 2, 4, 8, 128), F32),
            pltpu.VMEM((16, 8, 256), F32),
            pltpu.VMEM((9, 4, 8, 128), F32),
            pltpu.VMEM((5, 8 * SHIFT_ROWS, 128), F32),
            dma((18,)),
            dma((17,)),
            dma((17,)),
            dma((35,)),
            dma((35,)),
        ],
        compiler_params=pltpu.CompilerParams(
            vmem_limit_bytes=58 * 2**20, collective_id=0, has_side_effects=True
        ),
    )(sections, corner_offsets, jnp.asarray(PACKED))
    return pl.pallas_call(
        blend_kernel,
        out_shape=(
            jax.ShapeDtypeStruct((2, 2, 1, 8, 16), F32),
            jax.ShapeDtypeStruct((2, 1, 256, 512), F32),
        ),
        in_specs=[vmem(), vmem()],
        out_specs=(vmem(), anywhere),
        scratch_shapes=[pltpu.VMEM((256, 8, 128), F32), dma((32,))],
        compiler_params=pltpu.CompilerParams(vmem_limit_bytes=20 * 2**20),
    )(coef, block)


def solution(mesh):
    in_specs = (P("sec", "tile", None, None), P(None, "sec", "tile", None, None))
    out_specs = (P("sec", None, "tile", None, None), P("sec", "tile", None, None))
    return jax.shard_map(shards, mesh=mesh, in_specs=in_specs, out_specs=out_specs, check_vma=False)
```

```python
import math

import jax
import jax.numpy as jnp
import ml_dtypes
import numpy as np
from jax import lax
from jax.experimental import pallas as pl
from jax.experimental.pallas import tpu as pltpu
from jax.sharding import PartitionSpec as P

TILE_GRID = 8
PATCH = 128
STRIDE = 32
SHIFTS = 32
ITERS = 4
HALO = 48
EPS = 1e-05
STEP_RATE = 0.15
ROWS = 352
LANES = 640
OWN_LANES = 512
F32 = jnp.float32
BF16 = jnp.bfloat16


def build_tables():
    k = np.arange(PATCH)
    u = np.arange(SHIFTS) - SHIFTS // 2

    def cos_of(m):
        return np.cos(2 * np.pi * (m % PATCH) / PATCH)

    def sin_of(m):
        return np.sin(2 * np.pi * (m % PATCH) / PATCH)

    c, s = cos_of(np.outer(k, k)), sin_of(np.outer(k, k))
    gc, gs = cos_of(np.outer(u, k)), sin_of(np.outer(u, k))
    factor = np.where(k[:64] == 0, 1.0, 2.0)
    first = []
    for count, shift, slot in ((4, 16, 0), (2, 0, 0), (2, 96, 2)):
        table = np.zeros((128 * count + 16, 256))
        for i in range(count):
            rows = slice(32 * i + shift, 32 * i + shift + 128)
            table[i : 64 * count : count, rows] = c[:64]
            table[64 * count + i : 128 * count : count, rows] = -s[:64]
            table[128 * count + slot + i, rows] = (-1.0) ** k
        first.append(table)
    second = np.block([[c, -s], [s, c]])
    back_second = np.zeros((1024, 256))
    for w in range(4):
        rows, lanes = 256 * w, 32 * w
        back_second[rows : rows + 128, lanes : lanes + 32] = gc.T
        back_second[rows + 128 : rows + 256, lanes : lanes + 32] = -gs.T
        back_second[rows : rows + 128, 128 + lanes : 160 + lanes] = gs.T
        back_second[rows + 128 : rows + 256, 128 + lanes : 160 + lanes] = gc.T
    inner, outer = np.zeros((128, 512)), np.zeros((128, 512))
    for i in range(4):
        inner[i::4, i:256:4] = factor * gc[:, :64]
        inner[i::4, 256 + i : 512 : 4] = -factor * gs[:, :64]
        start = 128 * (i // 2) + i % 2
        outer[i::4, start : 128 * (i // 2) + 128 : 2] = factor * gc[:, :64]
        outer[i::4, 256 + start : 384 + 128 * (i // 2) : 2] = -factor * gs[:, :64]
    energy_cols = np.zeros((384, 128))
    for jj in range(4):
        energy_cols[128 + 32 * jj - HALO : 256 + 32 * jj - HALO, 32 * jj : 32 * jj + 32] = 1.0
    sums = np.zeros((256, 256))
    for lane in range(128):
        jj, comp = lane % 4, (lane // 32) % 2
        sums[32 * jj : 32 * jj + 32, lane] = 1.0
        if comp == 0:
            sums[128 + 32 * jj : 160 + 32 * jj, 128 + lane] = 1.0
        else:
            sums[32 * jj : 32 * jj + 32, 128 + lane] = u
    tables = {
        "inner": first[0], "upper": first[1], "lower": first[2], "second": second, "back_second": back_second,
        "back_first": np.concatenate([inner, outer], axis=0), "energy_cols": energy_cols, "sums": sums,
    }
    places, pieces, base = {}, [], 0
    for name, table in tables.items():
        rows, tiles = table.shape[0], table.shape[1] // 128
        places[name] = (base, rows, tiles)
        pieces += [table[:, 128 * t : 128 * t + 128] for t in range(tiles)]
        base += rows * tiles
    packed = np.concatenate(pieces, axis=0).astype(np.float32).astype(ml_dtypes.bfloat16)
    return places, packed


PLACES, PACKED = build_tables()


class Table:
    def __init__(self, ref, name):
        self.ref = ref
        self.base, self.rows, self.tiles = PLACES[name]

    def read(self, rows=None, tiles=None):
        rows = rows or slice(0, self.rows)
        tiles = range(self.tiles) if tiles is None else tiles
        starts = [self.base + t * self.rows for t in tiles]
        parts = [self.ref[b + rows.start : b + rows.stop, :] for b in starts]
        return parts[0] if len(parts) == 1 else jnp.concatenate(parts, axis=1)

    def read_part(self, part, rows):
        starts = [self.base + t * self.rows for t in range(self.tiles)]
        parts = [self.ref[pl.ds(pl.multiple_of(b + part * rows, 16), rows), :] for b in starts]
        return jnp.concatenate(parts, axis=1)


def mm(a, b):
    return jnp.dot(a, b, preferred_element_type=F32)


def split3(x):
    hi = x.astype(BF16)
    rest = x - hi.astype(F32)
    mid = rest.astype(BF16)
    low = (rest - mid.astype(F32)).astype(BF16)
    return jnp.concatenate([hi, mid, low], axis=0)


def mm_exact(x, w):
    n = x.shape[0]
    y = mm(split3(x), w)
    return y[:n] + y[n : 2 * n] + y[2 * n :]


def block_energies(s, blocks, lanes, pad, eb):
    for b in blocks:
        x = pad[s, 32 * b : 32 * b + 32, lanes].astype(F32)
        eb[s, b : b + 1, lanes] = jnp.sum(x * x, axis=0, keepdims=True)


def node_energies(s, columns, eb, en, energy_cols):
    e4 = eb[s, 0:8, :] + eb[s, 1:9, :] + eb[s, 2:10, :] + eb[s, 3:11, :]
    tiles = [e4[:, 128 * t : 128 * t + 128] for t in range(5)]
    rows = [jnp.concatenate([tiles[(q - 1) % 5], tiles[q], tiles[q + 1]], axis=1) for q in columns]
    y = mm_exact(jnp.concatenate(rows, axis=0), energy_cols.read())
    row = lax.broadcasted_iota(jnp.int32, (8, 128), 0)
    for n, q in enumerate(columns):
        e = y[8 * n : 8 * n + 8] * (1.0 / PATCH**2) + EPS
        en[s, INNER, q] = jnp.where(row < 4, pltpu.roll(e, 6, 0), pltpu.roll(e, 2, 0))
        en[s, OUTER, q] = jnp.where((row < 2) | (row >= 6), e, pltpu.roll(e, 4, 0))


INNER, OUTER = 0, 1
OWN_COLS, SIDE_COLS = (slice(0, 256), slice(256, 512)), (slice(512, 640),)


def first_transform(s, group, columns, pad, spec, tables):
    for lanes in columns:
        if group == INNER:
            parts = [(0, 256, mm(tables["inner"].read(), pad[s, HALO : HALO + 256, lanes]))]
        else:
            parts = [
                (0, 128, mm(tables["upper"].read(), pad[s, 0:256, lanes])),
                (128, 128, mm(tables["lower"].read(), pad[s, 96:352, lanes])),
            ]
        for n in range((lanes.stop - lanes.start) // 128):
            t = (lanes.start // 128 + n + 1) % 5
            cols = slice(128 * n, 128 * n + 128)
            last = None
            for row, count, y in parts:
                spec[s, group, t, 0, row : row + count, :] = y[0:count, cols].astype(BF16)
                spec[s, group, t, 1, row : row + count, :] = y[count : 2 * count, cols].astype(BF16)
                end = y[2 * count : 2 * count + 16, cols]
                last = end if last is None else last + end
            spec[s, group, t, 0, 256:272, :] = last.astype(BF16)
            spec[s, group, t, 1, 256:272, :] = jnp.zeros((16, 128), BF16)


def window(s, group, q, w, spec):
    start = 32 * w - HALO
    before = lax.rem(q + (1 if start >= 0 else 0), 5)
    after = lax.rem(before + 1, 5)
    lane = lax.broadcasted_iota(jnp.int32, (272, 128), 1)
    parts = []
    for part in range(2):
        parts.append(jnp.where(lane < start % 128, spec[s, group, after, part], spec[s, group, before, part]))
    return jnp.concatenate(parts, axis=1)


def cross(x0, x1):
    ar, ai, br, bi = x0[:, :128], x0[:, 128:], x1[:, :128], x1[:, 128:]
    return jnp.concatenate([(ar * br + ai * bi).astype(BF16), (ar * bi - ai * br).astype(BF16)], axis=1)


def unit_of(n):
    m = lax.rem(n, 4)
    return n // 8, lax.rem(n // 4, 2), lax.rem(m + 1, 3) + 2 * (m // 3)


def cross_unit(pair, n, spec, kept, crossed, tables):
    _, group, q = unit_of(n)
    for w in range(4):
        x1 = mm(window(pair + 1, group, q, w, spec), tables["second"].read())
        if pair == 0:
            x0 = mm(window(0, group, q, w, spec), tables["second"].read())
            kept[group, q, w] = x1.astype(BF16)
        else:
            x0 = kept[group, q, w].astype(F32)
        crossed[:, 256 * w : 256 * w + 256] = cross(x0, x1)


def columns_back(crossed, turned, last_row, tables):
    back = mm(crossed[...], tables["back_second"].read())
    turned[0:256, :] = back[0:256, :128].astype(BF16)
    turned[256:512, :] = back[0:256, 128:].astype(BF16)
    last = back[256:264, 0:128]
    low = lax.broadcasted_iota(jnp.int32, (8, 128), 0) < 4
    last_row[...] = jnp.where(low, last, -pltpu.roll(last, 4, 0))


def rows_back(n, turned, last_row, en, unit_sums, tables):
    pair, group, q = unit_of(n)
    corr = mm(tables["back_first"].read_part(group, 128), turned[...])
    low = lax.broadcasted_iota(jnp.int32, (8, 128), 0) < 4
    scale = (PATCH / 2.0 / PATCH**4) * lax.rsqrt(en[pair, group, q] * en[pair + 1, group, q])
    last = last_row[...]
    total = jnp.zeros((8, 128), F32)
    along = jnp.zeros((8, 128), F32)
    for u in range(0, SHIFTS, 2):
        weight = jnp.exp((corr[4 * u : 4 * u + 8] + last) * scale)
        total += weight
        along += weight * jnp.where(low, float(u - SHIFTS // 2), float(u + 1 - SHIFTS // 2))
    unit_sums[n, :, 0:128] = total + pltpu.roll(total, 4, 0)
    unit_sums[n, :, 128:256] = along + pltpu.roll(along, 4, 0)


def flow_block(unit_sums, sums, last_sec):
    row = lax.broadcasted_iota(jnp.int32, (8, 256), 0)
    pieces = []
    for pair in range(2):
        for q in range(4):
            m = (2, 0, 1, 3)[q]
            inner, outer = unit_sums[8 * pair + m], unit_sums[8 * pair + 4 + m]
            pieces.append(jnp.where((row >= 2) & (row < 6), pltpu.roll(inner, 2, 0), outer))
    y = mm_exact(jnp.concatenate(pieces, axis=0), sums.read())
    flow = y[:, 128:] / y[:, :128]
    lane = lax.broadcasted_iota(jnp.int32, (8, 128), 1)
    block = jnp.zeros((8, 128), F32)
    for pair in range(2):
        for q in range(4):
            first = 8 + 4 * q
            mine = (lane // 64 == pair) & (lane % 32 >= first) & (lane % 32 < first + 4)
            r = 32 * pair + 8 * q
            block = jnp.where(mine, flow[r : r + 8], block)
    return jnp.where((lane >= 64) & last_sec, 0.0, block)


def extend(own, left, right):
    lane = lax.broadcasted_iota(jnp.int32, own.shape, own.ndim - 1) % 32
    from_left = pltpu.roll(left, 112, own.ndim - 1)
    from_right = pltpu.roll(right, 16, own.ndim - 1)
    return jnp.where(lane < 8, from_left, jnp.where(lane >= 24, from_right, own))


def relax(flow, row_pos, col_pos):
    shape = flow[0].shape
    row = lax.broadcasted_iota(jnp.int32, shape, 0)
    lane = lax.broadcasted_iota(jnp.int32, shape, 1)
    node = lane % 32
    inside = ((row >= 8) | (row_pos > 0)) & ((row < 16) | (row_pos < TILE_GRID - 1))
    inside &= ((node >= 8) | (col_pos > 0)) & ((node < 24) | (col_pos < TILE_GRID - 1))
    mask = jnp.where(inside, 1.0, 0.0)
    low = lane < 64
    count = len(flow)
    zero = jnp.zeros(shape, F32)

    def following(f):
        turned = [pltpu.roll(x, 64, 1) for x in f] + [zero]
        return [jnp.where(low, turned[d], turned[d + 1]) for d in range(count)]

    def preceding(f):
        turned = [zero] + [pltpu.roll(x, 64, 1) for x in f]
        return [jnp.where(low, turned[d], turned[d + 1]) for d in range(count)]

    flow = [f * mask for f in flow]
    mesh = [zero] * count
    for step in range(ITERS):
        if step == 0:
            spring = [-f for f in flow]
        else:
            spring = [m - n - f for m, n, f in zip(mesh, following(mesh), flow)]
        earlier = preceding(spring)
        updated = []
        for m, sp, ea in zip(mesh, spring, earlier):
            change = sp - ea
            if step > 0:
                around = pltpu.roll(m, 1, 0) + pltpu.roll(m, 23, 0) + pltpu.roll(m, 1, 1) + pltpu.roll(m, 127, 1)
                change = change + 4.0 * m - around
            updated.append((m - STEP_RATE * change) * mask)
        mesh = updated
    return mesh


SHIFT_ROWS = 288


def shifted_columns(pad, cols):
    @pl.loop(0, SHIFT_ROWS // 16)
    def _(k):
        for s in range(2):
            x = pad[s, pl.ds(pl.multiple_of(32 + 16 * k, 16), 16), :].astype(F32)
            for d in range(5):
                y = x if d == 2 else pltpu.roll(x, (2 - d) % LANES, 1)
                for t in range(4):
                    cols[d, pl.ds(128 * k + (4 * s + t), 16, stride=8), :] = y[:, 128 * t : 128 * t + 128]


def pick_pair(high, odd, values):
    near = [jnp.where(high, values[k + 2], values[k]) for k in range(3)]
    return jnp.where(odd, near[1], near[0]), jnp.where(odd, near[2], near[1])


def corners(r, offsets, cols, coef):
    base = pl.multiple_of(8 * r, 8)
    view = []
    for k in range(12):
        rows = pl.ds(pl.multiple_of(8 * (base + 14 + k), 8), 8)
        view.append([cols[d, rows, :] for d in range(5)])
    for k in range(8):
        ro, co = offsets[0, base + k], offsets[1, base + k]
        row_high, row_odd = ro >= 0, (ro & 1) == 1
        col_high, col_odd = co >= 0, (co & 1) == 1
        pairs = [pick_pair(col_high, col_odd, view[k + dr]) for dr in range(5)]
        i00, i10 = pick_pair(row_high, row_odd, [p[0] for p in pairs])
        i01, i11 = pick_pair(row_high, row_odd, [p[1] for p in pairs])
        rf, cf = ro.astype(F32), co.astype(F32)
        top, low = i01 - i00, i11 - i10
        top0, low0 = i00 - cf * top, i10 - cf * low
        twist, lean = low - top, low0 - top0
        coef[0, base + k] = top0 - rf * lean
        coef[1, base + k] = lean
        coef[2, base + k] = top - rf * twist
        coef[3, base + k] = twist


def write_mesh(mesh, out):
    for s in range(2):
        for c in range(2):
            lane = 64 * s + 32 * c + 8
            out[s, c, 0] = mesh[:, lane : lane + 16]


def spread_lanes(mesh, i, c):
    tile = lax.broadcasted_iota(jnp.int32, (8, 128), 0)
    lane = lax.broadcasted_iota(jnp.int32, (8, 128), 1)
    place = 64 * (tile // 4) + 4 * (tile % 4) + lane // 32 + (32 * c + 8)
    return jnp.take_along_axis(jnp.broadcast_to(mesh[i : i + 1], (8, 128)), place, axis=1)


MESH = pl.DeviceIdType.MESH
AROUND = [(0, -1), (0, 1), (-1, 0), (1, 0), (-1, -1), (-1, 1), (1, -1), (1, 1)]


def pixel_part(dr, dc, sections, pad, from_left, from_right, src, dst):
    src_rows = {-1: pl.ds(0, HALO), 0: pl.ds(0, 256), 1: pl.ds(256 - HALO, HALO)}[dr]
    dst_rows = {-1: pl.ds(HALO + 256, HALO), 0: pl.ds(HALO, 256), 1: pl.ds(0, HALO)}[dr]
    if dc == 0:
        return sections.at[src, 0, src_rows, :], pad.at[dst, dst_rows, pl.ds(0, OWN_LANES)]
    if dc < 0:
        return sections.at[src, 0, src_rows, pl.ds(0, 128)], from_right.at[dst, dst_rows, :]
    return sections.at[src, 0, src_rows, pl.ds(OWN_LANES - 128, 128)], from_left.at[dst, dst_rows, :]


def merge_sides(s, rows, pad, from_left, from_right, col_pos):
    lane = lax.broadcasted_iota(jnp.int32, (rows.stop - rows.start, 128), 1)
    side = jnp.where(lane < 64, from_right[s, rows, :].astype(F32), from_left[s, rows, :].astype(F32))
    keep = ((lane < 64) & (col_pos < TILE_GRID - 1)) | ((lane >= 64) & (col_pos > 0))
    pad[s, rows, OWN_LANES:LANES] = jnp.where(keep, side, 0.0).astype(BF16)


def clear_edges(s, pad, row_pos):
    @pl.when(row_pos == 0)
    def _():
        pad[s, 0:HALO, :] = jnp.zeros((HALO, LANES), BF16)

    @pl.when(row_pos == TILE_GRID - 1)
    def _():
        pad[s, ROWS - HALO : ROWS, :] = jnp.zeros((HALO, LANES), BF16)


def pixel_forward(dr, dc, pad, from_left, from_right):
    src_rows = {-1: pl.ds(HALO, HALO), 0: pl.ds(HALO, 256), 1: pl.ds(256, HALO)}[dr]
    dst_rows = {-1: pl.ds(HALO + 256, HALO), 0: pl.ds(HALO, 256), 1: pl.ds(0, HALO)}[dr]
    if dc == 0:
        return pad.at[2, src_rows, pl.ds(0, OWN_LANES)], pad.at[2, dst_rows, pl.ds(0, OWN_LANES)]
    if dc < 0:
        return pad.at[2, src_rows, pl.ds(0, 128)], from_right.at[2, dst_rows, :]
    return pad.at[2, src_rows, pl.ds(OWN_LANES - 128, 128)], from_left.at[2, dst_rows, :]


def flow_kernel(sections, offsets_in, packed_in, coef, block_out,
                pad, from_left, from_right, offsets, packed, spec, kept, crossed, turned, last_row, eb, en, unit_sums, flows, cols,
                local_sem, pixel_send, pixel_recv, flow_send, flow_recv):
    tables = {name: Table(packed, name) for name in PLACES}
    sec, tile = lax.axis_index("sec"), lax.axis_index("tile")
    sec_count = lax.axis_size("sec")
    row_pos, col_pos = tile // TILE_GRID, tile % TILE_GRID

    def device(ds, dr, dc):
        row = lax.rem(row_pos + (dr + TILE_GRID), TILE_GRID)
        col = lax.rem(col_pos + (dc + TILE_GRID), TILE_GRID)
        return (lax.rem(sec + ds, sec_count), row * TILE_GRID + col)

    barrier = pltpu.get_barrier_semaphore()
    partners = [(ds, dr, dc) for ds in range(4) for dr, dc in AROUND + [(0, 0)] if (ds, dr, dc) != (0, 0, 0)]
    for p in partners:
        pl.semaphore_signal(barrier, inc=1, device_id=device(*p), device_id_type=MESH)
    own_copy = pltpu.make_async_copy(
        sections.at[:, 0], pad.at[pl.ds(0, 2), pl.ds(HALO, 256), pl.ds(0, OWN_LANES)], local_sem.at[0]
    )
    offset_copies = [
        pltpu.make_async_copy(
            offsets_in.at[c, s, 0, :, pl.ds(128 * t, 128)],
            offsets.at[c, :, 4 * s + t, :],
            local_sem.at[2 + 8 * c + 4 * s + t],
        )
        for c in range(2) for s in range(2) for t in range(4)
    ]
    table_copy = pltpu.make_async_copy(packed_in, packed, local_sem.at[1])
    pl.semaphore_wait(barrier, len(partners))

    def pixel_copy(k, ds, dr, dc, refs):
        return pltpu.make_async_remote_copy(
            src_ref=refs[0], dst_ref=refs[1], send_sem=pixel_send.at[k], recv_sem=pixel_recv.at[k],
            device_id=device(ds, dr, dc), device_id_type=MESH,
        )

    both = pl.ds(0, 2)
    own = [
        pixel_copy(k, 0, dr, dc, pixel_part(dr, dc, sections, pad, from_left, from_right, both, both))
        for k, (dr, dc) in enumerate(AROUND)
    ]
    after = pixel_copy(
        8, 3, 0, 0, pixel_part(0, 0, sections, pad, from_left, from_right, pl.ds(0, 1), pl.ds(2, 1))
    )
    for copy in [after] + own:
        copy.start()
    own_copy.start()
    table_copy.start()

    def transform(s, group, columns):
        first_transform(s, group, columns, pad, spec, tables)

    def energies(s, blocks, lanes, columns):
        block_energies(s, blocks, lanes, pad, eb)
        node_energies(s, columns, eb, en, tables["energy_cols"])

    def units(pair, first, count):
        @pl.loop(0, count)
        def _(k):
            n = first + k
            rows_back(n - 2, turned, last_row, en, unit_sums, tables)
            columns_back(crossed, turned, last_row, tables)
            cross_unit(pair, n, spec, kept, crossed, tables)

    inner_blocks, outer_blocks = range(2, 9), (0, 1, 9, 10)
    own_lanes, side_lanes, all_lanes = slice(0, OWN_LANES), slice(OWN_LANES, LANES), slice(0, LANES)

    def inner_own(s):
        transform(s, INNER, OWN_COLS)
        energies(s, inner_blocks, own_lanes, (1, 2))

    def inner_sides(s):
        merge_sides(s, slice(HALO, HALO + 256), pad, from_left, from_right, col_pos)
        transform(s, INNER, SIDE_COLS)
        energies(s, inner_blocks, side_lanes, (0, 3))

    def outer(s):
        merge_sides(s, slice(0, HALO), pad, from_left, from_right, col_pos)
        merge_sides(s, slice(HALO + 256, ROWS), pad, from_left, from_right, col_pos)
        clear_edges(s, pad, row_pos)
        transform(s, OUTER, OWN_COLS + SIDE_COLS)
        energies(s, outer_blocks, all_lanes, (0, 1, 2, 3))

    def corner_rows(first, count):
        @pl.loop(0, count)
        def _(k):
            corners(first + k, offsets, cols, coef)

    eb[...] = jnp.zeros(eb.shape, F32)
    own_copy.wait()
    table_copy.wait()
    pl.loop(0, 2)(inner_own)
    for copy in offset_copies:
        copy.start()
    cross_unit(0, 0, spec, kept, crossed, tables)
    columns_back(crossed, turned, last_row, tables)
    cross_unit(0, 1, spec, kept, crossed, tables)
    own[0].wait_recv()
    own[1].wait_recv()
    pl.loop(0, 2)(inner_sides)
    units(0, 2, 2)
    for copy in own[2:]:
        copy.wait_recv()
    pl.loop(0, 2)(outer)
    units(0, 4, 2)
    after.wait_recv()
    forward = [
        pixel_copy(9 + k, 0, dr, dc, pixel_forward(dr, dc, pad, from_left, from_right))
        for k, (dr, dc) in enumerate(AROUND)
    ]
    for copy in forward:
        copy.start()
    units(0, 6, 2)
    inner_own(2)
    units(1, 8, 2)
    forward[0].wait_recv()
    forward[1].wait_recv()
    inner_sides(2)
    units(1, 10, 2)
    for copy in forward[2:]:
        copy.wait_recv()
    outer(2)
    units(1, 12, 4)
    rows_back(14, turned, last_row, en, unit_sums, tables)
    columns_back(crossed, turned, last_row, tables)
    rows_back(15, turned, last_row, en, unit_sums, tables)

    flows[4, sec] = flow_block(unit_sums, tables["sums"], sec == sec_count - 1)
    spread = [(ds, dr, dc) for ds in range(4) for dr, dc in AROUND + [(0, 0)] if (ds, dr, dc) != (0, 0, 0)]
    spread.sort(key=lambda p: (2 - abs(2 - p[0]), abs(p[1]) + abs(p[2])), reverse=True)
    share = [
        pltpu.make_async_remote_copy(
            src_ref=flows.at[4, sec], dst_ref=flows.at[3 * (1 - dr) + 1 - dc, sec], send_sem=flow_send.at[k],
            recv_sem=flow_recv.at[k], device_id=device(ds, dr, dc), device_id_type=MESH,
        )
        for k, (ds, dr, dc) in enumerate(spread)
    ]
    for copy in share:
        copy.start()
    for copy in offset_copies:
        copy.wait()
    shifted_columns(pad, cols)
    corner_rows(0, 32)
    for copy in share:
        copy.wait_recv()

    def column(d, c):
        return jnp.concatenate([flows[c, d], flows[3 + c, d], flows[6 + c, d]], axis=0)

    mesh = relax([extend(column(d, 1), column(d, 0), column(d, 2)) for d in range(4)], row_pos, col_pos)
    mine = mesh[0][8:16]
    for d in range(1, 4):
        mine = jnp.where(sec == d, mesh[d][8:16], mine)
    block_out[...] = mine
    for copy in own + [after] + forward + share:
        copy.wait_send()


def blend_kernel(coef, block, mesh_out, warped, result, sem):
    mesh = block[...]
    write_mesh(mesh, mesh_out)
    copies = []
    for i in range(8):
        a, b = spread_lanes(mesh, i, 0), spread_lanes(mesh, i, 1)
        for k in range(32):
            r = 32 * i + k
            first = coef[0, r] + a * coef[1, r]
            second = coef[2, r] + a * coef[3, r]
            result[r] = first + b * second
        if i % 2 == 1:
            rows = pl.ds(32 * i - 32, 64)
            for s in range(2):
                for t in range(4):
                    copy = pltpu.make_async_copy(
                        result.at[rows, 4 * s + t, :], warped.at[s, 0, rows, pl.ds(128 * t, 128)], sem.at[len(copies)]
                    )
                    copy.start()
                    copies.append(copy)
    for copy in copies:
        copy.wait()


def vmem():
    return pl.BlockSpec(memory_space=pltpu.VMEM)


def shards(sections, corner_offsets):
    anywhere = pl.BlockSpec(memory_space=pl.ANY)
    dma = pltpu.SemaphoreType.DMA
    coef, block = pl.pallas_call(
        flow_kernel,
        out_shape=(pltpu.VMEM((4, 256, 8, 128), F32), pltpu.VMEM((8, 128), F32)),
        in_specs=[anywhere, anywhere, anywhere],
        out_specs=(vmem(), vmem()),
        scratch_shapes=[
            pltpu.VMEM((3, ROWS, LANES), BF16),
            pltpu.VMEM((3, ROWS, 128), BF16),
            pltpu.VMEM((3, ROWS, 128), BF16),
            pltpu.VMEM((2, 256, 8, 128), jnp.int32),
            pltpu.VMEM(PACKED.shape, BF16),
            pltpu.VMEM((3, 2, 5, 2, 272, 128), BF16),
            pltpu.VMEM((2, 4, 4, 272, 256), BF16),
            pltpu.VMEM((272, 1024), BF16),
            pltpu.VMEM((512, 128), BF16),
            pltpu.VMEM((8, 128), F32),
            pltpu.VMEM((3, 16, LANES), F32),
            pltpu.VMEM((3, 2, 4, 8, 128), F32),
            pltpu.VMEM((16, 8, 256), F32),
            pltpu.VMEM((9, 4, 8, 128), F32),
            pltpu.VMEM((5, 8 * SHIFT_ROWS, 128), F32),
            dma((18,)),
            dma((17,)),
            dma((17,)),
            dma((35,)),
            dma((35,)),
        ],
        compiler_params=pltpu.CompilerParams(
            vmem_limit_bytes=58 * 2**20, collective_id=0, has_side_effects=True
        ),
    )(sections, corner_offsets, jnp.asarray(PACKED))
    return pl.pallas_call(
        blend_kernel,
        out_shape=(
            jax.ShapeDtypeStruct((2, 2, 1, 8, 16), F32),
            jax.ShapeDtypeStruct((2, 1, 256, 512), F32),
        ),
        in_specs=[vmem(), vmem()],
        out_specs=(vmem(), anywhere),
        scratch_shapes=[pltpu.VMEM((256, 8, 128), F32), dma((32,))],
        compiler_params=pltpu.CompilerParams(vmem_limit_bytes=20 * 2**20),
    )(coef, block)


def solution(mesh):
    in_specs = (P("sec", "tile", None, None), P(None, "sec", "tile", None, None))
    out_specs = (P("sec", None, "tile", None, None), P("sec", "tile", None, None))
    return jax.shard_map(shards, mesh=mesh, in_specs=in_specs, out_specs=out_specs, check_vma=False)
```

```python
import math

import jax
import jax.numpy as jnp
import ml_dtypes
import numpy as np
from jax import lax
from jax.experimental import pallas as pl
from jax.experimental.pallas import tpu as pltpu
from jax.sharding import PartitionSpec as P

TILE_GRID = 8
PATCH = 128
STRIDE = 32
SHIFTS = 32
ITERS = 4
HALO = 48
EPS = 1e-05
STEP_RATE = 0.15
ROWS = 352
LANES = 640
OWN_LANES = 512
F32 = jnp.float32
BF16 = jnp.bfloat16


def build_tables():
    k = np.arange(PATCH)
    u = np.arange(SHIFTS) - SHIFTS // 2

    def cos_of(m):
        return np.cos(2 * np.pi * (m % PATCH) / PATCH)

    def sin_of(m):
        return np.sin(2 * np.pi * (m % PATCH) / PATCH)

    c, s = cos_of(np.outer(k, k)), sin_of(np.outer(k, k))
    gc, gs = cos_of(np.outer(u, k)), sin_of(np.outer(u, k))
    factor = np.where(k[:64] == 0, 1.0, 2.0)
    first = []
    for count, shift, slot in ((4, 16, 0), (2, 0, 0), (2, 96, 2)):
        table = np.zeros((128 * count + 16, 256))
        for i in range(count):
            rows = slice(32 * i + shift, 32 * i + shift + 128)
            table[i : 64 * count : count, rows] = c[:64]
            table[64 * count + i : 128 * count : count, rows] = -s[:64]
            table[128 * count + slot + i, rows] = (-1.0) ** k
        first.append(table)
    second = np.block([[c, -s], [s, c]])
    back_second = np.zeros((1024, 256))
    for w in range(4):
        rows, lanes = 256 * w, 32 * w
        back_second[rows : rows + 128, lanes : lanes + 32] = gc.T
        back_second[rows + 128 : rows + 256, lanes : lanes + 32] = -gs.T
        back_second[rows : rows + 128, 128 + lanes : 160 + lanes] = gs.T
        back_second[rows + 128 : rows + 256, 128 + lanes : 160 + lanes] = gc.T
    inner, outer = np.zeros((128, 512)), np.zeros((128, 512))
    for i in range(4):
        inner[i::4, i:256:4] = factor * gc[:, :64]
        inner[i::4, 256 + i : 512 : 4] = -factor * gs[:, :64]
        start = 128 * (i // 2) + i % 2
        outer[i::4, start : 128 * (i // 2) + 128 : 2] = factor * gc[:, :64]
        outer[i::4, 256 + start : 384 + 128 * (i // 2) : 2] = -factor * gs[:, :64]
    energy_cols = np.zeros((384, 128))
    for jj in range(4):
        energy_cols[128 + 32 * jj - HALO : 256 + 32 * jj - HALO, 32 * jj : 32 * jj + 32] = 1.0
    sums = np.zeros((256, 256))
    for lane in range(128):
        jj, comp = lane % 4, (lane // 32) % 2
        sums[32 * jj : 32 * jj + 32, lane] = 1.0
        if comp == 0:
            sums[128 + 32 * jj : 160 + 32 * jj, 128 + lane] = 1.0
        else:
            sums[32 * jj : 32 * jj + 32, 128 + lane] = u
    tables = {
        "inner": first[0], "upper": first[1], "lower": first[2], "second": second, "back_second": back_second,
        "back_first": np.concatenate([inner, outer], axis=0), "energy_cols": energy_cols, "sums": sums,
    }
    places, pieces, base = {}, [], 0
    for name, table in tables.items():
        rows, tiles = table.shape[0], table.shape[1] // 128
        places[name] = (base, rows, tiles)
        pieces += [table[:, 128 * t : 128 * t + 128] for t in range(tiles)]
        base += rows * tiles
    packed = np.concatenate(pieces, axis=0).astype(np.float32).astype(ml_dtypes.bfloat16)
    return places, packed


PLACES, PACKED = build_tables()


class Table:
    def __init__(self, ref, name):
        self.ref = ref
        self.base, self.rows, self.tiles = PLACES[name]

    def read(self, rows=None, tiles=None):
        rows = rows or slice(0, self.rows)
        tiles = range(self.tiles) if tiles is None else tiles
        starts = [self.base + t * self.rows for t in tiles]
        parts = [self.ref[b + rows.start : b + rows.stop, :] for b in starts]
        return parts[0] if len(parts) == 1 else jnp.concatenate(parts, axis=1)

    def read_part(self, part, rows):
        starts = [self.base + t * self.rows for t in range(self.tiles)]
        parts = [self.ref[pl.ds(pl.multiple_of(b + part * rows, 16), rows), :] for b in starts]
        return jnp.concatenate(parts, axis=1)


def mm(a, b):
    return jnp.dot(a, b, preferred_element_type=F32)


def split3(x):
    hi = x.astype(BF16)
    rest = x - hi.astype(F32)
    mid = rest.astype(BF16)
    low = (rest - mid.astype(F32)).astype(BF16)
    return jnp.concatenate([hi, mid, low], axis=0)


def mm_exact(x, w):
    n = x.shape[0]
    y = mm(split3(x), w)
    return y[:n] + y[n : 2 * n] + y[2 * n :]


def block_energies(s, blocks, lanes, pad, eb):
    for b in blocks:
        x = pad[s, 32 * b : 32 * b + 32, lanes].astype(F32)
        eb[s, b : b + 1, lanes] = jnp.sum(x * x, axis=0, keepdims=True)


def node_energies(s, columns, eb, en, energy_cols):
    e4 = eb[s, 0:8, :] + eb[s, 1:9, :] + eb[s, 2:10, :] + eb[s, 3:11, :]
    tiles = [e4[:, 128 * t : 128 * t + 128] for t in range(5)]
    rows = [jnp.concatenate([tiles[(q - 1) % 5], tiles[q], tiles[q + 1]], axis=1) for q in columns]
    y = mm_exact(jnp.concatenate(rows, axis=0), energy_cols.read())
    row = lax.broadcasted_iota(jnp.int32, (8, 128), 0)
    for n, q in enumerate(columns):
        e = y[8 * n : 8 * n + 8] * (1.0 / PATCH**2) + EPS
        en[s, INNER, q] = jnp.where(row < 4, pltpu.roll(e, 6, 0), pltpu.roll(e, 2, 0))
        en[s, OUTER, q] = jnp.where((row < 2) | (row >= 6), e, pltpu.roll(e, 4, 0))


INNER, OUTER = 0, 1
OWN_COLS, SIDE_COLS = (slice(0, 256), slice(256, 512)), (slice(512, 640),)


def first_transform(s, group, columns, pad, spec, tables):
    for lanes in columns:
        if group == INNER:
            parts = [(0, 256, mm(tables["inner"].read(), pad[s, HALO : HALO + 256, lanes]))]
        else:
            parts = [
                (0, 128, mm(tables["upper"].read(), pad[s, 0:256, lanes])),
                (128, 128, mm(tables["lower"].read(), pad[s, 96:352, lanes])),
            ]
        for n in range((lanes.stop - lanes.start) // 128):
            t = (lanes.start // 128 + n + 1) % 5
            cols = slice(128 * n, 128 * n + 128)
            last = None
            for row, count, y in parts:
                spec[s, group, t, 0, row : row + count, :] = y[0:count, cols].astype(BF16)
                spec[s, group, t, 1, row : row + count, :] = y[count : 2 * count, cols].astype(BF16)
                end = y[2 * count : 2 * count + 16, cols]
                last = end if last is None else last + end
            spec[s, group, t, 0, 256:272, :] = last.astype(BF16)
            spec[s, group, t, 1, 256:272, :] = jnp.zeros((16, 128), BF16)


def window(s, group, q, w, spec):
    start = 32 * w - HALO
    before = lax.rem(q + (1 if start >= 0 else 0), 5)
    after = lax.rem(before + 1, 5)
    lane = lax.broadcasted_iota(jnp.int32, (272, 128), 1)
    parts = []
    for part in range(2):
        parts.append(jnp.where(lane < start % 128, spec[s, group, after, part], spec[s, group, before, part]))
    return jnp.concatenate(parts, axis=1)


def cross(x0, x1):
    ar, ai, br, bi = x0[:, :128], x0[:, 128:], x1[:, :128], x1[:, 128:]
    return jnp.concatenate([(ar * br + ai * bi).astype(BF16), (ar * bi - ai * br).astype(BF16)], axis=1)


def unit_of(n):
    m = lax.rem(n, 4)
    return n // 8, lax.rem(n // 4, 2), lax.rem(m + 1, 3) + 2 * (m // 3)


def cross_unit(pair, n, spec, kept, crossed, tables):
    _, group, q = unit_of(n)
    for w in range(4):
        x1 = mm(window(pair + 1, group, q, w, spec), tables["second"].read())
        if pair == 0:
            x0 = mm(window(0, group, q, w, spec), tables["second"].read())
            kept[group, q, w] = x1.astype(BF16)
        else:
            x0 = kept[group, q, w].astype(F32)
        crossed[:, 256 * w : 256 * w + 256] = cross(x0, x1)


def columns_back(crossed, turned, last_row, tables):
    back = mm(crossed[...], tables["back_second"].read())
    turned[0:256, :] = back[0:256, :128].astype(BF16)
    turned[256:512, :] = back[0:256, 128:].astype(BF16)
    last = back[256:264, 0:128]
    low = lax.broadcasted_iota(jnp.int32, (8, 128), 0) < 4
    last_row[...] = jnp.where(low, last, -pltpu.roll(last, 4, 0))


def rows_back(n, turned, last_row, en, unit_sums, tables):
    pair, group, q = unit_of(n)
    corr = mm(tables["back_first"].read_part(group, 128), turned[...])
    low = lax.broadcasted_iota(jnp.int32, (8, 128), 0) < 4
    scale = (PATCH / 2.0 / PATCH**4) * lax.rsqrt(en[pair, group, q] * en[pair + 1, group, q])
    last = last_row[...]
    total = jnp.zeros((8, 128), F32)
    along = jnp.zeros((8, 128), F32)
    for u in range(0, SHIFTS, 2):
        weight = jnp.exp((corr[4 * u : 4 * u + 8] + last) * scale)
        total += weight
        along += weight * jnp.where(low, float(u - SHIFTS // 2), float(u + 1 - SHIFTS // 2))
    unit_sums[n, :, 0:128] = total + pltpu.roll(total, 4, 0)
    unit_sums[n, :, 128:256] = along + pltpu.roll(along, 4, 0)


def flow_block(unit_sums, sums, last_sec):
    row = lax.broadcasted_iota(jnp.int32, (8, 256), 0)
    pieces = []
    for pair in range(2):
        for q in range(4):
            m = (2, 0, 1, 3)[q]
            inner, outer = unit_sums[8 * pair + m], unit_sums[8 * pair + 4 + m]
            pieces.append(jnp.where((row >= 2) & (row < 6), pltpu.roll(inner, 2, 0), outer))
    y = mm_exact(jnp.concatenate(pieces, axis=0), sums.read())
    flow = y[:, 128:] / y[:, :128]
    lane = lax.broadcasted_iota(jnp.int32, (8, 128), 1)
    block = jnp.zeros((8, 128), F32)
    for pair in range(2):
        for q in range(4):
            first = 8 + 4 * q
            mine = (lane // 64 == pair) & (lane % 32 >= first) & (lane % 32 < first + 4)
            r = 32 * pair + 8 * q
            block = jnp.where(mine, flow[r : r + 8], block)
    return jnp.where((lane >= 64) & last_sec, 0.0, block)


def extend(own, left, right):
    lane = lax.broadcasted_iota(jnp.int32, own.shape, own.ndim - 1) % 32
    from_left = pltpu.roll(left, 112, own.ndim - 1)
    from_right = pltpu.roll(right, 16, own.ndim - 1)
    return jnp.where(lane < 8, from_left, jnp.where(lane >= 24, from_right, own))


def relax(flow, row_pos, col_pos):
    shape = flow[0].shape
    row = lax.broadcasted_iota(jnp.int32, shape, 0)
    lane = lax.broadcasted_iota(jnp.int32, shape, 1)
    node = lane % 32
    inside = ((row >= 8) | (row_pos > 0)) & ((row < 16) | (row_pos < TILE_GRID - 1))
    inside &= ((node >= 8) | (col_pos > 0)) & ((node < 24) | (col_pos < TILE_GRID - 1))
    mask = jnp.where(inside, 1.0, 0.0)
    low = lane < 64
    count = len(flow)
    zero = jnp.zeros(shape, F32)

    def following(f):
        turned = [pltpu.roll(x, 64, 1) for x in f] + [zero]
        return [jnp.where(low, turned[d], turned[d + 1]) for d in range(count)]

    def preceding(f):
        turned = [zero] + [pltpu.roll(x, 64, 1) for x in f]
        return [jnp.where(low, turned[d], turned[d + 1]) for d in range(count)]

    flow = [f * mask for f in flow]
    mesh = [zero] * count
    for step in range(ITERS):
        if step == 0:
            spring = [-f for f in flow]
        else:
            spring = [m - n - f for m, n, f in zip(mesh, following(mesh), flow)]
        earlier = preceding(spring)
        updated = []
        for m, sp, ea in zip(mesh, spring, earlier):
            change = sp - ea
            if step > 0:
                around = pltpu.roll(m, 1, 0) + pltpu.roll(m, 23, 0) + pltpu.roll(m, 1, 1) + pltpu.roll(m, 127, 1)
                change = change + 4.0 * m - around
            updated.append((m - STEP_RATE * change) * mask)
        mesh = updated
    return mesh


SHIFT_ROWS = 288


def shifted_columns(k, pad, cols):
    for s in range(2):
        x = pad[s, pl.ds(pl.multiple_of(32 + 16 * k, 16), 16), :].astype(F32)
        for d in range(5):
            y = x if d == 2 else pltpu.roll(x, (2 - d) % LANES, 1)
            for t in range(4):
                cols[d, pl.ds(128 * k + (4 * s + t), 16, stride=8), :] = y[:, 128 * t : 128 * t + 128]


def pick_pair(high, odd, values):
    near = [jnp.where(high, values[k + 2], values[k]) for k in range(3)]
    return jnp.where(odd, near[1], near[0]), jnp.where(odd, near[2], near[1])


def corners(r, offsets, cols, coef):
    base = pl.multiple_of(8 * r, 8)
    view = []
    for k in range(12):
        rows = pl.ds(pl.multiple_of(8 * (base + 14 + k), 8), 8)
        view.append([cols[d, rows, :] for d in range(5)])
    for k in range(8):
        ro, co = offsets[0, base + k], offsets[1, base + k]
        row_high, row_odd = ro >= 0, (ro & 1) == 1
        col_high, col_odd = co >= 0, (co & 1) == 1
        pairs = [pick_pair(col_high, col_odd, view[k + dr]) for dr in range(5)]
        i00, i10 = pick_pair(row_high, row_odd, [p[0] for p in pairs])
        i01, i11 = pick_pair(row_high, row_odd, [p[1] for p in pairs])
        rf, cf = ro.astype(F32), co.astype(F32)
        top, low = i01 - i00, i11 - i10
        top0, low0 = i00 - cf * top, i10 - cf * low
        twist, lean = low - top, low0 - top0
        coef[0, base + k] = top0 - rf * lean
        coef[1, base + k] = lean
        coef[2, base + k] = top - rf * twist
        coef[3, base + k] = twist


def write_mesh(mesh, out):
    for s in range(2):
        for c in range(2):
            lane = 64 * s + 32 * c + 8
            out[s, c, 0] = mesh[:, lane : lane + 16]


def spread_lanes(mesh, i, c):
    tile = lax.broadcasted_iota(jnp.int32, (8, 128), 0)
    lane = lax.broadcasted_iota(jnp.int32, (8, 128), 1)
    place = 64 * (tile // 4) + 4 * (tile % 4) + lane // 32 + (32 * c + 8)
    return jnp.take_along_axis(jnp.broadcast_to(mesh[i : i + 1], (8, 128)), place, axis=1)


MESH = pl.DeviceIdType.MESH
AROUND = [(0, -1), (0, 1), (-1, 0), (1, 0), (-1, -1), (-1, 1), (1, -1), (1, 1)]


def pixel_part(dr, dc, sections, pad, from_left, from_right, src, dst):
    src_rows = {-1: pl.ds(0, HALO), 0: pl.ds(0, 256), 1: pl.ds(256 - HALO, HALO)}[dr]
    dst_rows = {-1: pl.ds(HALO + 256, HALO), 0: pl.ds(HALO, 256), 1: pl.ds(0, HALO)}[dr]
    if dc == 0:
        return sections.at[src, 0, src_rows, :], pad.at[dst, dst_rows, pl.ds(0, OWN_LANES)]
    if dc < 0:
        return sections.at[src, 0, src_rows, pl.ds(0, 128)], from_right.at[dst, dst_rows, :]
    return sections.at[src, 0, src_rows, pl.ds(OWN_LANES - 128, 128)], from_left.at[dst, dst_rows, :]


def merge_sides(s, rows, pad, from_left, from_right, col_pos):
    lane = lax.broadcasted_iota(jnp.int32, (rows.stop - rows.start, 128), 1)
    side = jnp.where(lane < 64, from_right[s, rows, :].astype(F32), from_left[s, rows, :].astype(F32))
    keep = ((lane < 64) & (col_pos < TILE_GRID - 1)) | ((lane >= 64) & (col_pos > 0))
    pad[s, rows, OWN_LANES:LANES] = jnp.where(keep, side, 0.0).astype(BF16)


def clear_edges(s, pad, row_pos):
    @pl.when(row_pos == 0)
    def _():
        pad[s, 0:HALO, :] = jnp.zeros((HALO, LANES), BF16)

    @pl.when(row_pos == TILE_GRID - 1)
    def _():
        pad[s, ROWS - HALO : ROWS, :] = jnp.zeros((HALO, LANES), BF16)


def pixel_forward(dr, dc, pad, from_left, from_right):
    src_rows = {-1: pl.ds(HALO, HALO), 0: pl.ds(HALO, 256), 1: pl.ds(256, HALO)}[dr]
    dst_rows = {-1: pl.ds(HALO + 256, HALO), 0: pl.ds(HALO, 256), 1: pl.ds(0, HALO)}[dr]
    if dc == 0:
        return pad.at[2, src_rows, pl.ds(0, OWN_LANES)], pad.at[2, dst_rows, pl.ds(0, OWN_LANES)]
    if dc < 0:
        return pad.at[2, src_rows, pl.ds(0, 128)], from_right.at[2, dst_rows, :]
    return pad.at[2, src_rows, pl.ds(OWN_LANES - 128, 128)], from_left.at[2, dst_rows, :]


def flow_kernel(sections, offsets_in, packed_in, coef, block_out,
                pad, from_left, from_right, offsets, packed, spec, kept, crossed, turned, last_row, eb, en, unit_sums, flows, cols,
                local_sem, pixel_send, pixel_recv, flow_send, flow_recv):
    tables = {name: Table(packed, name) for name in PLACES}
    sec, tile = lax.axis_index("sec"), lax.axis_index("tile")
    sec_count = lax.axis_size("sec")
    row_pos, col_pos = tile // TILE_GRID, tile % TILE_GRID

    def device(ds, dr, dc):
        row = lax.rem(row_pos + (dr + TILE_GRID), TILE_GRID)
        col = lax.rem(col_pos + (dc + TILE_GRID), TILE_GRID)
        return (lax.rem(sec + ds, sec_count), row * TILE_GRID + col)

    barrier = pltpu.get_barrier_semaphore()
    partners = [(ds, dr, dc) for ds in range(4) for dr, dc in AROUND + [(0, 0)] if (ds, dr, dc) != (0, 0, 0)]
    for p in partners:
        pl.semaphore_signal(barrier, inc=1, device_id=device(*p), device_id_type=MESH)
    own_copy = pltpu.make_async_copy(
        sections.at[:, 0], pad.at[pl.ds(0, 2), pl.ds(HALO, 256), pl.ds(0, OWN_LANES)], local_sem.at[0]
    )
    offset_copies = [
        pltpu.make_async_copy(
            offsets_in.at[c, s, 0, :, pl.ds(128 * t, 128)],
            offsets.at[c, :, 4 * s + t, :],
            local_sem.at[2 + 8 * c + 4 * s + t],
        )
        for c in range(2) for s in range(2) for t in range(4)
    ]
    table_copy = pltpu.make_async_copy(packed_in, packed, local_sem.at[1])
    own_copy.start()
    table_copy.start()
    for copy in offset_copies:
        copy.start()
    pl.semaphore_wait(barrier, len(partners))

    def pixel_copy(k, ds, dr, dc, refs):
        return pltpu.make_async_remote_copy(
            src_ref=refs[0], dst_ref=refs[1], send_sem=pixel_send.at[k], recv_sem=pixel_recv.at[k],
            device_id=device(ds, dr, dc), device_id_type=MESH,
        )

    both = pl.ds(0, 2)
    own = [
        pixel_copy(k, 0, dr, dc, pixel_part(dr, dc, sections, pad, from_left, from_right, both, both))
        for k, (dr, dc) in enumerate(AROUND)
    ]
    after = pixel_copy(
        8, 3, 0, 0, pixel_part(0, 0, sections, pad, from_left, from_right, pl.ds(0, 1), pl.ds(2, 1))
    )
    for copy in own + [after]:
        copy.start()

    def transform(s, group, columns):
        first_transform(s, group, columns, pad, spec, tables)

    def energies(s, blocks, lanes, columns):
        block_energies(s, blocks, lanes, pad, eb)
        node_energies(s, columns, eb, en, tables["energy_cols"])

    def units(pair, first, count, beside=lambda k: None):
        @pl.loop(0, count)
        def _(k):
            n = first + k
            rows_back(n - 2, turned, last_row, en, unit_sums, tables)
            columns_back(crossed, turned, last_row, tables)
            cross_unit(pair, n, spec, kept, crossed, tables)
            beside(k)

    def shifts(first, each):
        def run(k):
            for i in range(each):
                shifted_columns(first + each * k + i, pad, cols)

        return run

    inner_blocks, outer_blocks = range(2, 9), (0, 1, 9, 10)
    own_lanes, side_lanes, all_lanes = slice(0, OWN_LANES), slice(OWN_LANES, LANES), slice(0, LANES)

    def inner_own(s):
        transform(s, INNER, OWN_COLS)
        energies(s, inner_blocks, own_lanes, (1, 2))

    def inner_sides(s):
        merge_sides(s, slice(HALO, HALO + 256), pad, from_left, from_right, col_pos)
        transform(s, INNER, SIDE_COLS)
        energies(s, inner_blocks, side_lanes, (0, 3))

    def outer(s):
        merge_sides(s, slice(0, HALO), pad, from_left, from_right, col_pos)
        merge_sides(s, slice(HALO + 256, ROWS), pad, from_left, from_right, col_pos)
        clear_edges(s, pad, row_pos)
        transform(s, OUTER, OWN_COLS + SIDE_COLS)
        energies(s, outer_blocks, all_lanes, (0, 1, 2, 3))

    def corner_rows(first, count):
        @pl.loop(0, count)
        def _(k):
            corners(first + k, offsets, cols, coef)

    eb[...] = jnp.zeros(eb.shape, F32)
    own_copy.wait()
    table_copy.wait()
    pl.loop(0, 2)(inner_own)
    cross_unit(0, 0, spec, kept, crossed, tables)
    columns_back(crossed, turned, last_row, tables)
    cross_unit(0, 1, spec, kept, crossed, tables)
    own[0].wait_recv()
    own[1].wait_recv()
    pl.loop(0, 2)(inner_sides)
    units(0, 2, 2)
    for copy in own[2:]:
        copy.wait_recv()
    pl.loop(0, 2)(outer)
    units(0, 4, 2, shifts(0, 5))
    after.wait_recv()
    forward = [
        pixel_copy(9 + k, 0, dr, dc, pixel_forward(dr, dc, pad, from_left, from_right))
        for k, (dr, dc) in enumerate(AROUND)
    ]
    for copy in forward:
        copy.start()
    units(0, 6, 2, shifts(10, 4))
    inner_own(2)
    units(1, 8, 2)
    forward[0].wait_recv()
    forward[1].wait_recv()
    inner_sides(2)
    units(1, 10, 2)
    for copy in forward[2:]:
        copy.wait_recv()
    outer(2)
    units(1, 12, 4)
    rows_back(14, turned, last_row, en, unit_sums, tables)
    columns_back(crossed, turned, last_row, tables)
    rows_back(15, turned, last_row, en, unit_sums, tables)

    flows[4, sec] = flow_block(unit_sums, tables["sums"], sec == sec_count - 1)
    spread = [(ds, dr, dc) for ds in range(4) for dr, dc in AROUND + [(0, 0)] if (ds, dr, dc) != (0, 0, 0)]
    share = [
        pltpu.make_async_remote_copy(
            src_ref=flows.at[4, sec], dst_ref=flows.at[3 * (1 - dr) + 1 - dc, sec], send_sem=flow_send.at[k],
            recv_sem=flow_recv.at[k], device_id=device(ds, dr, dc), device_id_type=MESH,
        )
        for k, (ds, dr, dc) in enumerate(spread)
    ]
    for copy in share:
        copy.start()
    for copy in offset_copies:
        copy.wait()
    corner_rows(0, 32)
    for copy in share:
        copy.wait_recv()

    def column(d, c):
        return jnp.concatenate([flows[c, d], flows[3 + c, d], flows[6 + c, d]], axis=0)

    mesh = relax([extend(column(d, 1), column(d, 0), column(d, 2)) for d in range(4)], row_pos, col_pos)
    mine = mesh[0][8:16]
    for d in range(1, 4):
        mine = jnp.where(sec == d, mesh[d][8:16], mine)
    block_out[...] = mine
    for copy in own + [after] + forward + share:
        copy.wait_send()


def blend_kernel(coef, block, mesh_out, warped, result, sem):
    mesh = block[...]
    write_mesh(mesh, mesh_out)
    copies = []
    for i in range(8):
        a, b = spread_lanes(mesh, i, 0), spread_lanes(mesh, i, 1)
        for k in range(32):
            r = 32 * i + k
            first = coef[0, r] + a * coef[1, r]
            second = coef[2, r] + a * coef[3, r]
            result[r] = first + b * second
        if i % 2 == 1:
            rows = pl.ds(32 * i - 32, 64)
            for s in range(2):
                for t in range(4):
                    copy = pltpu.make_async_copy(
                        result.at[rows, 4 * s + t, :], warped.at[s, 0, rows, pl.ds(128 * t, 128)], sem.at[len(copies)]
                    )
                    copy.start()
                    copies.append(copy)
    for copy in copies:
        copy.wait()


def vmem():
    return pl.BlockSpec(memory_space=pltpu.VMEM)


def shards(sections, corner_offsets):
    anywhere = pl.BlockSpec(memory_space=pl.ANY)
    dma = pltpu.SemaphoreType.DMA
    coef, block = pl.pallas_call(
        flow_kernel,
        out_shape=(pltpu.VMEM((4, 256, 8, 128), F32), pltpu.VMEM((8, 128), F32)),
        in_specs=[anywhere, anywhere, anywhere],
        out_specs=(vmem(), vmem()),
        scratch_shapes=[
            pltpu.VMEM((3, ROWS, LANES), BF16),
            pltpu.VMEM((3, ROWS, 128), BF16),
            pltpu.VMEM((3, ROWS, 128), BF16),
            pltpu.VMEM((2, 256, 8, 128), jnp.int32),
            pltpu.VMEM(PACKED.shape, BF16),
            pltpu.VMEM((3, 2, 5, 2, 272, 128), BF16),
            pltpu.VMEM((2, 4, 4, 272, 256), BF16),
            pltpu.VMEM((272, 1024), BF16),
            pltpu.VMEM((512, 128), BF16),
            pltpu.VMEM((8, 128), F32),
            pltpu.VMEM((3, 16, LANES), F32),
            pltpu.VMEM((3, 2, 4, 8, 128), F32),
            pltpu.VMEM((16, 8, 256), F32),
            pltpu.VMEM((9, 4, 8, 128), F32),
            pltpu.VMEM((5, 8 * SHIFT_ROWS, 128), F32),
            dma((18,)),
            dma((17,)),
            dma((17,)),
            dma((35,)),
            dma((35,)),
        ],
        compiler_params=pltpu.CompilerParams(
            vmem_limit_bytes=58 * 2**20, collective_id=0, has_side_effects=True
        ),
    )(sections, corner_offsets, jnp.asarray(PACKED))
    return pl.pallas_call(
        blend_kernel,
        out_shape=(
            jax.ShapeDtypeStruct((2, 2, 1, 8, 16), F32),
            jax.ShapeDtypeStruct((2, 1, 256, 512), F32),
        ),
        in_specs=[vmem(), vmem()],
        out_specs=(vmem(), anywhere),
        scratch_shapes=[pltpu.VMEM((256, 8, 128), F32), dma((32,))],
        compiler_params=pltpu.CompilerParams(vmem_limit_bytes=20 * 2**20),
    )(coef, block)


def solution(mesh):
    in_specs = (P("sec", "tile", None, None), P(None, "sec", "tile", None, None))
    out_specs = (P("sec", None, "tile", None, None), P("sec", "tile", None, None))
    return jax.shard_map(shards, mesh=mesh, in_specs=in_specs, out_specs=out_specs, check_vma=False)
```

```python
import math

import jax
import jax.numpy as jnp
import ml_dtypes
import numpy as np
from jax import lax
from jax.experimental import pallas as pl
from jax.experimental.pallas import tpu as pltpu
from jax.sharding import PartitionSpec as P

TILE_GRID = 8
PATCH = 128
STRIDE = 32
SHIFTS = 32
ITERS = 4
HALO = 48
EPS = 1e-05
STEP_RATE = 0.15
ROWS = 352
LANES = 640
OWN_LANES = 512
F32 = jnp.float32
BF16 = jnp.bfloat16


def build_tables():
    k = np.arange(PATCH)
    u = np.arange(SHIFTS) - SHIFTS // 2

    def cos_of(m):
        return np.cos(2 * np.pi * (m % PATCH) / PATCH)

    def sin_of(m):
        return np.sin(2 * np.pi * (m % PATCH) / PATCH)

    c, s = cos_of(np.outer(k, k)), sin_of(np.outer(k, k))
    gc, gs = cos_of(np.outer(u, k)), sin_of(np.outer(u, k))
    factor = np.where(k[:64] == 0, 1.0, 2.0)
    first = []
    for count, shift, slot in ((4, 16, 0), (2, 0, 0), (2, 96, 2)):
        table = np.zeros((128 * count + 16, 256))
        for i in range(count):
            rows = slice(32 * i + shift, 32 * i + shift + 128)
            table[i : 64 * count : count, rows] = c[:64]
            table[64 * count + i : 128 * count : count, rows] = -s[:64]
            table[128 * count + slot + i, rows] = (-1.0) ** k
        first.append(table)
    second = np.block([[c, -s], [s, c]])
    back_second = np.zeros((1024, 256))
    for w in range(4):
        rows, lanes = 256 * w, 32 * w
        back_second[rows : rows + 128, lanes : lanes + 32] = gc.T
        back_second[rows + 128 : rows + 256, lanes : lanes + 32] = -gs.T
        back_second[rows : rows + 128, 128 + lanes : 160 + lanes] = gs.T
        back_second[rows + 128 : rows + 256, 128 + lanes : 160 + lanes] = gc.T
    inner, outer = np.zeros((128, 512)), np.zeros((128, 512))
    for i in range(4):
        inner[i::4, i:256:4] = factor * gc[:, :64]
        inner[i::4, 256 + i : 512 : 4] = -factor * gs[:, :64]
        start = 128 * (i // 2) + i % 2
        outer[i::4, start : 128 * (i // 2) + 128 : 2] = factor * gc[:, :64]
        outer[i::4, 256 + start : 384 + 128 * (i // 2) : 2] = -factor * gs[:, :64]
    energy_cols = np.zeros((384, 128))
    for jj in range(4):
        energy_cols[128 + 32 * jj - HALO : 256 + 32 * jj - HALO, 32 * jj : 32 * jj + 32] = 1.0
    sums = np.zeros((256, 256))
    for lane in range(128):
        jj, comp = lane % 4, (lane // 32) % 2
        sums[32 * jj : 32 * jj + 32, lane] = 1.0
        if comp == 0:
            sums[128 + 32 * jj : 160 + 32 * jj, 128 + lane] = 1.0
        else:
            sums[32 * jj : 32 * jj + 32, 128 + lane] = u
    tables = {
        "inner": first[0], "upper": first[1], "lower": first[2], "second": second, "back_second": back_second,
        "back_first": np.concatenate([inner, outer], axis=0), "energy_cols": energy_cols, "sums": sums,
    }
    places, pieces, base = {}, [], 0
    for name, table in tables.items():
        rows, tiles = table.shape[0], table.shape[1] // 128
        places[name] = (base, rows, tiles)
        pieces += [table[:, 128 * t : 128 * t + 128] for t in range(tiles)]
        base += rows * tiles
    packed = np.concatenate(pieces, axis=0).astype(np.float32).astype(ml_dtypes.bfloat16)
    return places, packed


PLACES, PACKED = build_tables()


class Table:
    def __init__(self, ref, name):
        self.ref = ref
        self.base, self.rows, self.tiles = PLACES[name]

    def read(self, rows=None, tiles=None):
        rows = rows or slice(0, self.rows)
        tiles = range(self.tiles) if tiles is None else tiles
        starts = [self.base + t * self.rows for t in tiles]
        parts = [self.ref[b + rows.start : b + rows.stop, :] for b in starts]
        return parts[0] if len(parts) == 1 else jnp.concatenate(parts, axis=1)

    def read_part(self, part, rows):
        starts = [self.base + t * self.rows for t in range(self.tiles)]
        parts = [self.ref[pl.ds(pl.multiple_of(b + part * rows, 16), rows), :] for b in starts]
        return jnp.concatenate(parts, axis=1)


def mm(a, b):
    return jnp.dot(a, b, preferred_element_type=F32)


def split3(x):
    hi = x.astype(BF16)
    rest = x - hi.astype(F32)
    mid = rest.astype(BF16)
    low = (rest - mid.astype(F32)).astype(BF16)
    return jnp.concatenate([hi, mid, low], axis=0)


def mm_exact(x, w):
    n = x.shape[0]
    y = mm(split3(x), w)
    return y[:n] + y[n : 2 * n] + y[2 * n :]


def block_energies(s, blocks, lanes, pad, eb):
    for b in blocks:
        x = pad[s, 32 * b : 32 * b + 32, lanes].astype(F32)
        eb[s, b : b + 1, lanes] = jnp.sum(x * x, axis=0, keepdims=True)


def node_energies(s, columns, eb, en, energy_cols):
    e4 = eb[s, 0:8, :] + eb[s, 1:9, :] + eb[s, 2:10, :] + eb[s, 3:11, :]
    tiles = [e4[:, 128 * t : 128 * t + 128] for t in range(5)]
    rows = [jnp.concatenate([tiles[(q - 1) % 5], tiles[q], tiles[q + 1]], axis=1) for q in columns]
    y = mm_exact(jnp.concatenate(rows, axis=0), energy_cols.read())
    row = lax.broadcasted_iota(jnp.int32, (8, 128), 0)
    for n, q in enumerate(columns):
        e = y[8 * n : 8 * n + 8] * (1.0 / PATCH**2) + EPS
        en[s, INNER, q] = jnp.where(row < 4, pltpu.roll(e, 6, 0), pltpu.roll(e, 2, 0))
        en[s, OUTER, q] = jnp.where((row < 2) | (row >= 6), e, pltpu.roll(e, 4, 0))


INNER, OUTER = 0, 1
OWN_COLS, SIDE_COLS = (slice(0, 256), slice(256, 512)), (slice(512, 640),)


def first_transform(s, group, columns, pad, spec, tables):
    for lanes in columns:
        if group == INNER:
            parts = [(0, 256, mm(tables["inner"].read(), pad[s, HALO : HALO + 256, lanes]))]
        else:
            parts = [
                (0, 128, mm(tables["upper"].read(), pad[s, 0:256, lanes])),
                (128, 128, mm(tables["lower"].read(), pad[s, 96:352, lanes])),
            ]
        for n in range((lanes.stop - lanes.start) // 128):
            t = (lanes.start // 128 + n + 1) % 5
            cols = slice(128 * n, 128 * n + 128)
            last = None
            for row, count, y in parts:
                spec[s, group, t, 0, row : row + count, :] = y[0:count, cols].astype(BF16)
                spec[s, group, t, 1, row : row + count, :] = y[count : 2 * count, cols].astype(BF16)
                end = y[2 * count : 2 * count + 16, cols]
                last = end if last is None else last + end
            spec[s, group, t, 0, 256:272, :] = last.astype(BF16)
            spec[s, group, t, 1, 256:272, :] = jnp.zeros((16, 128), BF16)


def window(s, group, q, w, spec):
    start = 32 * w - HALO
    before = lax.rem(q + (1 if start >= 0 else 0), 5)
    after = lax.rem(before + 1, 5)
    lane = lax.broadcasted_iota(jnp.int32, (272, 128), 1)
    parts = []
    for part in range(2):
        parts.append(jnp.where(lane < start % 128, spec[s, group, after, part], spec[s, group, before, part]))
    return jnp.concatenate(parts, axis=1)


def cross(x0, x1):
    ar, ai, br, bi = x0[:, :128], x0[:, 128:], x1[:, :128], x1[:, 128:]
    return jnp.concatenate([(ar * br + ai * bi).astype(BF16), (ar * bi - ai * br).astype(BF16)], axis=1)


def unit_of(n):
    m = lax.rem(n, 4)
    return n // 8, lax.rem(n // 4, 2), lax.rem(m + 1, 3) + 2 * (m // 3)


def cross_unit(pair, n, spec, kept, crossed, tables):
    _, group, q = unit_of(n)
    for w in range(4):
        x1 = mm(window(pair + 1, group, q, w, spec), tables["second"].read())
        if pair == 0:
            x0 = mm(window(0, group, q, w, spec), tables["second"].read())
            kept[group, q, w] = x1.astype(BF16)
        else:
            x0 = kept[group, q, w].astype(F32)
        crossed[:, 256 * w : 256 * w + 256] = cross(x0, x1)


def columns_back(crossed, turned, last_row, tables):
    back = mm(crossed[...], tables["back_second"].read())
    turned[0:256, :] = back[0:256, :128].astype(BF16)
    turned[256:512, :] = back[0:256, 128:].astype(BF16)
    last = back[256:264, 0:128]
    low = lax.broadcasted_iota(jnp.int32, (8, 128), 0) < 4
    last_row[...] = jnp.where(low, last, -pltpu.roll(last, 4, 0))


def rows_back(n, turned, last_row, en, unit_sums, tables):
    pair, group, q = unit_of(n)
    corr = mm(tables["back_first"].read_part(group, 128), turned[...])
    low = lax.broadcasted_iota(jnp.int32, (8, 128), 0) < 4
    scale = (PATCH / 2.0 / PATCH**4) * lax.rsqrt(en[pair, group, q] * en[pair + 1, group, q])
    last = last_row[...]
    total = jnp.zeros((8, 128), F32)
    along = jnp.zeros((8, 128), F32)
    for u in range(0, SHIFTS, 2):
        weight = jnp.exp((corr[4 * u : 4 * u + 8] + last) * scale)
        total += weight
        along += weight * jnp.where(low, float(u - SHIFTS // 2), float(u + 1 - SHIFTS // 2))
    unit_sums[n, :, 0:128] = total + pltpu.roll(total, 4, 0)
    unit_sums[n, :, 128:256] = along + pltpu.roll(along, 4, 0)


def flow_block(unit_sums, sums, last_sec):
    row = lax.broadcasted_iota(jnp.int32, (8, 256), 0)
    pieces = []
    for pair in range(2):
        for q in range(4):
            m = (2, 0, 1, 3)[q]
            inner, outer = unit_sums[8 * pair + m], unit_sums[8 * pair + 4 + m]
            pieces.append(jnp.where((row >= 2) & (row < 6), pltpu.roll(inner, 2, 0), outer))
    y = mm_exact(jnp.concatenate(pieces, axis=0), sums.read())
    flow = y[:, 128:] / y[:, :128]
    lane = lax.broadcasted_iota(jnp.int32, (8, 128), 1)
    block = jnp.zeros((8, 128), F32)
    for pair in range(2):
        for q in range(4):
            first = 8 + 4 * q
            mine = (lane // 64 == pair) & (lane % 32 >= first) & (lane % 32 < first + 4)
            r = 32 * pair + 8 * q
            block = jnp.where(mine, flow[r : r + 8], block)
    return jnp.where((lane >= 64) & last_sec, 0.0, block)


def extend(own, left, right):
    lane = lax.broadcasted_iota(jnp.int32, own.shape, own.ndim - 1) % 32
    from_left = pltpu.roll(left, 112, own.ndim - 1)
    from_right = pltpu.roll(right, 16, own.ndim - 1)
    return jnp.where(lane < 8, from_left, jnp.where(lane >= 24, from_right, own))


def relax(flow, row_pos, col_pos):
    shape = flow[0].shape
    row = lax.broadcasted_iota(jnp.int32, shape, 0)
    lane = lax.broadcasted_iota(jnp.int32, shape, 1)
    node = lane % 32
    inside = ((row >= 8) | (row_pos > 0)) & ((row < 16) | (row_pos < TILE_GRID - 1))
    inside &= ((node >= 8) | (col_pos > 0)) & ((node < 24) | (col_pos < TILE_GRID - 1))
    mask = jnp.where(inside, 1.0, 0.0)
    low = lane < 64
    count = len(flow)
    zero = jnp.zeros(shape, F32)

    def beside_sections(f):
        turned = [zero] + [pltpu.roll(x, 64, 1) for x in f] + [zero]
        later = [jnp.where(low, turned[d + 1], turned[d + 2]) for d in range(count)]
        earlier = [jnp.where(low, turned[d], turned[d + 1]) for d in range(count)]
        return later, earlier

    flow = [f * mask for f in flow]
    before = beside_sections(flow)[1]
    pull = [(STEP_RATE * mask) * (f - p) for f, p in zip(flow, before)]
    mesh = pull
    rate = STEP_RATE * mask
    for step in range(1, ITERS):
        later, earlier = beside_sections(mesh)
        updated = []
        for d, m in enumerate(mesh):
            own = 6.0 if d > 0 else jnp.where(low, 5.0, 6.0)
            around = pltpu.roll(m, 1, 0) + pltpu.roll(m, 23, 0) + pltpu.roll(m, 1, 1) + pltpu.roll(m, 127, 1)
            updated.append(m - rate * (own * m - later[d] - earlier[d] - around) + pull[d])
        mesh = updated
    return mesh


SHIFT_ROWS = 288


def shifted_columns(pad, cols):
    @pl.loop(0, SHIFT_ROWS // 16)
    def _(k):
        for s in range(2):
            x = pad[s, pl.ds(pl.multiple_of(32 + 16 * k, 16), 16), :].astype(F32)
            for d in range(5):
                y = x if d == 2 else pltpu.roll(x, (2 - d) % LANES, 1)
                for t in range(4):
                    cols[d, pl.ds(128 * k + (4 * s + t), 16, stride=8), :] = y[:, 128 * t : 128 * t + 128]


def pick_pair(high, odd, values):
    near = [jnp.where(high, values[k + 2], values[k]) for k in range(3)]
    return jnp.where(odd, near[1], near[0]), jnp.where(odd, near[2], near[1])


def corners(r, offsets, cols, coef):
    base = pl.multiple_of(8 * r, 8)
    view = []
    for k in range(12):
        rows = pl.ds(pl.multiple_of(8 * (base + 14 + k), 8), 8)
        view.append([cols[d, rows, :] for d in range(5)])
    for k in range(8):
        ro, co = offsets[0, base + k], offsets[1, base + k]
        row_high, row_odd = ro >= 0, (ro & 1) == 1
        col_high, col_odd = co >= 0, (co & 1) == 1
        pairs = [pick_pair(col_high, col_odd, view[k + dr]) for dr in range(5)]
        i00, i10 = pick_pair(row_high, row_odd, [p[0] for p in pairs])
        i01, i11 = pick_pair(row_high, row_odd, [p[1] for p in pairs])
        rf, cf = ro.astype(F32), co.astype(F32)
        top, low = i01 - i00, i11 - i10
        top0, low0 = i00 - cf * top, i10 - cf * low
        twist, lean = low - top, low0 - top0
        coef[0, base + k] = top0 - rf * lean
        coef[1, base + k] = lean
        coef[2, base + k] = top - rf * twist
        coef[3, base + k] = twist


def write_mesh(mesh, out):
    for s in range(2):
        for c in range(2):
            lane = 64 * s + 32 * c + 8
            out[s, c, 0] = mesh[:, lane : lane + 16]


def spread_lanes(mesh, i, c):
    tile = lax.broadcasted_iota(jnp.int32, (8, 128), 0)
    lane = lax.broadcasted_iota(jnp.int32, (8, 128), 1)
    place = 64 * (tile // 4) + 4 * (tile % 4) + lane // 32 + (32 * c + 8)
    return jnp.take_along_axis(jnp.broadcast_to(mesh[i : i + 1], (8, 128)), place, axis=1)


MESH = pl.DeviceIdType.MESH
AROUND = [(0, -1), (0, 1), (-1, 0), (1, 0), (-1, -1), (-1, 1), (1, -1), (1, 1)]


def pixel_part(dr, dc, sections, pad, from_left, from_right, src, dst):
    src_rows = {-1: pl.ds(0, HALO), 0: pl.ds(0, 256), 1: pl.ds(256 - HALO, HALO)}[dr]
    dst_rows = {-1: pl.ds(HALO + 256, HALO), 0: pl.ds(HALO, 256), 1: pl.ds(0, HALO)}[dr]
    if dc == 0:
        return sections.at[src, 0, src_rows, :], pad.at[dst, dst_rows, pl.ds(0, OWN_LANES)]
    if dc < 0:
        return sections.at[src, 0, src_rows, pl.ds(0, 128)], from_right.at[dst, dst_rows, :]
    return sections.at[src, 0, src_rows, pl.ds(OWN_LANES - 128, 128)], from_left.at[dst, dst_rows, :]


def merge_sides(s, rows, pad, from_left, from_right, col_pos):
    lane = lax.broadcasted_iota(jnp.int32, (rows.stop - rows.start, 128), 1)
    side = jnp.where(lane < 64, from_right[s, rows, :].astype(F32), from_left[s, rows, :].astype(F32))
    keep = ((lane < 64) & (col_pos < TILE_GRID - 1)) | ((lane >= 64) & (col_pos > 0))
    pad[s, rows, OWN_LANES:LANES] = jnp.where(keep, side, 0.0).astype(BF16)


def clear_edges(s, pad, row_pos):
    @pl.when(row_pos == 0)
    def _():
        pad[s, 0:HALO, :] = jnp.zeros((HALO, LANES), BF16)

    @pl.when(row_pos == TILE_GRID - 1)
    def _():
        pad[s, ROWS - HALO : ROWS, :] = jnp.zeros((HALO, LANES), BF16)


def pixel_forward(dr, dc, pad, from_left, from_right):
    src_rows = {-1: pl.ds(HALO, HALO), 0: pl.ds(HALO, 256), 1: pl.ds(256, HALO)}[dr]
    dst_rows = {-1: pl.ds(HALO + 256, HALO), 0: pl.ds(HALO, 256), 1: pl.ds(0, HALO)}[dr]
    if dc == 0:
        return pad.at[2, src_rows, pl.ds(0, OWN_LANES)], pad.at[2, dst_rows, pl.ds(0, OWN_LANES)]
    if dc < 0:
        return pad.at[2, src_rows, pl.ds(0, 128)], from_right.at[2, dst_rows, :]
    return pad.at[2, src_rows, pl.ds(OWN_LANES - 128, 128)], from_left.at[2, dst_rows, :]


def flow_kernel(sections, offsets_in, packed_in, coef, block_out,
                pad, from_left, from_right, offsets, packed, spec, kept, crossed, turned, last_row, eb, en, unit_sums, flows, cols,
                local_sem, pixel_send, pixel_recv, flow_send, flow_recv):
    tables = {name: Table(packed, name) for name in PLACES}
    sec, tile = lax.axis_index("sec"), lax.axis_index("tile")
    sec_count = lax.axis_size("sec")
    row_pos, col_pos = tile // TILE_GRID, tile % TILE_GRID

    def device(ds, dr, dc):
        row = lax.rem(row_pos + (dr + TILE_GRID), TILE_GRID)
        col = lax.rem(col_pos + (dc + TILE_GRID), TILE_GRID)
        return (lax.rem(sec + ds, sec_count), row * TILE_GRID + col)

    barrier = pltpu.get_barrier_semaphore()
    partners = [
        (ds, dr, dc) for ds in range(4) for dr, dc in AROUND + [(0, 0)]
        if (ds, dr, dc) != (0, 0, 0) and not (ds == 2 and dr * dc != 0)
    ]
    for p in partners:
        pl.semaphore_signal(barrier, inc=1, device_id=device(*p), device_id_type=MESH)
    own_copy = pltpu.make_async_copy(
        sections.at[:, 0], pad.at[pl.ds(0, 2), pl.ds(HALO, 256), pl.ds(0, OWN_LANES)], local_sem.at[0]
    )
    offset_copies = [
        pltpu.make_async_copy(
            offsets_in.at[c, s, 0, :, pl.ds(128 * t, 128)],
            offsets.at[c, :, 4 * s + t, :],
            local_sem.at[2 + 8 * c + 4 * s + t],
        )
        for c in range(2) for s in range(2) for t in range(4)
    ]
    table_copy = pltpu.make_async_copy(packed_in, packed, local_sem.at[1])
    own_copy.start()
    table_copy.start()
    for copy in offset_copies:
        copy.start()
    pl.semaphore_wait(barrier, len(partners))

    def pixel_copy(k, ds, dr, dc, refs):
        return pltpu.make_async_remote_copy(
            src_ref=refs[0], dst_ref=refs[1], send_sem=pixel_send.at[k], recv_sem=pixel_recv.at[k],
            device_id=device(ds, dr, dc), device_id_type=MESH,
        )

    both = pl.ds(0, 2)
    own = [
        pixel_copy(k, 0, dr, dc, pixel_part(dr, dc, sections, pad, from_left, from_right, both, both))
        for k, (dr, dc) in enumerate(AROUND)
    ]
    after = pixel_copy(
        8, 3, 0, 0, pixel_part(0, 0, sections, pad, from_left, from_right, pl.ds(0, 1), pl.ds(2, 1))
    )
    for copy in own + [after]:
        copy.start()

    def transform(s, group, columns):
        first_transform(s, group, columns, pad, spec, tables)

    def energies(s, blocks, lanes, columns):
        block_energies(s, blocks, lanes, pad, eb)
        node_energies(s, columns, eb, en, tables["energy_cols"])

    def units(pair, first, count):
        @pl.loop(0, count)
        def _(k):
            n = first + k
            rows_back(n - 2, turned, last_row, en, unit_sums, tables)
            columns_back(crossed, turned, last_row, tables)
            cross_unit(pair, n, spec, kept, crossed, tables)

    inner_blocks, outer_blocks = range(2, 9), (0, 1, 9, 10)
    own_lanes, side_lanes, all_lanes = slice(0, OWN_LANES), slice(OWN_LANES, LANES), slice(0, LANES)

    def inner_own(s):
        transform(s, INNER, OWN_COLS)
        energies(s, inner_blocks, own_lanes, (1, 2))

    def inner_sides(s):
        merge_sides(s, slice(HALO, HALO + 256), pad, from_left, from_right, col_pos)
        transform(s, INNER, SIDE_COLS)
        energies(s, inner_blocks, side_lanes, (0, 3))

    def outer(s):
        merge_sides(s, slice(0, HALO), pad, from_left, from_right, col_pos)
        merge_sides(s, slice(HALO + 256, ROWS), pad, from_left, from_right, col_pos)
        clear_edges(s, pad, row_pos)
        transform(s, OUTER, OWN_COLS + SIDE_COLS)
        energies(s, outer_blocks, all_lanes, (0, 1, 2, 3))

    def corner_rows(first, count):
        @pl.loop(0, count)
        def _(k):
            corners(first + k, offsets, cols, coef)

    eb[...] = jnp.zeros(eb.shape, F32)
    for slot in (0, 2, 6, 8):
        flows[slot, lax.rem(sec + 2, sec_count)] = jnp.zeros((8, 128), F32)
    own_copy.wait()
    table_copy.wait()
    pl.loop(0, 2)(inner_own)
    cross_unit(0, 0, spec, kept, crossed, tables)
    columns_back(crossed, turned, last_row, tables)
    cross_unit(0, 1, spec, kept, crossed, tables)
    own[0].wait_recv()
    own[1].wait_recv()
    pl.loop(0, 2)(inner_sides)
    units(0, 2, 2)
    for copy in own[2:]:
        copy.wait_recv()
    pl.loop(0, 2)(outer)
    units(0, 4, 2)
    after.wait_recv()
    forward = [
        pixel_copy(9 + k, 0, dr, dc, pixel_forward(dr, dc, pad, from_left, from_right))
        for k, (dr, dc) in enumerate(AROUND)
    ]
    for copy in forward:
        copy.start()
    units(0, 6, 2)
    inner_own(2)
    units(1, 8, 2)
    forward[0].wait_recv()
    forward[1].wait_recv()
    inner_sides(2)
    units(1, 10, 2)
    for copy in forward[2:]:
        copy.wait_recv()
    outer(2)
    units(1, 12, 4)
    rows_back(14, turned, last_row, en, unit_sums, tables)
    columns_back(crossed, turned, last_row, tables)
    rows_back(15, turned, last_row, en, unit_sums, tables)

    flows[4, sec] = flow_block(unit_sums, tables["sums"], sec == sec_count - 1)
    share = [
        pltpu.make_async_remote_copy(
            src_ref=flows.at[4, sec], dst_ref=flows.at[3 * (1 - dr) + 1 - dc, sec], send_sem=flow_send.at[k],
            recv_sem=flow_recv.at[k], device_id=device(ds, dr, dc), device_id_type=MESH,
        )
        for k, (ds, dr, dc) in enumerate(partners)
    ]
    for copy in share:
        copy.start()
    for copy in offset_copies:
        copy.wait()
    shifted_columns(pad, cols)
    corner_rows(0, 32)
    for copy in own + [after] + forward + share:
        copy.wait_send()
    for copy in share:
        copy.wait_recv()

    def column(d, c):
        return jnp.concatenate([flows[c, d], flows[3 + c, d], flows[6 + c, d]], axis=0)

    mesh = relax([extend(column(d, 1), column(d, 0), column(d, 2)) for d in range(4)], row_pos, col_pos)
    mine = mesh[0][8:16]
    for d in range(1, 4):
        mine = jnp.where(sec == d, mesh[d][8:16], mine)
    block_out[...] = mine


def blend_kernel(coef, block, mesh_out, warped, result, sem):
    mesh = block[...]
    write_mesh(mesh, mesh_out)
    copies = []
    for i in range(8):
        a, b = spread_lanes(mesh, i, 0), spread_lanes(mesh, i, 1)
        for k in range(32):
            r = 32 * i + k
            first = coef[0, r] + a * coef[1, r]
            second = coef[2, r] + a * coef[3, r]
            result[r] = first + b * second
        if i % 2 == 1:
            rows = pl.ds(32 * i - 32, 64)
            for s in range(2):
                for t in range(4):
                    copy = pltpu.make_async_copy(
                        result.at[rows, 4 * s + t, :], warped.at[s, 0, rows, pl.ds(128 * t, 128)], sem.at[len(copies)]
                    )
                    copy.start()
                    copies.append(copy)
    for copy in copies:
        copy.wait()


def vmem():
    return pl.BlockSpec(memory_space=pltpu.VMEM)


def shards(sections, corner_offsets):
    anywhere = pl.BlockSpec(memory_space=pl.ANY)
    dma = pltpu.SemaphoreType.DMA
    coef, block = pl.pallas_call(
        flow_kernel,
        out_shape=(pltpu.VMEM((4, 256, 8, 128), F32), pltpu.VMEM((8, 128), F32)),
        in_specs=[anywhere, anywhere, anywhere],
        out_specs=(vmem(), vmem()),
        scratch_shapes=[
            pltpu.VMEM((3, ROWS, LANES), BF16),
            pltpu.VMEM((3, ROWS, 128), BF16),
            pltpu.VMEM((3, ROWS, 128), BF16),
            pltpu.VMEM((2, 256, 8, 128), jnp.int32),
            pltpu.VMEM(PACKED.shape, BF16),
            pltpu.VMEM((3, 2, 5, 2, 272, 128), BF16),
            pltpu.VMEM((2, 4, 4, 272, 256), BF16),
            pltpu.VMEM((272, 1024), BF16),
            pltpu.VMEM((512, 128), BF16),
            pltpu.VMEM((8, 128), F32),
            pltpu.VMEM((3, 16, LANES), F32),
            pltpu.VMEM((3, 2, 4, 8, 128), F32),
            pltpu.VMEM((16, 8, 256), F32),
            pltpu.VMEM((9, 4, 8, 128), F32),
            pltpu.VMEM((5, 8 * SHIFT_ROWS, 128), F32),
            dma((18,)),
            dma((17,)),
            dma((17,)),
            dma((31,)),
            dma((31,)),
        ],
        compiler_params=pltpu.CompilerParams(
            vmem_limit_bytes=58 * 2**20, collective_id=0, has_side_effects=True
        ),
    )(sections, corner_offsets, jnp.asarray(PACKED))
    return pl.pallas_call(
        blend_kernel,
        out_shape=(
            jax.ShapeDtypeStruct((2, 2, 1, 8, 16), F32),
            jax.ShapeDtypeStruct((2, 1, 256, 512), F32),
        ),
        in_specs=[vmem(), vmem()],
        out_specs=(vmem(), anywhere),
        scratch_shapes=[pltpu.VMEM((256, 8, 128), F32), dma((32,))],
        compiler_params=pltpu.CompilerParams(vmem_limit_bytes=20 * 2**20),
    )(coef, block)


def solution(mesh):
    in_specs = (P("sec", "tile", None, None), P(None, "sec", "tile", None, None))
    out_specs = (P("sec", None, "tile", None, None), P("sec", "tile", None, None))
    return jax.shard_map(shards, mesh=mesh, in_specs=in_specs, out_specs=out_specs, check_vma=False)
```

```python
import functools
import math

import jax
import jax.numpy as jnp
import ml_dtypes
import numpy as np
from jax import lax
from jax.experimental import pallas as pl
from jax.experimental.pallas import tpu as pltpu
from jax.sharding import PartitionSpec as P

TILE_GRID = 8
PATCH = 128
STRIDE = 32
SHIFTS = 32
ITERS = 4
HALO = 48
EPS = 1e-05
STEP_RATE = 0.15
ROWS = 352
LANES = 640
OWN_LANES = 512
F32 = jnp.float32
BF16 = jnp.bfloat16


def build_tables():
    k = np.arange(PATCH)
    u = np.arange(SHIFTS) - SHIFTS // 2

    def cos_of(m):
        return np.cos(2 * np.pi * (m % PATCH) / PATCH)

    def sin_of(m):
        return np.sin(2 * np.pi * (m % PATCH) / PATCH)

    c, s = cos_of(np.outer(k, k)), sin_of(np.outer(k, k))
    gc, gs = cos_of(np.outer(u, k)), sin_of(np.outer(u, k))
    factor = np.where(k[:64] == 0, 1.0, 2.0)
    first = []
    for count, shift, slot in ((4, 16, 0), (2, 0, 0), (2, 96, 2)):
        table = np.zeros((128 * count + 16, 256))
        for i in range(count):
            rows = slice(32 * i + shift, 32 * i + shift + 128)
            table[i : 64 * count : count, rows] = c[:64]
            table[64 * count + i : 128 * count : count, rows] = -s[:64]
            table[128 * count + slot + i, rows] = (-1.0) ** k
        first.append(table)
    second = np.block([[c, -s], [s, c]])
    back_second = np.zeros((1024, 256))
    for w in range(4):
        rows, lanes = 256 * w, 32 * w
        back_second[rows : rows + 128, lanes : lanes + 32] = gc.T
        back_second[rows + 128 : rows + 256, lanes : lanes + 32] = -gs.T
        back_second[rows : rows + 128, 128 + lanes : 160 + lanes] = gs.T
        back_second[rows + 128 : rows + 256, 128 + lanes : 160 + lanes] = gc.T
    inner, outer = np.zeros((128, 512)), np.zeros((128, 512))
    for i in range(4):
        inner[i::4, i:256:4] = factor * gc[:, :64]
        inner[i::4, 256 + i : 512 : 4] = -factor * gs[:, :64]
        start = 128 * (i // 2) + i % 2
        outer[i::4, start : 128 * (i // 2) + 128 : 2] = factor * gc[:, :64]
        outer[i::4, 256 + start : 384 + 128 * (i // 2) : 2] = -factor * gs[:, :64]
    energy_cols = np.zeros((384, 128))
    for jj in range(4):
        energy_cols[128 + 32 * jj - HALO : 256 + 32 * jj - HALO, 32 * jj : 32 * jj + 32] = 1.0
    sums = np.zeros((256, 256))
    for lane in range(128):
        jj, comp = lane % 4, (lane // 32) % 2
        sums[32 * jj : 32 * jj + 32, lane] = 1.0
        if comp == 0:
            sums[128 + 32 * jj : 160 + 32 * jj, 128 + lane] = 1.0
        else:
            sums[32 * jj : 32 * jj + 32, 128 + lane] = u
    tables = {
        "inner": first[0], "upper": first[1], "lower": first[2], "second": second, "back_second": back_second,
        "back_first": np.concatenate([inner, outer], axis=0), "energy_cols": energy_cols, "sums": sums,
    }
    places, pieces, base = {}, [], 0
    for name, table in tables.items():
        rows, tiles = table.shape[0], table.shape[1] // 128
        places[name] = (base, rows, tiles)
        pieces += [table[:, 128 * t : 128 * t + 128] for t in range(tiles)]
        base += rows * tiles
    packed = np.concatenate(pieces, axis=0).astype(np.float32).astype(ml_dtypes.bfloat16)
    return places, packed


PLACES, PACKED = build_tables()


class Table:
    def __init__(self, ref, name):
        self.ref = ref
        self.base, self.rows, self.tiles = PLACES[name]

    def read(self, rows=None, tiles=None):
        rows = rows or slice(0, self.rows)
        tiles = range(self.tiles) if tiles is None else tiles
        starts = [self.base + t * self.rows for t in tiles]
        parts = [self.ref[b + rows.start : b + rows.stop, :] for b in starts]
        return parts[0] if len(parts) == 1 else jnp.concatenate(parts, axis=1)

    def read_part(self, part, rows):
        starts = [self.base + t * self.rows for t in range(self.tiles)]
        parts = [self.ref[pl.ds(pl.multiple_of(b + part * rows, 16), rows), :] for b in starts]
        return jnp.concatenate(parts, axis=1)


def mm(a, b):
    return jnp.dot(a, b, preferred_element_type=F32)


def split3(x):
    hi = x.astype(BF16)
    rest = x - hi.astype(F32)
    mid = rest.astype(BF16)
    low = (rest - mid.astype(F32)).astype(BF16)
    return jnp.concatenate([hi, mid, low], axis=0)


def mm_exact(x, w):
    n = x.shape[0]
    y = mm(split3(x), w)
    return y[:n] + y[n : 2 * n] + y[2 * n :]


def block_energies(s, blocks, lanes, pad, eb):
    for b in blocks:
        x = pad[s, 32 * b : 32 * b + 32, lanes].astype(F32)
        eb[s, b : b + 1, lanes] = jnp.sum(x * x, axis=0, keepdims=True)


def node_energies(s, columns, eb, en, energy_cols):
    e4 = eb[s, 0:8, :] + eb[s, 1:9, :] + eb[s, 2:10, :] + eb[s, 3:11, :]
    tiles = [e4[:, 128 * t : 128 * t + 128] for t in range(5)]
    rows = [jnp.concatenate([tiles[(q - 1) % 5], tiles[q], tiles[q + 1]], axis=1) for q in columns]
    y = mm_exact(jnp.concatenate(rows, axis=0), energy_cols.read())
    row = lax.broadcasted_iota(jnp.int32, (8, 128), 0)
    for n, q in enumerate(columns):
        e = y[8 * n : 8 * n + 8] * (1.0 / PATCH**2) + EPS
        en[s, INNER, q] = jnp.where(row < 4, pltpu.roll(e, 6, 0), pltpu.roll(e, 2, 0))
        en[s, OUTER, q] = jnp.where((row < 2) | (row >= 6), e, pltpu.roll(e, 4, 0))


INNER, OUTER = 0, 1
OWN_COLS, SIDE_COLS = (slice(0, 256), slice(256, 512)), (slice(512, 640),)


def first_transform(s, group, columns, pad, spec, tables):
    for lanes in columns:
        if group == INNER:
            parts = [(0, 256, mm(tables["inner"].read(), pad[s, HALO : HALO + 256, lanes]))]
        else:
            parts = [
                (0, 128, mm(tables["upper"].read(), pad[s, 0:256, lanes])),
                (128, 128, mm(tables["lower"].read(), pad[s, 96:352, lanes])),
            ]
        for n in range((lanes.stop - lanes.start) // 128):
            t = (lanes.start // 128 + n + 1) % 5
            cols = slice(128 * n, 128 * n + 128)
            last = None
            for row, count, y in parts:
                spec[s, group, t, 0, row : row + count, :] = y[0:count, cols].astype(BF16)
                spec[s, group, t, 1, row : row + count, :] = y[count : 2 * count, cols].astype(BF16)
                end = y[2 * count : 2 * count + 16, cols]
                last = end if last is None else last + end
            spec[s, group, t, 0, 256:272, :] = last.astype(BF16)
            spec[s, group, t, 1, 256:272, :] = jnp.zeros((16, 128), BF16)


def window(s, group, q, w, spec):
    start = 32 * w - HALO
    before = lax.rem(q + (1 if start >= 0 else 0), 5)
    after = lax.rem(before + 1, 5)
    lane = lax.broadcasted_iota(jnp.int32, (272, 128), 1)
    parts = []
    for part in range(2):
        parts.append(jnp.where(lane < start % 128, spec[s, group, after, part], spec[s, group, before, part]))
    return jnp.concatenate(parts, axis=1)


def cross(x0, x1):
    ar, ai, br, bi = x0[:, :128], x0[:, 128:], x1[:, :128], x1[:, 128:]
    return jnp.concatenate([(ar * br + ai * bi).astype(BF16), (ar * bi - ai * br).astype(BF16)], axis=1)


def unit_of(n):
    m = lax.rem(n, 4)
    return n // 8, lax.rem(n // 4, 2), lax.rem(m + 1, 3) + 2 * (m // 3)


def cross_unit(pair, n, spec, kept, crossed, tables):
    _, group, q = unit_of(n)
    for w in range(4):
        x1 = mm(window(pair + 1, group, q, w, spec), tables["second"].read())
        if pair == 0:
            x0 = mm(window(0, group, q, w, spec), tables["second"].read())
            kept[group, q, w] = x1.astype(BF16)
        else:
            x0 = kept[group, q, w].astype(F32)
        crossed[:, 256 * w : 256 * w + 256] = cross(x0, x1)


def columns_back(crossed, turned, last_row, tables):
    back = mm(crossed[...], tables["back_second"].read())
    turned[0:256, :] = back[0:256, :128].astype(BF16)
    turned[256:512, :] = back[0:256, 128:].astype(BF16)
    last = back[256:264, 0:128]
    low = lax.broadcasted_iota(jnp.int32, (8, 128), 0) < 4
    last_row[...] = jnp.where(low, last, -pltpu.roll(last, 4, 0))


def rows_back(n, turned, last_row, en, unit_sums, tables):
    pair, group, q = unit_of(n)
    corr = mm(tables["back_first"].read_part(group, 128), turned[...])
    low = lax.broadcasted_iota(jnp.int32, (8, 128), 0) < 4
    scale = (PATCH / 2.0 / PATCH**4) * lax.rsqrt(en[pair, group, q] * en[pair + 1, group, q])
    last = last_row[...]
    total = jnp.zeros((8, 128), F32)
    along = jnp.zeros((8, 128), F32)
    for u in range(0, SHIFTS, 2):
        weight = jnp.exp((corr[4 * u : 4 * u + 8] + last) * scale)
        total += weight
        along += weight * jnp.where(low, float(u - SHIFTS // 2), float(u + 1 - SHIFTS // 2))
    unit_sums[n, :, 0:128] = total + pltpu.roll(total, 4, 0)
    unit_sums[n, :, 128:256] = along + pltpu.roll(along, 4, 0)


def flow_block(unit_sums, sums, last_sec):
    row = lax.broadcasted_iota(jnp.int32, (8, 256), 0)
    pieces = []
    for pair in range(2):
        for q in range(4):
            m = (2, 0, 1, 3)[q]
            inner, outer = unit_sums[8 * pair + m], unit_sums[8 * pair + 4 + m]
            pieces.append(jnp.where((row >= 2) & (row < 6), pltpu.roll(inner, 2, 0), outer))
    y = mm_exact(jnp.concatenate(pieces, axis=0), sums.read())
    flow = y[:, 128:] / y[:, :128]
    lane = lax.broadcasted_iota(jnp.int32, (8, 128), 1)
    block = jnp.zeros((8, 128), F32)
    for pair in range(2):
        for q in range(4):
            first = 8 + 4 * q
            mine = (lane // 64 == pair) & (lane % 32 >= first) & (lane % 32 < first + 4)
            r = 32 * pair + 8 * q
            block = jnp.where(mine, flow[r : r + 8], block)
    return jnp.where((lane >= 64) & last_sec, 0.0, block)


def extend(own, left, right):
    lane = lax.broadcasted_iota(jnp.int32, own.shape, own.ndim - 1) % 32
    from_left = pltpu.roll(left, 112, own.ndim - 1)
    from_right = pltpu.roll(right, 16, own.ndim - 1)
    return jnp.where(lane < 8, from_left, jnp.where(lane >= 24, from_right, own))


def relax(flow, row_pos, col_pos):
    shape = flow[0].shape
    row = lax.broadcasted_iota(jnp.int32, shape, 0)
    lane = lax.broadcasted_iota(jnp.int32, shape, 1)
    node = lane % 32
    inside = ((row >= 8) | (row_pos > 0)) & ((row < 16) | (row_pos < TILE_GRID - 1))
    inside &= ((node >= 8) | (col_pos > 0)) & ((node < 24) | (col_pos < TILE_GRID - 1))
    mask = jnp.where(inside, 1.0, 0.0)
    low = lane < 64
    count = len(flow)
    zero = jnp.zeros(shape, F32)

    def beside_sections(f):
        turned = [zero] + [pltpu.roll(x, 64, 1) for x in f] + [zero]
        later = [jnp.where(low, turned[d + 1], turned[d + 2]) for d in range(count)]
        earlier = [jnp.where(low, turned[d], turned[d + 1]) for d in range(count)]
        return later, earlier

    flow = [f * mask for f in flow]
    before = beside_sections(flow)[1]
    pull = [(STEP_RATE * mask) * (f - p) for f, p in zip(flow, before)]
    mesh = pull
    rate = STEP_RATE * mask
    for step in range(1, ITERS):
        later, earlier = beside_sections(mesh)
        updated = []
        for d, m in enumerate(mesh):
            own = 6.0 if d > 0 else jnp.where(low, 5.0, 6.0)
            around = pltpu.roll(m, 1, 0) + pltpu.roll(m, 23, 0) + pltpu.roll(m, 1, 1) + pltpu.roll(m, 127, 1)
            updated.append(m - rate * (own * m - later[d] - earlier[d] - around) + pull[d])
        mesh = updated
    return mesh


SHIFT_ROWS = 288


def shifted_columns(pad, cols):
    @pl.loop(0, SHIFT_ROWS // 16)
    def _(k):
        for s in range(2):
            x = pad[s, pl.ds(pl.multiple_of(32 + 16 * k, 16), 16), :].astype(F32)
            for d in range(5):
                y = x if d == 2 else pltpu.roll(x, (2 - d) % LANES, 1)
                for t in range(4):
                    cols[d, pl.ds(128 * k + (4 * s + t), 16, stride=8), :] = y[:, 128 * t : 128 * t + 128]


def pick_pair(high, odd, values):
    near = [jnp.where(high, values[k + 2], values[k]) for k in range(3)]
    return jnp.where(odd, near[1], near[0]), jnp.where(odd, near[2], near[1])


def corners(r, offsets, cols, coef):
    base = pl.multiple_of(8 * r, 8)
    view = []
    for k in range(12):
        rows = pl.ds(pl.multiple_of(8 * (base + 14 + k), 8), 8)
        view.append([cols[d, rows, :] for d in range(5)])
    for k in range(8):
        ro, co = offsets[0, base + k], offsets[1, base + k]
        row_high, row_odd = ro >= 0, (ro & 1) == 1
        col_high, col_odd = co >= 0, (co & 1) == 1
        pairs = [pick_pair(col_high, col_odd, view[k + dr]) for dr in range(5)]
        i00, i10 = pick_pair(row_high, row_odd, [p[0] for p in pairs])
        i01, i11 = pick_pair(row_high, row_odd, [p[1] for p in pairs])
        rf, cf = ro.astype(F32), co.astype(F32)
        top, low = i01 - i00, i11 - i10
        top0, low0 = i00 - cf * top, i10 - cf * low
        twist, lean = low - top, low0 - top0
        coef[0, base + k] = top0 - rf * lean
        coef[1, base + k] = lean
        coef[2, base + k] = top - rf * twist
        coef[3, base + k] = twist


def write_mesh(mesh, out):
    for s in range(2):
        for c in range(2):
            lane = 64 * s + 32 * c + 8
            out[s, c, 0] = mesh[:, lane : lane + 16]


def spread_lanes(mesh, i, c):
    tile = lax.broadcasted_iota(jnp.int32, (8, 128), 0)
    lane = lax.broadcasted_iota(jnp.int32, (8, 128), 1)
    place = 64 * (tile // 4) + 4 * (tile % 4) + lane // 32 + (32 * c + 8)
    return jnp.take_along_axis(jnp.broadcast_to(mesh[i : i + 1], (8, 128)), place, axis=1)


MESH = pl.DeviceIdType.MESH
AROUND = [(0, -1), (0, 1), (-1, 0), (1, 0), (-1, -1), (-1, 1), (1, -1), (1, 1)]


def pixel_part(dr, dc, sections, pad, from_left, from_right, src, dst):
    src_rows = {-1: pl.ds(0, HALO), 0: pl.ds(0, 256), 1: pl.ds(256 - HALO, HALO)}[dr]
    dst_rows = {-1: pl.ds(HALO + 256, HALO), 0: pl.ds(HALO, 256), 1: pl.ds(0, HALO)}[dr]
    if dc == 0:
        return sections.at[src, 0, src_rows, :], pad.at[dst, dst_rows, pl.ds(0, OWN_LANES)]
    if dc < 0:
        return sections.at[src, 0, src_rows, pl.ds(0, 128)], from_right.at[dst, dst_rows, :]
    return sections.at[src, 0, src_rows, pl.ds(OWN_LANES - 128, 128)], from_left.at[dst, dst_rows, :]


def merge_sides(s, rows, pad, from_left, from_right, col_pos):
    lane = lax.broadcasted_iota(jnp.int32, (rows.stop - rows.start, 128), 1)
    side = jnp.where(lane < 64, from_right[s, rows, :].astype(F32), from_left[s, rows, :].astype(F32))
    keep = ((lane < 64) & (col_pos < TILE_GRID - 1)) | ((lane >= 64) & (col_pos > 0))
    pad[s, rows, OWN_LANES:LANES] = jnp.where(keep, side, 0.0).astype(BF16)


def clear_edges(s, pad, row_pos):
    @pl.when(row_pos == 0)
    def _():
        pad[s, 0:HALO, :] = jnp.zeros((HALO, LANES), BF16)

    @pl.when(row_pos == TILE_GRID - 1)
    def _():
        pad[s, ROWS - HALO : ROWS, :] = jnp.zeros((HALO, LANES), BF16)


def pixel_forward(dr, dc, pad, from_left, from_right):
    src_rows = {-1: pl.ds(HALO, HALO), 0: pl.ds(HALO, 256), 1: pl.ds(256, HALO)}[dr]
    dst_rows = {-1: pl.ds(HALO + 256, HALO), 0: pl.ds(HALO, 256), 1: pl.ds(0, HALO)}[dr]
    if dc == 0:
        return pad.at[2, src_rows, pl.ds(0, OWN_LANES)], pad.at[2, dst_rows, pl.ds(0, OWN_LANES)]
    if dc < 0:
        return pad.at[2, src_rows, pl.ds(0, 128)], from_right.at[2, dst_rows, :]
    return pad.at[2, src_rows, pl.ds(OWN_LANES - 128, 128)], from_left.at[2, dst_rows, :]


def flow_kernel(sections, offsets_in, packed_in, coef, block_out,
                pad, from_left, from_right, offsets, packed, spec, kept, crossed, turned, last_row, eb, en, unit_sums, flows, cols,
                local_sem, pixel_send, pixel_recv, flow_send, flow_recv):
    tables = {name: Table(packed, name) for name in PLACES}
    sec, tile = lax.axis_index("sec"), lax.axis_index("tile")
    sec_count = lax.axis_size("sec")
    row_pos, col_pos = tile // TILE_GRID, tile % TILE_GRID

    def device(ds, dr, dc):
        row = lax.rem(row_pos + (dr + TILE_GRID), TILE_GRID)
        col = lax.rem(col_pos + (dc + TILE_GRID), TILE_GRID)
        return (lax.rem(sec + ds, sec_count), row * TILE_GRID + col)

    barrier = pltpu.get_barrier_semaphore()
    partners = [
        (ds, dr, dc) for ds in range(4) for dr, dc in AROUND + [(0, 0)]
        if (ds, dr, dc) != (0, 0, 0) and not (ds == 2 and dr * dc != 0)
    ]
    flows[...] = jnp.zeros(flows.shape, F32)

    def there(dr, dc):
        row, col = row_pos + dr, col_pos + dc
        return (row >= 0) & (row < TILE_GRID) & (col >= 0) & (col < TILE_GRID)

    def toward(dr, dc, action):
        if (dr, dc) == (0, 0):
            action()
        else:
            pl.when(there(dr, dc))(action)

    def start_all(copies):
        for way in AROUND + [(0, 0)]:
            toward(*way, lambda way=way: [c.start() for w, c in copies if w == way] and None)

    def wait_sent(copies):
        for way in AROUND + [(0, 0)]:
            toward(*way, lambda way=way: [c.wait_send() for w, c in copies if w == way] and None)

    def wait_come(copies):
        for way in AROUND + [(0, 0)]:
            if any(w == way for w, _ in copies):
                toward(-way[0], -way[1], lambda way=way: [c.wait_recv() for w, c in copies if w == way] and None)

    def greet(way):
        for p in partners:
            if p[1:] == way:
                pl.semaphore_signal(barrier, inc=1, device_id=device(*p), device_id_type=MESH)

    expected = jnp.int32(0)
    for way in AROUND + [(0, 0)]:
        toward(*way, functools.partial(greet, way))
        count = sum(p[1:] == way for p in partners)
        expected += count if way == (0, 0) else count * there(*way).astype(jnp.int32)
    own_copy = pltpu.make_async_copy(
        sections.at[:, 0], pad.at[pl.ds(0, 2), pl.ds(HALO, 256), pl.ds(0, OWN_LANES)], local_sem.at[0]
    )
    offset_copies = [
        pltpu.make_async_copy(
            offsets_in.at[c, s, 0, :, pl.ds(128 * t, 128)],
            offsets.at[c, :, 4 * s + t, :],
            local_sem.at[2 + 8 * c + 4 * s + t],
        )
        for c in range(2) for s in range(2) for t in range(4)
    ]
    table_copy = pltpu.make_async_copy(packed_in, packed, local_sem.at[1])
    own_copy.start()
    table_copy.start()
    for copy in offset_copies:
        copy.start()
    pl.semaphore_wait(barrier, expected)

    def pixel_copy(k, ds, dr, dc, refs):
        return pltpu.make_async_remote_copy(
            src_ref=refs[0], dst_ref=refs[1], send_sem=pixel_send.at[k], recv_sem=pixel_recv.at[k],
            device_id=device(ds, dr, dc), device_id_type=MESH,
        )

    both = pl.ds(0, 2)
    own = [
        ((dr, dc), pixel_copy(k, 0, dr, dc, pixel_part(dr, dc, sections, pad, from_left, from_right, both, both)))
        for k, (dr, dc) in enumerate(AROUND)
    ]
    after = pixel_copy(
        8, 3, 0, 0, pixel_part(0, 0, sections, pad, from_left, from_right, pl.ds(0, 1), pl.ds(2, 1))
    )
    start_all(own)
    after.start()

    def transform(s, group, columns):
        first_transform(s, group, columns, pad, spec, tables)

    def energies(s, blocks, lanes, columns):
        block_energies(s, blocks, lanes, pad, eb)
        node_energies(s, columns, eb, en, tables["energy_cols"])

    def units(pair, first, count):
        @pl.loop(0, count)
        def _(k):
            n = first + k
            rows_back(n - 2, turned, last_row, en, unit_sums, tables)
            columns_back(crossed, turned, last_row, tables)
            cross_unit(pair, n, spec, kept, crossed, tables)

    inner_blocks, outer_blocks = range(2, 9), (0, 1, 9, 10)
    own_lanes, side_lanes, all_lanes = slice(0, OWN_LANES), slice(OWN_LANES, LANES), slice(0, LANES)

    def inner_own(s):
        transform(s, INNER, OWN_COLS)
        energies(s, inner_blocks, own_lanes, (1, 2))

    def inner_sides(s):
        merge_sides(s, slice(HALO, HALO + 256), pad, from_left, from_right, col_pos)
        transform(s, INNER, SIDE_COLS)
        energies(s, inner_blocks, side_lanes, (0, 3))

    def outer(s):
        merge_sides(s, slice(0, HALO), pad, from_left, from_right, col_pos)
        merge_sides(s, slice(HALO + 256, ROWS), pad, from_left, from_right, col_pos)
        clear_edges(s, pad, row_pos)
        transform(s, OUTER, OWN_COLS + SIDE_COLS)
        energies(s, outer_blocks, all_lanes, (0, 1, 2, 3))

    def corner_rows(first, count):
        @pl.loop(0, count)
        def _(k):
            corners(first + k, offsets, cols, coef)

    eb[...] = jnp.zeros(eb.shape, F32)
    own_copy.wait()
    table_copy.wait()
    pl.loop(0, 2)(inner_own)
    cross_unit(0, 0, spec, kept, crossed, tables)
    columns_back(crossed, turned, last_row, tables)
    cross_unit(0, 1, spec, kept, crossed, tables)
    wait_come(own[:2])
    pl.loop(0, 2)(inner_sides)
    units(0, 2, 2)
    wait_come(own[2:])
    pl.loop(0, 2)(outer)
    units(0, 4, 2)
    after.wait_recv()
    forward = [
        ((dr, dc), pixel_copy(9 + k, 0, dr, dc, pixel_forward(dr, dc, pad, from_left, from_right)))
        for k, (dr, dc) in enumerate(AROUND)
    ]
    start_all(forward)
    units(0, 6, 2)
    inner_own(2)
    units(1, 8, 2)
    wait_come(forward[:2])
    inner_sides(2)
    units(1, 10, 2)
    wait_come(forward[2:])
    outer(2)
    units(1, 12, 4)
    rows_back(14, turned, last_row, en, unit_sums, tables)
    columns_back(crossed, turned, last_row, tables)
    rows_back(15, turned, last_row, en, unit_sums, tables)

    flows[4, sec] = flow_block(unit_sums, tables["sums"], sec == sec_count - 1)
    share = [
        ((dr, dc), pltpu.make_async_remote_copy(
            src_ref=flows.at[4, sec], dst_ref=flows.at[3 * (1 - dr) + 1 - dc, sec], send_sem=flow_send.at[k],
            recv_sem=flow_recv.at[k], device_id=device(ds, dr, dc), device_id_type=MESH,
        ))
        for k, (ds, dr, dc) in enumerate(partners)
    ]
    start_all(share)
    for copy in offset_copies:
        copy.wait()
    shifted_columns(pad, cols)
    corner_rows(0, 32)
    wait_sent(own + forward + share)
    after.wait_send()
    wait_come(share)

    def column(d, c):
        return jnp.concatenate([flows[c, d], flows[3 + c, d], flows[6 + c, d]], axis=0)

    mesh = relax([extend(column(d, 1), column(d, 0), column(d, 2)) for d in range(4)], row_pos, col_pos)
    mine = mesh[0][8:16]
    for d in range(1, 4):
        mine = jnp.where(sec == d, mesh[d][8:16], mine)
    block_out[...] = mine


def blend_kernel(coef, block, mesh_out, warped, result, sem):
    mesh = block[...]
    write_mesh(mesh, mesh_out)
    copies = []
    for i in range(8):
        a, b = spread_lanes(mesh, i, 0), spread_lanes(mesh, i, 1)
        for k in range(32):
            r = 32 * i + k
            first = coef[0, r] + a * coef[1, r]
            second = coef[2, r] + a * coef[3, r]
            result[r] = first + b * second
        if i % 2 == 1:
            rows = pl.ds(32 * i - 32, 64)
            for s in range(2):
                for t in range(4):
                    copy = pltpu.make_async_copy(
                        result.at[rows, 4 * s + t, :], warped.at[s, 0, rows, pl.ds(128 * t, 128)], sem.at[len(copies)]
                    )
                    copy.start()
                    copies.append(copy)
    for copy in copies:
        copy.wait()


def vmem():
    return pl.BlockSpec(memory_space=pltpu.VMEM)


def shards(sections, corner_offsets):
    anywhere = pl.BlockSpec(memory_space=pl.ANY)
    dma = pltpu.SemaphoreType.DMA
    coef, block = pl.pallas_call(
        flow_kernel,
        out_shape=(pltpu.VMEM((4, 256, 8, 128), F32), pltpu.VMEM((8, 128), F32)),
        in_specs=[anywhere, anywhere, anywhere],
        out_specs=(vmem(), vmem()),
        scratch_shapes=[
            pltpu.VMEM((3, ROWS, LANES), BF16),
            pltpu.VMEM((3, ROWS, 128), BF16),
            pltpu.VMEM((3, ROWS, 128), BF16),
            pltpu.VMEM((2, 256, 8, 128), jnp.int32),
            pltpu.VMEM(PACKED.shape, BF16),
            pltpu.VMEM((3, 2, 5, 2, 272, 128), BF16),
            pltpu.VMEM((2, 4, 4, 272, 256), BF16),
            pltpu.VMEM((272, 1024), BF16),
            pltpu.VMEM((512, 128), BF16),
            pltpu.VMEM((8, 128), F32),
            pltpu.VMEM((3, 16, LANES), F32),
            pltpu.VMEM((3, 2, 4, 8, 128), F32),
            pltpu.VMEM((16, 8, 256), F32),
            pltpu.VMEM((9, 4, 8, 128), F32),
            pltpu.VMEM((5, 8 * SHIFT_ROWS, 128), F32),
            dma((18,)),
            dma((17,)),
            dma((17,)),
            dma((31,)),
            dma((31,)),
        ],
        compiler_params=pltpu.CompilerParams(
            vmem_limit_bytes=58 * 2**20, collective_id=0, has_side_effects=True
        ),
    )(sections, corner_offsets, jnp.asarray(PACKED))
    return pl.pallas_call(
        blend_kernel,
        out_shape=(
            jax.ShapeDtypeStruct((2, 2, 1, 8, 16), F32),
            jax.ShapeDtypeStruct((2, 1, 256, 512), F32),
        ),
        in_specs=[vmem(), vmem()],
        out_specs=(vmem(), anywhere),
        scratch_shapes=[pltpu.VMEM((256, 8, 128), F32), dma((32,))],
        compiler_params=pltpu.CompilerParams(vmem_limit_bytes=20 * 2**20),
    )(coef, block)


def solution(mesh):
    in_specs = (P("sec", "tile", None, None), P(None, "sec", "tile", None, None))
    out_specs = (P("sec", None, "tile", None, None), P("sec", "tile", None, None))
    return jax.shard_map(shards, mesh=mesh, in_specs=in_specs, out_specs=out_specs, check_vma=False)
```
